32 devices in a mesh: section: 2 (over x), wide: 4 (over z), tp: 4 (over y, core).
Axes of the slice: x: 2, y: 2, z: 4, core: 2. Of those that a mesh axis runs over, the one named last changes fastest.
Arguments:
- inputs: bfloat16 [2, 4, 2048, 768], P(None, 'tp', 'wide'), may hold values from -6 to 6
- cotangent: bfloat16 [2, 4, 2048, 768], P(None, 'tp', 'wide'), may hold values from -6 to 6
- segment_ids: int32 [2, 4, 2048], replicated, may hold values from 0 to 3, as said below
- norm_gain: float32 [2, 2, 768], P('section'), may hold values from 0.5 to 1.5
- norm_shift: float32 [2, 2, 768], P('section'), may hold values from -1.75 to 1.75
- qkv_weight: bfloat16 [2, 768, 3, 768], P('section', 'wide', None, 'tp'), may hold values from -0.21875 to 0.21875
- qkv_bias: float32 [2, 3, 768], P('section', None, 'tp'), may hold values from -1.75 to 1.75
- out_weight: bfloat16 [2, 768, 768], P('section', 'tp', 'wide'), may hold values from -1.75 to 1.75
- out_bias: float32 [2, 768], P('section'), may hold values from -1.75 to 1.75
- up_weight: bfloat16 [2, 768, 3072], P('section', 'wide', 'tp'), may hold values from -0.21875 to 0.21875
- up_bias: float32 [2, 3072], P('section', 'tp'), may hold values from -1.75 to 1.75
- down_weight: bfloat16 [2, 3072, 768], P('section', 'tp', 'wide'), may hold values from -0.109375 to 0.109375
- down_bias: float32 [2, 768], P('section'), may hold values from -1.75 to 1.75
Outputs:
- section_outputs: bfloat16 [2, 2, 4, 2048, 768], P('section', None, 'tp', 'wide')
- input_grads: float32 [2, 2, 4, 2048, 768], P('section', None, 'tp', 'wide')
- norm_gain_grad: float32 [2, 2, 768], P('section')
- norm_shift_grad: float32 [2, 2, 768], P('section')
- qkv_weight_grad: float32 [2, 768, 3, 768], P('section', 'wide', None, 'tp')
- qkv_bias_grad: float32 [2, 3, 768], P('section', None, 'tp')
- out_weight_grad: float32 [2, 768, 768], P('section', 'tp', 'wide')
- out_bias_grad: float32 [2, 768], P('section')
- up_weight_grad: float32 [2, 768, 3072], P('section', 'wide', 'tp')
- up_bias_grad: float32 [2, 3072], P('section', 'tp')
- down_weight_grad: float32 [2, 3072, 768], P('section', 'tp', 'wide')
- down_bias_grad: float32 [2, 768], P('section')
The draws below stay inside these ranges and needn't reach their ends.
Inputs may be any that keep to these rules, and one draw needn't show every extreme that they name: `segment_ids`: along each sequence the ids start at 0 and rise by one where a new document starts, never falling; in each micro-batch one sequence is a single document and another reaches the largest id.
All inputs are finite; a program needn't handle non-finite values.
Results may differ from the reference program's by a relative error of at most 0.025.
Values may be sent and summed in bfloat16 or wider, within the bound.
No kernel may reach another device: no remote copies, remote signals or barrier semaphores. Data moves between devices by JAX's collectives and lax.ppermute only.
A program may use at most 448 MiB of HBM per device.

```python
import math
import jax
import jax.numpy as jnp
from jax import lax

D = 768
HEADS = 12
HEAD_DIM = 64
ROTARY = 16
FF = 3072
MICRO = 2
LEN = 2048
BATCH = 4
SECTIONS = 2


def draw_segment_ids(key, part):
    key = jax.random.fold_in(key, 11)
    flag_key, pick_key = jax.random.split(key)
    average = max(2, LEN // 5)
    starts = (jax.random.randint(flag_key, (MICRO, BATCH, LEN), 0, average) == 0).astype(jnp.int32)
    places = jnp.arange(LEN, dtype=jnp.int32)
    starts = jnp.where(places[None, None, :] > 0, starts, 0)
    forced = ((places == LEN // 4) | (places == LEN // 2) | (places == 3 * LEN // 4)).astype(jnp.int32)
    chosen = jax.random.randint(pick_key, (MICRO, 1), 0, BATCH)
    rows = jnp.arange(BATCH, dtype=jnp.int32)[None, :]
    other = rows == (chosen + 1) % BATCH
    starts = jnp.where(other[:, :, None], forced[None, None, :], starts)
    numbers = jnp.minimum(jnp.cumsum(starts, -1), 3)
    whole = rows == chosen
    return jnp.where(whole[:, :, None], 0, numbers).astype(jnp.int32)


def steps_of(own_key, extent, shards, least, top_value):
    def one(axis_at, parts):
        draws = jax.random.uniform(jax.random.fold_in(jax.random.fold_in(own_key, 6), axis_at), (parts,), jnp.float32, least / len(shards), top_value / len(shards))
        return jnp.repeat(jnp.exp(draws), extent[axis_at] // parts).reshape((-1,) + (1,) * (len(extent) - axis_at - 1))

    level = one(*shards[0])
    for cut in shards[1:]:
        level = level * one(*cut)
    return level


def gaussian(stream_key, shape, scale, most, shards=(), kind=jnp.bfloat16):
    drawn = scale * jax.random.normal(stream_key, shape, jnp.float32)
    if shards:
        drawn = drawn * steps_of(stream_key, shape, shards, -0.22, 0.18)
    return jnp.clip(drawn, -most, most).astype(kind)


def setup_inputs(seed: int = 0) -> dict:
    key_list = jax.random.split(jax.random.key(seed), 14)
    return {
        "inputs": gaussian(key_list[0], (MICRO, BATCH, LEN, D), 1.0, 6.0, ((1, 4), (2, 4))),
        "cotangent": gaussian(key_list[1], (MICRO, BATCH, LEN, D), 1.0, 6.0, ((1, 4), (2, 4))),
        "segment_ids": draw_segment_ids(jax.random.fold_in(key_list[13], 71), 0),
        "norm_gain": jnp.clip(1.0 + 0.1 * jax.random.normal(key_list[3], (SECTIONS, 2, D), jnp.float32), 0.5, 1.5),
        "norm_shift": gaussian(key_list[4], (SECTIONS, 2, D), 0.3, 1.75, ((0, 2),), jnp.float32),
        "qkv_weight": gaussian(key_list[5], (SECTIONS, D, 3, D), D ** -0.5, 0.21875, ((0, 2), (1, 4), (3, 4))),
        "qkv_bias": gaussian(key_list[6], (SECTIONS, 3, D), 0.3, 1.75, ((0, 2), (2, 4)), jnp.float32),
        "out_weight": gaussian(key_list[7], (SECTIONS, D, D), (max(1, D // 64)) ** -0.5, 1.75, ((0, 2), (1, 4), (2, 4))),
        "out_bias": gaussian(key_list[8], (SECTIONS, D), 0.3, 1.75, ((0, 2),), jnp.float32),
        "up_weight": gaussian(key_list[9], (SECTIONS, D, FF), D ** -0.5, 0.21875, ((0, 2), (1, 4), (2, 4))),
        "up_bias": gaussian(key_list[10], (SECTIONS, FF), 0.3, 1.75, ((0, 2), (1, 4)), jnp.float32),
        "down_weight": gaussian(key_list[11], (SECTIONS, FF, D), FF ** -0.5, 0.109375, ((0, 2), (1, 4), (2, 4))),
        "down_bias": gaussian(key_list[12], (SECTIONS, D), 0.3, 1.75, ((0, 2),), jnp.float32),
    }


@jax.custom_vjp
def low(v):
    return lax.optimization_barrier(v.astype(jnp.bfloat16)).astype(jnp.float32)

@jax.custom_vjp
def low_back(v):
    return v

def low_keep(v):
    return (low(v), None)

def low_pass(kept, grad):
    return (grad,)

def back_keep(v):
    return (v, None)

def back_low(kept, grad):
    return (low(grad),)
low.defvjp(low_keep, low_pass)
low_back.defvjp(back_keep, back_low)
highest = lax.Precision.HIGHEST
epsilon = 1e-05
rotary_base = 10000.0

def normalize(values, gain, shift):
    centred = values - lax.optimization_barrier(jnp.mean(values, -1, keepdims=True))
    variance = lax.optimization_barrier(jnp.mean(centred * centred, -1, keepdims=True))
    return centred * lax.rsqrt(variance + epsilon) * gain + shift

def angles(length):
    positions = jnp.arange(length, dtype=jnp.float32)
    freqs = rotary_base ** (-(2.0 * jnp.arange(ROTARY // 2, dtype=jnp.float32)) / ROTARY)
    turned = positions[:, None] * freqs[None, :]
    turned = jnp.concatenate([turned, turned], -1)
    return (jnp.cos(turned)[:, None, :], jnp.sin(turned)[:, None, :])

def rotate(values, cosine, sine):
    half = ROTARY // 2
    front = values[..., :ROTARY]
    turned = jnp.concatenate([-front[..., half:], front[..., :half]], -1)
    return jnp.concatenate([front * cosine + turned * sine, values[..., ROTARY:]], -1)

def attend(query, keys, values, segment):
    raw = low_back(jnp.einsum('qhd,khd->hqk', query, keys, precision=highest))
    places = jnp.arange(segment.shape[0])
    allowed = (segment[:, None] == segment[None, :]) & (places[:, None] >= places[None, :])
    scores = jnp.where(allowed[None], raw * HEAD_DIM ** (-0.5), -jnp.inf)
    weights = low(jax.nn.softmax(scores, -1))
    return jnp.einsum('hqk,khd->qhd', weights, values, precision=highest)

def attend_item(item):
    return attend(item[0], item[1], item[2], item[3])

def layer(inputs, params, segments):
    gain, shift, w_qkv, b_qkv, w_out, b_out, w_up, b_up, w_down, b_down = params
    batch, length = (inputs.shape[0], inputs.shape[1])
    first = low(normalize(inputs, gain[0], shift[0]))
    second = low(normalize(inputs, gain[1], shift[1]))
    mixed = low_back(jnp.einsum('bld,dte->blte', first, w_qkv, precision=highest) + b_qkv)
    heads = mixed.reshape(batch, length, 3, HEADS, HEAD_DIM)
    cosine, sine = angles(length)
    query = low(rotate(heads[:, :, 0], cosine, sine))
    keys = low(rotate(heads[:, :, 1], cosine, sine))
    values = low(heads[:, :, 2])
    attended = lax.map(jax.checkpoint(attend_item), (query, keys, values, segments))
    attended = low_back(low(attended.reshape(batch, length, D)))
    hidden_in = low_back(jnp.einsum('bld,df->blf', second, w_up, precision=highest) + b_up)
    hidden = low(jax.nn.gelu(hidden_in, approximate=False))
    branch = low_back(jnp.einsum('bld,de->ble', attended, w_out, precision=highest) + jnp.einsum('blf,fe->ble', hidden, w_down, precision=highest))
    return inputs + branch + b_out + b_down

def run_layer(inputs, params, segments):
    group = math.gcd(BATCH, max(1, 4096 // LEN))

    def visit(carry, item):
        return (carry, jax.checkpoint(layer)(item[0], params, item[1]))
    grouped = (inputs.reshape(-1, group, LEN, D), segments.reshape(-1, group, LEN))
    _, outputs = lax.scan(visit, None, grouped)
    return outputs.reshape(inputs.shape)

def reference(inputs, cotangent, segment_ids, norm_gain, norm_shift, qkv_weight, qkv_bias, out_weight, out_bias, up_weight, up_bias, down_weight, down_bias):
    params = tuple((item.astype(jnp.float32) for item in (norm_gain, norm_shift, qkv_weight, qkv_bias, out_weight, out_bias, up_weight, up_bias, down_weight, down_bias)))
    source = inputs.astype(jnp.float32)
    probe = jnp.zeros((SECTIONS,) + source.shape, jnp.float32)

    def forward(probe, params):
        finals, every = ([], [])
        for batch_index in range(MICRO):
            passed = source[batch_index] + probe[0, batch_index]
            results = []
            for section_number in range(SECTIONS):
                section_params = tuple((item[section_number] for item in params))
                result = run_layer(passed, section_params, segment_ids[batch_index])
                results.append(result)
                if section_number + 1 < SECTIONS:
                    passed = low_back(low(result)) + probe[section_number + 1, batch_index]
            every.append(jnp.stack(results))
            finals.append(results[-1])
        return (jnp.stack(finals), jnp.stack(every, 1))
    finals, pullback, every = jax.vjp(forward, probe, params, has_aux=True)
    probe_grad, grads = pullback(cotangent.astype(jnp.float32))
    return (every.astype(jnp.bfloat16), probe_grad, grads[0], grads[1], grads[2], grads[3], grads[4], grads[5], grads[6], grads[7], grads[8], grads[9])
```

```python
import functools

import jax
import jax.numpy as jnp
from jax import lax
from jax.experimental import pallas as pl
from jax.experimental.pallas import tpu as pltpu
from jax.sharding import PartitionSpec as P

HEAD_DIM = 64
ROTARY = 16
LANES = 256
CHUNKS = 2
QUERY_BLOCK = 256
KEY_BLOCK = 512
ROW_BLOCK = 256

epsilon = 1e-05
rotary_base = 10000.0
masked_out = -1e30
f32 = jnp.float32
bf16 = jnp.bfloat16
NT = (((1,), (1,)), ((), ()))


def params(size=44):
    return pltpu.CompilerParams(
        dimension_semantics=("arbitrary",), vmem_limit_bytes=size * 1024 * 1024
    )


def dot(left, right):
    return jnp.dot(left, right, preferred_element_type=f32)


def dot_nt(left, right):
    return lax.dot_general(left, right, NT, preferred_element_type=f32)


def rows_spec(rows, columns):
    return pl.BlockSpec((rows, columns), lambda i: (i, 0))


def whole_spec(array):
    return pl.BlockSpec(array.shape, lambda i: (0,) * array.ndim)


def smem_spec():
    return pl.BlockSpec(memory_space=pltpu.SMEM)


def standardize(values):
    centred = values - jnp.mean(values, -1, keepdims=True)
    inverse = lax.rsqrt(jnp.mean(centred * centred, -1, keepdims=True) + epsilon)
    return centred * inverse, inverse


def turn(values, cosine, low, high):
    half = ROTARY // 2
    ahead = pltpu.roll(values, LANES - half, 1)
    behind = pltpu.roll(values, half, 1)
    return values * cosine + ahead * low + behind * high


def turn_back(grads, cosine, low, high):
    half = ROTARY // 2
    ahead = pltpu.roll(grads * high, LANES - half, 1)
    behind = pltpu.roll(grads * low, half, 1)
    return grads * cosine + ahead + behind


def enter_kernel(
    heads,
    x_ref, gs_ref, wq_ref, bq_ref, wu_ref, bu_ref, c_ref, lo_ref, hi_ref, seg_ref,
    a0_ref, a1_ref, q_ref, k_ref, v_ref, h_ref, d_ref,
):
    normed, _ = standardize(x_ref[...].astype(f32))
    first = (normed * gs_ref[0:1] + gs_ref[2:3]).astype(bf16)
    second = (normed * gs_ref[1:2] + gs_ref[3:4]).astype(bf16)
    a0_ref[...] = first
    a1_ref[...] = second
    mixed = dot(first, wq_ref[...]) + bq_ref[...]
    cosine, low, high = c_ref[...], lo_ref[...], hi_ref[...]
    query = turn(mixed[:, :LANES], cosine, low, high)
    keys = turn(mixed[:, LANES : 2 * LANES], cosine, low, high)
    lane = lax.broadcasted_iota(jnp.int32, query.shape, 1)
    used = heads * HEAD_DIM
    mine = (lane - used) == seg_ref[...]
    spare = lane >= used
    q_ref[...] = jnp.where(
        spare, jnp.where(mine, 1.0, 0.0), query * HEAD_DIM ** (-0.5)
    ).astype(bf16)
    k_ref[...] = jnp.where(spare, jnp.where(mine, 0.0, masked_out), keys).astype(bf16)
    v_ref[...] = mixed[:, 2 * LANES :].astype(bf16)
    before = dot(second, wu_ref[...]) + bu_ref[...]
    phi = 0.5 + 0.5 * lax.erf(before * (0.5**0.5))
    density = jnp.exp(before * before * (-0.5)) * 0.3989422804014327
    h_ref[...] = (before * phi).astype(bf16)
    d_ref[...] = (phi + before * density).astype(bf16)


def enter(x, gs, wq, bq, wu, bu, tables, seg, heads):
    tokens, width = x.shape
    rows = min(ROW_BLOCK, tokens)
    hidden = wu.shape[1]
    columns = (width, width, LANES, LANES, LANES, hidden, hidden)
    return pl.pallas_call(
        functools.partial(enter_kernel, heads),
        grid=(tokens // rows,),
        in_specs=[rows_spec(rows, width)]
        + [whole_spec(item) for item in (gs, wq, bq, wu, bu)]
        + [rows_spec(rows, LANES)] * 3
        + [rows_spec(rows, 1)],
        out_specs=[rows_spec(rows, item) for item in columns],
        out_shape=[jax.ShapeDtypeStruct((tokens, item), bf16) for item in columns],
        compiler_params=params(),
        cost_estimate=pl.CostEstimate(
            flops=2 * tokens * width * (wq.shape[1] + hidden),
            bytes_accessed=20 * tokens * width,
            transcendentals=2 * tokens * hidden,
        ),
        name="enter",
    )(x, gs, wq, bq, wu, bu, *tables, seg)


def head_lanes(array, heads, spare):
    lane = lax.broadcasted_iota(jnp.int32, array.shape, 1)
    zero = jnp.zeros_like(array)
    result = []
    for head in range(heads):
        keep = (lane >= head * HEAD_DIM) & (lane < (head + 1) * HEAD_DIM)
        if spare:
            keep = keep | (lane >= heads * HEAD_DIM)
        result.append(jnp.where(keep, array, zero))
    return result


def attend_kernel(
    heads, key_block, start_ref, q_ref, k_ref, v_ref, h_ref, wo_ref, wd_ref,
    o_ref, lse_ref, part_ref, top_ref, sum_ref, acc_ref,
):
    rows = q_ref.shape[0]
    queries = head_lanes(q_ref[...], heads, True)
    first_row = start_ref[0] + pl.program_id(0) * rows
    full = first_row // key_block
    top_ref[...] = jnp.full(top_ref.shape, masked_out, f32)
    sum_ref[...] = jnp.zeros(sum_ref.shape, f32)
    acc_ref[...] = jnp.zeros(acc_ref.shape, f32)

    def step(block, diagonal):
        place = pl.ds(pl.multiple_of(block * key_block, key_block), key_block)
        keys = k_ref[place, :]
        for head in range(heads):
            half = head * HEAD_DIM // 128 * 128
            scores = dot_nt(queries[head], keys)
            if diagonal:
                row = lax.broadcasted_iota(jnp.int32, scores.shape, 0) + first_row
                column = lax.broadcasted_iota(jnp.int32, scores.shape, 1) + block * key_block
                scores = jnp.where(column <= row, scores, masked_out)
            before = top_ref[head]
            top = jnp.maximum(before, jnp.max(scores, -1, keepdims=True))
            fade = jnp.exp(before - top)
            probs = jnp.exp(scores - top[:, :1])
            top_ref[head] = top
            sum_ref[head] = sum_ref[head] * fade + jnp.sum(probs, -1, keepdims=True)
            acc_ref[head] = acc_ref[head] * fade + dot(
                probs.astype(bf16), v_ref[place, half : half + 128]
            )

    @pl.loop(0, full)
    def _(block):
        step(block, False)

    step(full, True)
    lane = lax.broadcasted_iota(jnp.int32, (rows, 128), 1)
    parts = []
    for half in range(LANES // 128):
        part = jnp.zeros((rows, 128), f32)
        for head in range(heads):
            offset = head * HEAD_DIM - half * 128
            if 0 <= offset < 128:
                keep = (lane >= offset) & (lane < offset + HEAD_DIM)
                part = jnp.where(keep, acc_ref[head] / sum_ref[head], part)
        parts.append(part)
    attended = jnp.concatenate(parts, 1).astype(bf16)
    o_ref[...] = attended
    totals = jnp.zeros((rows, 128), f32)
    for head in range(heads):
        totals = jnp.where(lane == head, top_ref[head] + jnp.log(sum_ref[head]), totals)
    lse_ref[...] = totals.T[: lse_ref.shape[0]]
    part_ref[...] = (
        dot_nt(attended, wo_ref[...]) + dot_nt(h_ref[...], wd_ref[...])
    ).astype(bf16)


def attend(start, q, k, v, h, wo, wd, heads):
    tokens = q.shape[0]
    rows = min(QUERY_BLOCK, tokens)
    key_block = min(KEY_BLOCK, k.shape[0])
    hidden, width = h.shape[1], wo.shape[0]
    return pl.pallas_call(
        functools.partial(attend_kernel, heads, key_block),
        grid=(tokens // rows,),
        in_specs=[smem_spec(), rows_spec(rows, LANES), whole_spec(k), whole_spec(v)]
        + [rows_spec(rows, hidden), whole_spec(wo), whole_spec(wd)],
        out_specs=[
            rows_spec(rows, LANES),
            pl.BlockSpec((8, rows), lambda i: (0, i)),
            rows_spec(rows, width),
        ],
        out_shape=[
            jax.ShapeDtypeStruct((tokens, LANES), bf16),
            jax.ShapeDtypeStruct((8, tokens), f32),
            jax.ShapeDtypeStruct((tokens, width), bf16),
        ],
        scratch_shapes=[pltpu.VMEM((heads, rows, 128), f32)] * 3,
        compiler_params=params(),
        cost_estimate=pl.CostEstimate(
            flops=3 * tokens * k.shape[0] * heads * 512 + 2 * tokens * width * (hidden + LANES),
            bytes_accessed=8 * tokens * width,
            transcendentals=tokens * k.shape[0] * heads,
        ),
        name="attend",
    )(start, q, k, v, h, wo, wd)


def attend_back_kernel(
    heads, key_block, carried, start_ref, gb_ref, wo_ref, wd_ref, d_ref, q_ref, o_ref, lse_ref,
    k_ref, v_ref, kt_ref, *rest,
):
    if carried:
        dk_in_ref, dv_in_ref, *rest = rest
    gu_ref, dq_ref, dk_ref, dv_ref, dqt_ref = rest
    rows = q_ref.shape[0]
    first_row = start_ref[0] + pl.program_id(0) * rows
    full = first_row // key_block

    @pl.when(pl.program_id(0) == 0)
    def _():
        dk_ref[...] = jnp.zeros(dk_ref.shape, f32)
        dv_ref[...] = jnp.zeros(dv_ref.shape, f32)
        if carried:
            dk_ref[...] = dk_in_ref[...]
            dv_ref[...] = dv_in_ref[...]

    grad = gb_ref[...]
    gu_ref[...] = (dot(grad, wd_ref[...]) * d_ref[...].astype(f32)).astype(bf16)
    grad_out = dot(grad, wo_ref[...]).astype(bf16)
    product = (grad_out.astype(f32) * o_ref[...].astype(f32)).T
    centres = [
        jnp.sum(product[head * HEAD_DIM : (head + 1) * HEAD_DIM], 0, keepdims=True)
        for head in range(heads)
    ]
    queries = head_lanes(q_ref[...], heads, True)
    grads = head_lanes(grad_out, heads, False)
    dqt_ref[...] = jnp.zeros(dqt_ref.shape, f32)

    def step(block, diagonal):
        place = pl.ds(pl.multiple_of(block * key_block, key_block), key_block)
        keys = k_ref[place, :]
        values = v_ref[place, :]
        grad_keys = dk_ref[place, :]
        grad_values = dv_ref[place, :]
        for head in range(heads):
            here = slice(head * HEAD_DIM, (head + 1) * HEAD_DIM)
            scores = dot_nt(keys, queries[head])
            probs = jnp.exp(scores - lse_ref[head : head + 1, :])
            if diagonal:
                column = lax.broadcasted_iota(jnp.int32, scores.shape, 0) + block * key_block
                row = lax.broadcasted_iota(jnp.int32, scores.shape, 1) + first_row
                probs = jnp.where(column <= row, probs, 0.0)
            grad_probs = dot_nt(values, grads[head])
            grad_scores = (probs * (grad_probs - centres[head])).astype(bf16)
            grad_values += dot(probs.astype(bf16), grads[head])
            grad_keys += dot(grad_scores, queries[head])
            dqt_ref[here, :] += dot(kt_ref[here, place], grad_scores)
        dk_ref[place, :] = grad_keys
        dv_ref[place, :] = grad_values

    @pl.loop(0, full)
    def _(block):
        step(block, False)

    step(full, True)
    dq_ref[...] = dqt_ref[...].T * HEAD_DIM ** (-0.5)


def attend_back(start, gb, wo, wd, d, q, o, lse, k, v, carried, heads):
    tokens, width = gb.shape
    rows = min(QUERY_BLOCK, tokens)
    span = k.shape[0]
    key_block = min(KEY_BLOCK, span)
    hidden = wd.shape[1]
    kt = k.T
    carried = list(carried)
    whole = pl.BlockSpec((span, LANES), lambda i: (0, 0))
    return pl.pallas_call(
        functools.partial(attend_back_kernel, heads, key_block, bool(carried)),
        grid=(tokens // rows,),
        in_specs=[smem_spec(), rows_spec(rows, width), whole_spec(wo), whole_spec(wd)]
        + [rows_spec(rows, hidden), rows_spec(rows, LANES), rows_spec(rows, LANES)]
        + [pl.BlockSpec((8, rows), lambda i: (0, i)), whole, whole, whole_spec(kt)]
        + [whole] * len(carried),
        out_specs=[rows_spec(rows, hidden), rows_spec(rows, LANES), whole, whole],
        out_shape=[
            jax.ShapeDtypeStruct((tokens, hidden), bf16),
            jax.ShapeDtypeStruct((tokens, LANES), f32),
            jax.ShapeDtypeStruct((span, LANES), f32),
            jax.ShapeDtypeStruct((span, LANES), f32),
        ],
        scratch_shapes=[pltpu.VMEM((LANES, rows), f32)],
        compiler_params=params(),
        cost_estimate=pl.CostEstimate(
            flops=7 * tokens * span * heads * 512 + 2 * tokens * width * (hidden + LANES),
            bytes_accessed=8 * tokens * width,
            transcendentals=tokens * span * heads,
        ),
        name="attend_back",
    )(start, gb, wo, wd, d, q, o, lse, k, v, kt, *carried)


def leave_kernel(
    x_ref, gs_ref, dq_ref, dk_ref, dv_ref, gu_ref, wq_ref, wu_ref, c_ref, lo_ref, hi_ref,
    gm_ref, e_ref, norm_ref, mixed_ref, up_ref,
):
    @pl.when(pl.program_id(0) == 0)
    def _():
        norm_ref[...] = jnp.zeros(norm_ref.shape, f32)
        mixed_ref[...] = jnp.zeros(mixed_ref.shape, f32)
        up_ref[...] = jnp.zeros(up_ref.shape, f32)

    cosine, low, high = c_ref[...], lo_ref[...], hi_ref[...]
    grads = jnp.concatenate(
        [
            turn_back(dq_ref[...], cosine, low, high),
            turn_back(dk_ref[...], cosine, low, high),
            dv_ref[...],
        ],
        1,
    ).astype(bf16)
    gm_ref[...] = grads
    grad_up = gu_ref[...]
    mixed_ref[...] += jnp.sum(grads.astype(f32), 0, keepdims=True)
    up_ref[...] += jnp.sum(grad_up.astype(f32), 0, keepdims=True)
    grad_first = dot_nt(grads, wq_ref[...])
    grad_second = dot_nt(grad_up, wu_ref[...])
    normed, _ = standardize(x_ref[...].astype(f32))
    norm_ref[0:1] += jnp.sum(grad_first * normed, 0, keepdims=True)
    norm_ref[1:2] += jnp.sum(grad_second * normed, 0, keepdims=True)
    norm_ref[2:3] += jnp.sum(grad_first, 0, keepdims=True)
    norm_ref[3:4] += jnp.sum(grad_second, 0, keepdims=True)
    e_ref[...] = (grad_first * gs_ref[0:1] + grad_second * gs_ref[1:2]).astype(bf16)


def leave(x, gs, dq, dk, dv, gu, wq, wu, tables):
    tokens, width = x.shape
    rows = min(ROW_BLOCK, tokens)
    hidden, mixed = wu.shape[1], wq.shape[1]
    sums = [(4, width), (1, mixed), (1, hidden)]
    return pl.pallas_call(
        leave_kernel,
        grid=(tokens // rows,),
        in_specs=[rows_spec(rows, width), whole_spec(gs)]
        + [rows_spec(rows, LANES)] * 3
        + [rows_spec(rows, hidden), whole_spec(wq), whole_spec(wu)]
        + [rows_spec(rows, LANES)] * 3,
        out_specs=[rows_spec(rows, mixed), rows_spec(rows, width)]
        + [pl.BlockSpec(item, lambda i: (0, 0)) for item in sums],
        out_shape=[
            jax.ShapeDtypeStruct((tokens, mixed), bf16),
            jax.ShapeDtypeStruct((tokens, width), bf16),
        ]
        + [jax.ShapeDtypeStruct(item, f32) for item in sums],
        compiler_params=params(),
        cost_estimate=pl.CostEstimate(
            flops=2 * tokens * width * (mixed + hidden),
            bytes_accessed=16 * tokens * width,
            transcendentals=tokens,
        ),
        name="leave",
    )(x, gs, dq, dk, dv, gu, wq, wu, *tables)


def pick(bit, zero, one):
    return jnp.where(bit == 0, zero, one)


def reverse_bits(index, bits):
    result = 0
    for bit in range(bits):
        result = result * 2 + ((index >> bit) & 1)
    return result


class Plan:
    def __init__(self, batch, length):
        self.wide, self.tp = lax.axis_size("wide"), lax.axis_size("tp")
        self.batch, self.length = batch, length
        self.bits = self.tp.bit_length() - 1
        self.group = self.wide // batch
        self.chunks = CHUNKS if self.group == 1 else 1
        self.unit = length // (self.wide * self.chunks)
        self.section = lax.axis_index("section")
        self.wide_index = lax.axis_index("wide")
        self.tp_index = lax.axis_index("tp")
        self.part = sum(
            ((self.tp_index >> bit) & 1) << (self.bits - 1 - bit) for bit in range(self.bits)
        )

    def units(self):
        for unit in range(self.wide * self.chunks):
            owner, half = divmod(unit, self.chunks)
            rest, part = divmod(unit, self.tp)
            sub, chunk = divmod(rest, self.chunks)
            for sequence in range(self.batch):
                worker = (sequence * self.group + sub) * self.tp + reverse_bits(part, self.bits)
                yield owner * self.tp + sequence, worker, half, chunk, part

    def to_work(self, block):
        chunks = []
        for chunk in range(self.chunks):
            result = None
            for half in range(self.chunks):
                pairs = [u[:2] for u in self.units() if u[2] == half and u[3] == chunk]
                piece = block[half * self.unit : (half + 1) * self.unit]
                piece = lax.ppermute(piece, ("wide", "tp"), pairs)
                if result is None:
                    result = piece
                else:
                    result = jnp.where(self.part % self.chunks == half, piece, result)
            chunks.append(result)
        return chunks

    def to_owner(self, chunks, cross):
        devices = self.wide * self.tp
        received = []
        for turn_index in range(self.chunks):
            piece = chunks[0]
            for chunk in range(1, self.chunks):
                here = (self.part + turn_index) % self.chunks == chunk
                piece = jnp.where(here, chunks[chunk], piece)
            pairs = []
            for owner, worker, _, chunk, part in self.units():
                if (part + turn_index) % self.chunks == chunk:
                    for section in range(2):
                        target = section ^ int(cross)
                        pairs.append((section * devices + worker, target * devices + owner))
            received.append(lax.ppermute(piece, ("section", "wide", "tp"), pairs))
        if self.chunks == 1:
            return received[0]
        chunk = (self.wide_index * self.chunks // self.tp) % self.chunks
        ordered = []
        for half in range(self.chunks):
            piece = received[0]
            for turn_index in range(1, self.chunks):
                piece = jnp.where(
                    (chunk - half) % self.chunks == turn_index, received[turn_index], piece
                )
            ordered.append(piece)
        return jnp.concatenate(ordered, 0)

    def exchange(self, first, second):
        mine = [pick(self.section, a, b) for a, b in zip(first, second)]
        other = [pick(self.section, b, a) for a, b in zip(first, second)]
        same, cross = self.to_owner(mine, False), self.to_owner(other, True)
        return jnp.stack([pick(self.section, same, cross), pick(self.section, cross, same)])

    def swap(self, value):
        return lax.ppermute(value, "section", [(0, 1), (1, 0)])

    def gather(self, block):
        for bit in reversed(range(self.bits)):
            other = lax.ppermute(
                block, "tp", [(index, index ^ (1 << bit)) for index in range(self.tp)]
            )
            here = (self.tp_index >> bit) & 1
            block = jnp.concatenate([pick(here, block, other), pick(here, other, block)], 0)
        return block

    def scatter(self, block):
        for bit in range(self.bits):
            half = block.shape[0] // 2
            here = (self.tp_index >> bit) & 1
            sent = pick(here, block[half:], block[:half]).astype(bf16)
            kept = pick(here, block[:half], block[half:]).astype(f32)
            other = lax.ppermute(
                sent, "tp", [(index, index ^ (1 << bit)) for index in range(self.tp)]
            )
            block = kept + other.astype(f32)
        return block

    def groups(self):
        return [
            [sequence * self.group + sub for sub in range(self.group)]
            for sequence in range(self.batch)
        ]

    def all_places(self, block):
        if self.group == 1:
            return block
        return lax.all_gather(block, "wide", axis=0, tiled=True, axis_index_groups=self.groups())

    def own_places(self, block):
        if self.group == 1:
            return block
        return lax.psum_scatter(
            block.astype(bf16), "wide", scatter_dimension=0, tiled=True,
            axis_index_groups=self.groups(),
        ).astype(f32)


def angle_tables(places, heads):
    half = ROTARY // 2
    freqs = rotary_base ** (-(2.0 * jnp.arange(half, dtype=f32)) / ROTARY)
    turned = places[:, None].astype(f32) * freqs[None, :]
    cosine, sine = jnp.cos(turned), jnp.sin(turned)
    none = jnp.zeros_like(sine)
    rest = jnp.zeros((places.shape[0], HEAD_DIM - ROTARY), f32)
    tail = jnp.zeros((places.shape[0], LANES - heads * HEAD_DIM), f32)
    return (
        jnp.concatenate([cosine, cosine, rest + 1.0] * heads + [tail + 1.0], 1),
        jnp.concatenate([-sine, none, rest] * heads + [tail], 1),
        jnp.concatenate([none, sine, rest] * heads + [tail], 1),
    )


def on_device(
    inputs, cotangent, segment_ids, norm_gain, norm_shift, qkv_weight, qkv_bias, out_weight,
    out_bias, up_weight, up_bias, down_weight, down_bias,
):
    batch, length = segment_ids.shape[1], segment_ids.shape[2]
    plan = Plan(batch, length)
    width = inputs.shape[-1]
    local = qkv_weight.shape[-1]
    hidden = up_weight.shape[-1]
    heads = local // HEAD_DIM
    section = plan.section

    source = plan.to_work(jnp.where(section == 0, inputs[0, 0], inputs[1, 0]))
    entry = jnp.concatenate([qkv_weight[0].reshape(-1, 3 * local), up_weight[0]], 1)
    exit_ = jnp.concatenate([out_weight[0].T, down_weight[0].T], 1)
    small = jnp.concatenate(
        [
            norm_gain[0].reshape(-1), norm_shift[0].reshape(-1), out_bias[0] + down_bias[0],
            qkv_bias[0].reshape(-1), up_bias[0],
        ]
    )
    entry_other, small_other = plan.swap(entry), plan.swap(small)
    exit_other = plan.swap(exit_)
    layers = []
    for layer in range(2):
        mine = section == layer
        entry_all = lax.all_gather(
            jnp.where(mine, entry, entry_other), "wide", axis=0, tiled=True
        )
        exit_all = lax.all_gather(jnp.where(mine, exit_, exit_other), "wide", axis=0, tiled=True)
        values = jnp.where(mine, small, small_other)
        gain_shift = values[: 4 * width].reshape(4, width)
        after_bias = values[4 * width : 5 * width]
        qkv_row = values[5 * width : 5 * width + 3 * local].reshape(1, 3, local)
        up_row = values[5 * width + 3 * local :].reshape(1, hidden)
        space = ((0, 0), (0, 0), (0, LANES - local))
        wq = jnp.pad(entry_all[:, : 3 * local].reshape(width, 3, local), space)
        bq = jnp.pad(qkv_row, space)
        layers.append(
            dict(
                gs=gain_shift,
                after=after_bias,
                wq=wq.reshape(width, 3 * LANES),
                bq=bq.reshape(1, 3 * LANES),
                wu=entry_all[:, 3 * local :],
                bu=up_row,
                wo=jnp.pad(exit_all[:, :local], ((0, 0), (0, LANES - local))),
                wd=exit_all[:, local:],
            )
        )

    segments = lax.dynamic_index_in_dim(segment_ids, section, 0, False)
    segments = lax.dynamic_index_in_dim(segments, plan.wide_index // plan.group, 0, False)
    sub_length = length // plan.group
    first_place = (plan.wide_index % plan.group) * sub_length
    segments = lax.dynamic_slice_in_dim(segments, first_place, sub_length, 0)
    tables = angle_tables(first_place + jnp.arange(sub_length, dtype=jnp.int32), heads)
    size = plan.unit * plan.tp
    starts = [(first_place + index * size).reshape(1) for index in range(plan.chunks)]
    spans = [slice(index * size, (index + 1) * size) for index in range(plan.chunks)]
    chunk_tables = [[table[span] for table in tables] for span in spans]
    chunk_segments = [segments[span].reshape(-1, 1) for span in spans]

    outputs, kept = [], []
    blocks = source
    for layer in range(2):
        w = layers[layer]
        state, after = [], []
        keys = values = None
        for index in range(plan.chunks):
            x = plan.gather(blocks[index])
            a0, a1, q, k, v, h, d = enter(
                x, w["gs"], w["wq"], w["bq"], w["wu"], w["bu"], chunk_tables[index],
                chunk_segments[index], heads,
            )
            k, v = plan.all_places(k), plan.all_places(v)
            keys = k if keys is None else jnp.concatenate([keys, k], 0)
            values = v if values is None else jnp.concatenate([values, v], 0)
            o, lse, part = attend(
                starts[index], q, keys, values, h, w["wo"], w["wd"], heads
            )
            branch = plan.scatter(part)
            result = blocks[index].astype(f32) + branch + w["after"]
            after.append(result.astype(bf16))
            state.append(
                dict(x=x, a0=a0, a1=a1, q=q, h=h, d=d, o=o, lse=lse, k=keys, v=values)
            )
        kept.append((blocks, state))
        outputs.append(after)
        blocks = after
    section_outputs = plan.exchange(outputs[0], outputs[1])

    grads = plan.to_work(jnp.where(section == 0, cotangent[0, 0], cotangent[1, 0]))
    input_grads, weight_grads, norm_grads, bias_grads = {}, {}, {}, {}
    for layer in reversed(range(2)):
        w = layers[layer]
        blocks, state = kept[layer]
        carried = ()
        gathered, grad_up, grad_mixed, after = {}, {}, {}, {}
        norm_sum = mixed_sum = up_sum = 0.0
        for index in reversed(range(plan.chunks)):
            s = state[index]
            gb = plan.gather(grads[index])
            gu, dq, dk, dv = attend_back(
                starts[index], gb, w["wo"], w["wd"], s["d"], s["q"], s["o"], s["lse"],
                s["k"], s["v"], carried, heads,
            )
            if plan.chunks > 1:
                carried = (dk[: index * size], dv[: index * size])
                dk, dv = dk[index * size :], dv[index * size :]
            dk, dv = plan.own_places(dk), plan.own_places(dv)
            gm, e, norm_part, mixed_part, up_part = leave(
                s["x"], w["gs"], dq, dk, dv, gu, w["wq"], w["wu"], chunk_tables[index]
            )
            norm_sum += norm_part
            mixed_sum += mixed_part
            up_sum += up_part
            scaled = plan.scatter(e)
            normed, inverse = standardize(blocks[index].astype(f32))
            after[index] = grads[index].astype(f32) + inverse * (
                scaled
                - jnp.mean(scaled, -1, keepdims=True)
                - normed * jnp.mean(scaled * normed, -1, keepdims=True)
            )
            gathered[index], grad_up[index], grad_mixed[index] = gb, gu, gm

        def join(items):
            return jnp.concatenate([items[index] for index in range(plan.chunks)], 0)

        def over_tokens(left, right):
            return lax.dot_general(
                left, right, (((0,), (0,)), ((), ())), preferred_element_type=f32
            )

        def saved(name):
            return join([s[name] for s in state])

        gb = join(gathered)
        out_term = over_tokens(gb, saved("o"))[:, :local]
        down_term = over_tokens(gb, saved("h"))
        up_term = over_tokens(saved("a1"), join(grad_up))
        qkv_term = over_tokens(saved("a0"), join(grad_mixed))
        qkv_term = qkv_term.reshape(width, 3, LANES)[:, :, :local].reshape(width, 3 * local)
        early = jnp.concatenate([out_term, down_term, up_term], 1).astype(bf16)
        weight_grads[layer] = [
            lax.psum_scatter(item, "wide", scatter_dimension=0, tiled=True)
            for item in (early, qkv_term.astype(bf16))
        ]
        bias = sum(jnp.sum(item.astype(f32), 0) for item in grads)
        norm_grads[layer] = jnp.concatenate([norm_sum.reshape(-1), bias])
        mixed_sum = mixed_sum.reshape(3, LANES)[:, :local].reshape(-1)
        bias_grads[layer] = jnp.concatenate([mixed_sum, up_sum.reshape(-1)])
        input_grads[layer] = [after[index].astype(bf16) for index in range(plan.chunks)]
        grads = input_grads[layer]

    all_grads = plan.exchange(input_grads[0], input_grads[1]).astype(f32)
    totals = []
    for first, second in zip(weight_grads[0], weight_grads[1]):
        mine, other = pick(section, first, second), pick(section, second, first)
        totals.append(mine.astype(f32) + plan.swap(other).astype(f32))
    early, qkv_grad = totals
    out_grad, down_grad = early[:, :local], early[:, local : local + hidden]
    up_grad = early[:, local + hidden :]
    norm_total = lax.psum(
        jnp.stack([norm_grads[0], norm_grads[1]]), ("section", "wide", "tp")
    )
    bias_total = lax.psum(jnp.stack([bias_grads[0], bias_grads[1]]), ("section", "wide"))
    norm_total = pick(section, norm_total[0], norm_total[1])
    bias_total = pick(section, bias_total[0], bias_total[1])
    bias_grad = norm_total[4 * width :]
    return (
        section_outputs[None, :, None],
        all_grads[None, :, None],
        norm_total[: 2 * width].reshape(1, 2, width),
        norm_total[2 * width : 4 * width].reshape(1, 2, width),
        qkv_grad.reshape(1, -1, 3, local),
        bias_total[: 3 * local].reshape(1, 3, local),
        out_grad.T[None],
        bias_grad[None],
        up_grad[None],
        bias_total[3 * local :][None],
        down_grad.T[None],
        bias_grad[None],
    )


def solution(mesh):
    return jax.shard_map(
        on_device,
        mesh=mesh,
        in_specs=(
            P(None, "tp", "wide", None),
            P(None, "tp", "wide", None),
            P(),
            P("section", None, None),
            P("section", None, None),
            P("section", "wide", None, "tp"),
            P("section", None, "tp"),
            P("section", "tp", "wide"),
            P("section", None),
            P("section", "wide", "tp"),
            P("section", "tp"),
            P("section", "tp", "wide"),
            P("section", None),
        ),
        out_specs=(
            P("section", None, "tp", "wide", None),
            P("section", None, "tp", "wide", None),
            P("section", None, None),
            P("section", None, None),
            P("section", "wide", None, "tp"),
            P("section", None, "tp"),
            P("section", "tp", "wide"),
            P("section", None),
            P("section", "wide", "tp"),
            P("section", "tp"),
            P("section", "tp", "wide"),
            P("section", None),
        ),
        check_vma=False,
    )
```

```python
import functools

import jax
import jax.numpy as jnp
import numpy as np
from jax import lax
from jax.experimental import pallas as pl
from jax.experimental.pallas import tpu as pltpu
from jax.sharding import PartitionSpec as P

HEAD_DIM = 64
ROTARY = 16
LANES = 256
CHUNKS = 2
QUERY_BLOCK = 256
KEY_BLOCK = 512
ROW_BLOCK = 256

epsilon = 1e-05
rotary_base = 10000.0
masked_out = -1e30
f32 = jnp.float32
bf16 = jnp.bfloat16
NT = (((1,), (1,)), ((), ()))


def params(size=44):
    return pltpu.CompilerParams(
        dimension_semantics=("arbitrary",), vmem_limit_bytes=size * 1024 * 1024
    )


def dot(left, right):
    return jnp.dot(left, right, preferred_element_type=f32)


def dot_nt(left, right):
    return lax.dot_general(left, right, NT, preferred_element_type=f32)


def rows_spec(rows, columns):
    return pl.BlockSpec((rows, columns), lambda i: (i, 0))


def whole_spec(array):
    return pl.BlockSpec(array.shape, lambda i: (0,) * array.ndim)


def smem_spec():
    return pl.BlockSpec(memory_space=pltpu.SMEM)


def standardize(values):
    centred = values - jnp.mean(values, -1, keepdims=True)
    inverse = lax.rsqrt(jnp.mean(centred * centred, -1, keepdims=True) + epsilon)
    return centred * inverse, inverse


def wide_table(ref):
    return jnp.concatenate([ref[...]] * (LANES // ref.shape[1]), 1)


def halves(signed):
    place = lax.broadcasted_iota(jnp.int32, signed.shape, 1) % HEAD_DIM
    zero = jnp.zeros_like(signed)
    half = ROTARY // 2
    return jnp.where(place < half, signed, zero), jnp.where(place < half, zero, signed)


def turn(values, cosine, signed):
    half = ROTARY // 2
    low, high = halves(signed)
    ahead = pltpu.roll(values, LANES - half, 1)
    behind = pltpu.roll(values, half, 1)
    return values * cosine + ahead * low + behind * high


def turn_back(grads, cosine, signed):
    half = ROTARY // 2
    low, high = halves(signed)
    ahead = pltpu.roll(grads * high, LANES - half, 1)
    behind = pltpu.roll(grads * low, half, 1)
    return grads * cosine + ahead + behind


def any_specs(arrays):
    return [pl.BlockSpec(memory_space=pl.ANY)] * len(arrays)


def cost(micros, transfers):
    return pl.CostEstimate(
        flops=int(micros * 1.15e9), bytes_accessed=int(transfers), transcendentals=0
    )


class View:
    def __init__(self, array, first, width):
        if first % width:
            array, first = array[:, first : first + width], 0
        self.array, self.block, self.shape = array, first // width, (array.shape[0], width)

    def spec(self):
        block = self.block
        return pl.BlockSpec(self.shape, lambda i: (0, block))


def project_kernel(heads, x_ref, gs_ref, w_ref, b_ref, c_ref, s_ref, seg_ref, *rest):
    a0_ref, a1_ref, q_ref, k_ref, v_ref = rest[-5:]
    normed, _ = standardize(x_ref[...].astype(f32))
    first = (normed * gs_ref[0:1] + gs_ref[2:3]).astype(bf16)
    a0_ref[...] = first
    a1_ref[...] = (normed * gs_ref[1:2] + gs_ref[3:4]).astype(bf16)
    mixed = dot(first, w_ref[...]) + b_ref[...]
    cosine, signed = wide_table(c_ref), wide_table(s_ref)
    query = turn(mixed[:, :LANES], cosine, signed)
    keys = turn(mixed[:, LANES : 2 * LANES], cosine, signed)
    lane = lax.broadcasted_iota(jnp.int32, query.shape, 1)
    used = heads * HEAD_DIM
    mine = (lane - used) == seg_ref[...]
    spare = lane >= used
    q_ref[...] = jnp.where(
        spare, jnp.where(mine, 1.0, 0.0), query * HEAD_DIM ** (-0.5)
    ).astype(bf16)
    k_ref[...] = jnp.where(spare, jnp.where(mine, 0.0, masked_out), keys).astype(bf16)
    v_ref[...] = mixed[:, 2 * LANES :].astype(bf16)


def project(x, w, tables, seg, heads, after=()):
    tokens, width = x.shape
    rows = min(ROW_BLOCK, tokens)
    columns = (width, width, LANES, LANES, LANES)
    return pl.pallas_call(
        functools.partial(project_kernel, heads),
        grid=(tokens // rows,),
        in_specs=[rows_spec(rows, width), whole_spec(w["gs"]), w["wq"].spec()]
        + [whole_spec(w["bq"])]
        + [rows_spec(rows, item.shape[1]) for item in tables]
        + [rows_spec(rows, 1)]
        + any_specs(after),
        out_specs=[rows_spec(rows, item) for item in columns],
        out_shape=[jax.ShapeDtypeStruct((tokens, item), bf16) for item in columns],
        compiler_params=params(),
        cost_estimate=cost(4.0 * tokens / 1024, 6 * tokens * width),
        name="project",
    )(x, w["gs"], w["wq"].array, w["bq"], *tables, seg, *after)


def feed_kernel(a_ref, o_ref, wu_ref, bu_ref, wd_ref, wo_ref, *rest):
    h_ref, d_ref, part_ref = rest[-3:]
    before = dot(a_ref[...], wu_ref[...]) + bu_ref[...]
    phi = 0.5 + 0.5 * lax.erf(before * (0.5**0.5))
    density = jnp.exp(before * before * (-0.5)) * 0.3989422804014327
    hidden = (before * phi).astype(bf16)
    h_ref[...] = hidden
    d_ref[...] = (phi + before * density).astype(bf16)
    part_ref[...] = (dot_nt(hidden, wd_ref[...]) + dot_nt(o_ref[...], wo_ref[...])).astype(bf16)


def feed(a1, o, w, after=()):
    tokens, width = a1.shape
    rows = min(ROW_BLOCK, tokens)
    hidden = w["bu"].shape[1]
    columns = (hidden, hidden, width)
    return pl.pallas_call(
        feed_kernel,
        grid=(tokens // rows,),
        in_specs=[rows_spec(rows, width), rows_spec(rows, LANES), w["wu"].spec()]
        + [whole_spec(w["bu"]), w["wd"].spec(), w["wo"].spec()]
        + any_specs(after),
        out_specs=[rows_spec(rows, item) for item in columns],
        out_shape=[jax.ShapeDtypeStruct((tokens, item), bf16) for item in columns],
        compiler_params=params(),
        cost_estimate=cost(5.0 * tokens / 1024, 6 * tokens * width),
        name="feed",
    )(a1, o, w["wu"].array, w["bu"], w["wd"].array, w["wo"].array, *after)


def feed_back_kernel(gb_ref, wd_ref, d_ref, *rest):
    rest[-1][...] = (dot(gb_ref[...], wd_ref[...]) * d_ref[...].astype(f32)).astype(bf16)


def feed_back(gb, w, d, after=()):
    tokens, width = gb.shape
    rows = min(ROW_BLOCK, tokens)
    hidden = d.shape[1]
    return pl.pallas_call(
        feed_back_kernel,
        grid=(tokens // rows,),
        in_specs=[rows_spec(rows, width), w["wd"].spec(), rows_spec(rows, hidden)]
        + any_specs(after),
        out_specs=rows_spec(rows, hidden),
        out_shape=jax.ShapeDtypeStruct((tokens, hidden), bf16),
        compiler_params=params(),
        cost_estimate=cost(2.0 * tokens / 1024, 6 * tokens * width),
        name="feed_back",
    )(gb, w["wd"].array, d, *after)


def head_lanes(array, heads, spare):
    lane = lax.broadcasted_iota(jnp.int32, array.shape, 1)
    zero = jnp.zeros_like(array)
    result = []
    for head in range(heads):
        keep = (lane >= head * HEAD_DIM) & (lane < (head + 1) * HEAD_DIM)
        if spare:
            keep = keep | (lane >= heads * HEAD_DIM)
        result.append(jnp.where(keep, array, zero))
    return result


def join_once(parts, target):
    @pl.when(pl.program_id(0) == 0)
    def _():
        first = 0
        for part in parts:
            target[first : first + part.shape[0], :] = part[...]
            first += part.shape[0]


def attend_kernel(heads, key_block, pieces, start_ref, q_ref, *rest):
    k_refs, v_refs = rest[:pieces], rest[pieces : 2 * pieces]
    o_ref, lse_ref, top_ref, sum_ref, acc_ref, k_ref, vt_ref = rest[-7:]
    join_once(k_refs, k_ref)

    @pl.when(pl.program_id(0) == 0)
    def _():
        acc_ref[...] = jnp.zeros(acc_ref.shape, f32)
        first = 0
        for ref in v_refs:
            block = min(key_block, ref.shape[0])
            for at in range(0, ref.shape[0], block):
                vt_ref[:, first + at : first + at + block] = ref[at : at + block, :].T
            first += ref.shape[0]

    rows = q_ref.shape[0]
    queries = head_lanes(q_ref[...], heads, True)
    first_row = start_ref[0] + pl.program_id(0) * rows
    full = first_row // key_block

    def step(block, diagonal, fresh):
        place = pl.ds(pl.multiple_of(block * key_block, key_block), key_block)
        keys = k_ref[place, :]
        for head in range(heads):
            here = slice(head * HEAD_DIM, (head + 1) * HEAD_DIM)
            line = slice(head, head + 1)
            scores = dot_nt(keys, queries[head])
            if diagonal:
                column = lax.broadcasted_iota(jnp.int32, scores.shape, 0) + block * key_block
                row = lax.broadcasted_iota(jnp.int32, scores.shape, 1) + first_row
                scores = jnp.where(column <= row, scores, masked_out)
            top = jnp.max(scores, 0, keepdims=True)
            if not fresh:
                before = top_ref[line, :]
                top = jnp.maximum(before, top)
                fade = jnp.exp(before - top)
            probs = jnp.exp(scores - top)
            total = jnp.sum(probs, 0, keepdims=True)
            value = dot(vt_ref[here, place], probs.astype(bf16))
            if not fresh:
                total += sum_ref[line, :] * fade
                value += acc_ref[here, :] * fade
            top_ref[line, :] = top
            sum_ref[line, :] = total
            acc_ref[here, :] = value

    step(full, True, True)

    @pl.loop(0, full)
    def _(block):
        step(block, False, False)

    for head in range(heads):
        here = slice(head * HEAD_DIM, (head + 1) * HEAD_DIM)
        acc_ref[here, :] = acc_ref[here, :] / sum_ref[head : head + 1, :]
    o_ref[...] = acc_ref[...].T.astype(bf16)
    lse_ref[...] = jnp.zeros(lse_ref.shape, f32)
    lse_ref[:heads, :] = top_ref[:heads, :] + jnp.log(sum_ref[:heads, :])


def attend(start, q, keys, values, heads, after=()):
    tokens = q.shape[0]
    rows = min(QUERY_BLOCK, tokens)
    span = sum(item.shape[0] for item in keys)
    key_block = min(KEY_BLOCK, span)
    return pl.pallas_call(
        functools.partial(attend_kernel, heads, key_block, len(keys)),
        grid=(tokens // rows,),
        in_specs=[smem_spec(), rows_spec(rows, LANES)]
        + [whole_spec(item) for item in (*keys, *values)]
        + any_specs(after),
        out_specs=[rows_spec(rows, LANES), pl.BlockSpec((8, rows), lambda i: (0, i))],
        out_shape=[
            jax.ShapeDtypeStruct((tokens, LANES), bf16),
            jax.ShapeDtypeStruct((8, tokens), f32),
        ],
        scratch_shapes=[pltpu.VMEM((8, rows), f32)] * 2
        + [pltpu.VMEM((LANES, rows), f32)]
        + [pltpu.VMEM((span, LANES), bf16), pltpu.VMEM((LANES, span), bf16)],
        compiler_params=params(),
        cost_estimate=cost(7.0 * tokens * span / 1024 / 1024, 6 * tokens * LANES),
        name="attend",
    )(start, q, *keys, *values, *after)


def attend_back_kernel(
    heads, key_block, pieces, carried, start_ref, gb_ref, w_ref, q_ref, o_ref, *rest,
):
    lse_ref, rest = rest[0], rest[1:]
    k_refs, v_refs, rest = rest[:pieces], rest[pieces : 2 * pieces], rest[2 * pieces :]
    carry_refs = rest[: 2 * carried]
    dq_ref, rest = rest[-(2 * pieces + 7)], rest[-(2 * pieces + 6) :]
    dk_refs, dv_refs, rest = rest[:pieces], rest[pieces : 2 * pieces], rest[2 * pieces :]
    k_ref, v_ref, kt_ref, dk_ref, dv_ref, dqt_ref = rest
    rows = q_ref.shape[0]
    first_row = start_ref[0] + pl.program_id(0) * rows
    full = first_row // key_block
    join_once(k_refs, k_ref)
    join_once(v_refs, v_ref)

    @pl.when(pl.program_id(0) == 0)
    def _():
        dk_ref[...] = jnp.zeros(dk_ref.shape, f32)
        dv_ref[...] = jnp.zeros(dv_ref.shape, f32)
        for refs, target in ((carry_refs[:carried], dk_ref), (carry_refs[carried:], dv_ref)):
            first = 0
            for ref in refs:
                target[first : first + ref.shape[0], :] = ref[...]
                first += ref.shape[0]
        for first in range(0, k_ref.shape[0], key_block):
            kt_ref[:, first : first + key_block] = k_ref[first : first + key_block, :].T

    grad = gb_ref[...]
    grad_out = dot(grad, w_ref[...]).astype(bf16)
    product = (grad_out.astype(f32) * o_ref[...].astype(f32)).T
    centres = [
        jnp.sum(product[head * HEAD_DIM : (head + 1) * HEAD_DIM], 0, keepdims=True)
        for head in range(heads)
    ]
    queries = head_lanes(q_ref[...], heads, True)
    grads = head_lanes(grad_out, heads, False)
    dqt_ref[...] = jnp.zeros(dqt_ref.shape, f32)

    def step(block, diagonal):
        place = pl.ds(pl.multiple_of(block * key_block, key_block), key_block)
        keys = k_ref[place, :]
        values = v_ref[place, :]
        grad_keys = dk_ref[place, :]
        grad_values = dv_ref[place, :]
        for head in range(heads):
            here = slice(head * HEAD_DIM, (head + 1) * HEAD_DIM)
            scores = dot_nt(keys, queries[head])
            probs = jnp.exp(scores - lse_ref[head : head + 1, :])
            if diagonal:
                column = lax.broadcasted_iota(jnp.int32, scores.shape, 0) + block * key_block
                row = lax.broadcasted_iota(jnp.int32, scores.shape, 1) + first_row
                probs = jnp.where(column <= row, probs, 0.0)
            grad_probs = dot_nt(values, grads[head])
            grad_scores = (probs * (grad_probs - centres[head])).astype(bf16)
            grad_values += dot(probs.astype(bf16), grads[head])
            grad_keys += dot(grad_scores, queries[head])
            dqt_ref[here, :] += dot(kt_ref[here, place], grad_scores)
        dk_ref[place, :] = grad_keys
        dv_ref[place, :] = grad_values

    @pl.loop(0, full)
    def _(block):
        step(block, False)

    step(full, True)
    dq_ref[...] = dqt_ref[...].T * HEAD_DIM ** (-0.5)

    @pl.when(pl.program_id(0) == pl.num_programs(0) - 1)
    def _():
        for refs, source in ((dk_refs, dk_ref), (dv_refs, dv_ref)):
            first = 0
            for ref in refs:
                ref[...] = source[first : first + ref.shape[0], :]
                first += ref.shape[0]


def attend_back(start, gb, w, q, o, lse, keys, values, carried, heads, after=()):
    tokens, width = gb.shape
    rows = min(QUERY_BLOCK, tokens)
    sizes = [item.shape[0] for item in keys]
    span = sum(sizes)
    key_block = min(KEY_BLOCK, span)
    carry_keys, carry_values = carried
    whole = [pl.BlockSpec((size, LANES), lambda i: (0, 0)) for size in sizes]
    result = pl.pallas_call(
        functools.partial(attend_back_kernel, heads, key_block, len(keys), len(carry_keys)),
        grid=(tokens // rows,),
        in_specs=[smem_spec(), rows_spec(rows, width), w["wo"].spec()]
        + [rows_spec(rows, LANES), rows_spec(rows, LANES)]
        + [pl.BlockSpec((8, rows), lambda i: (0, i))]
        + [whole_spec(item) for item in (*keys, *values, *carry_keys, *carry_values)]
        + any_specs(after),
        out_specs=[rows_spec(rows, LANES)] + whole + whole,
        out_shape=[jax.ShapeDtypeStruct((tokens, LANES), f32)]
        + [jax.ShapeDtypeStruct((size, LANES), f32) for size in sizes] * 2,
        scratch_shapes=[pltpu.VMEM((span, LANES), bf16)] * 2
        + [pltpu.VMEM((LANES, span), bf16)]
        + [pltpu.VMEM((span, LANES), f32)] * 2
        + [pltpu.VMEM((LANES, rows), f32)],
        compiler_params=params(),
        cost_estimate=cost(12.5 * tokens * span / 1024 / 1024, 4 * tokens * width),
        name="attend_back",
    )(start, gb, w["wo"].array, q, o, lse, *keys, *values, *carry_keys, *carry_values, *after)
    pieces = len(keys)
    return result[0], result[1 : 1 + pieces], result[1 + pieces :]


def leave_kernel(
    x_ref, gs_ref, dq_ref, dk_ref, dv_ref, gu_ref, wq_ref, wu_ref, c_ref, s_ref, *rest,
):
    gm_ref, e_ref, norm_ref, mixed_ref, up_ref = rest[-5:]

    @pl.when(pl.program_id(0) == 0)
    def _():
        norm_ref[...] = jnp.zeros(norm_ref.shape, f32)
        mixed_ref[...] = jnp.zeros(mixed_ref.shape, f32)
        up_ref[...] = jnp.zeros(up_ref.shape, f32)

    cosine, signed = wide_table(c_ref), wide_table(s_ref)
    grads = jnp.concatenate(
        [
            turn_back(dq_ref[...], cosine, signed),
            turn_back(dk_ref[...], cosine, signed),
            dv_ref[...],
        ],
        1,
    ).astype(bf16)
    gm_ref[...] = grads
    grad_up = gu_ref[...]
    mixed_ref[...] += jnp.sum(grads.astype(f32), 0, keepdims=True)
    up_ref[...] += jnp.sum(grad_up.astype(f32), 0, keepdims=True)
    grad_first = dot_nt(grads, wq_ref[...])
    grad_second = dot_nt(grad_up, wu_ref[...])
    normed, _ = standardize(x_ref[...].astype(f32))
    norm_ref[0:1] += jnp.sum(grad_first * normed, 0, keepdims=True)
    norm_ref[1:2] += jnp.sum(grad_second * normed, 0, keepdims=True)
    norm_ref[2:3] += jnp.sum(grad_first, 0, keepdims=True)
    norm_ref[3:4] += jnp.sum(grad_second, 0, keepdims=True)
    e_ref[...] = (grad_first * gs_ref[0:1] + grad_second * gs_ref[1:2]).astype(bf16)


def leave(x, dq, dk, dv, gu, w, tables, after=()):
    tokens, width = x.shape
    rows = min(ROW_BLOCK, tokens)
    mixed = 3 * LANES
    hidden = gu.shape[1]
    sums = [(4, width), (1, mixed), (1, hidden)]
    return pl.pallas_call(
        leave_kernel,
        grid=(tokens // rows,),
        in_specs=[rows_spec(rows, width), whole_spec(w["gs"])]
        + [rows_spec(rows, LANES)] * 3
        + [rows_spec(rows, hidden), w["wq"].spec(), w["wu"].spec()]
        + [rows_spec(rows, item.shape[1]) for item in tables]
        + any_specs(after),
        out_specs=[rows_spec(rows, mixed), rows_spec(rows, width)]
        + [pl.BlockSpec(item, lambda i: (0, 0)) for item in sums],
        out_shape=[
            jax.ShapeDtypeStruct((tokens, mixed), bf16),
            jax.ShapeDtypeStruct((tokens, width), bf16),
        ]
        + [jax.ShapeDtypeStruct(item, f32) for item in sums],
        compiler_params=params(),
        cost_estimate=cost(6.7 * tokens / 1024, 6 * tokens * width),
        name="leave",
    )(x, w["gs"], dq, dk, dv, gu, w["wq"].array, w["wu"].array, *tables, *after)


def hold(value, token):
    first = token[(slice(0, 1),) * token.ndim].reshape((1,) * value.ndim)
    return jnp.where(first == jnp.inf, jnp.zeros_like(value), value)


def pick(bit, zero, one):
    return jnp.where(bit == 0, zero, one)


def mirrored(index, bits):
    return sum(((index >> bit) & 1) << (bits - 1 - bit) for bit in range(bits))


class Plan:
    def __init__(self, batch, length):
        self.wide, self.tp = lax.axis_size("wide"), lax.axis_size("tp")
        self.batch, self.length = batch, length
        self.bits = self.tp.bit_length() - 1
        self.group = self.wide // batch
        self.sequence_bits = batch.bit_length() - 1
        self.chunks = CHUNKS if self.group == 1 else 1
        self.unit = length // (self.wide * self.chunks)
        self.section = lax.axis_index("section")
        self.wide_index = lax.axis_index("wide")
        self.tp_index = lax.axis_index("tp")
        self.sequence = mirrored(self.wide_index // self.group, self.sequence_bits)
        self.part = mirrored(self.tp_index, self.bits)

    def units(self):
        for unit in range(self.wide * self.chunks):
            owner, half = divmod(unit, self.chunks)
            rest, part = divmod(unit, self.tp)
            sub, chunk = divmod(rest, self.chunks)
            for sequence in range(self.batch):
                place = mirrored(sequence, self.sequence_bits) * self.group + sub
                worker = place * self.tp + mirrored(part, self.bits)
                yield owner * self.tp + sequence, worker, half, chunk, part

    def to_work(self, block):
        chunks = []
        for chunk in range(self.chunks):
            result = None
            for half in range(self.chunks):
                pairs = [u[:2] for u in self.units() if u[2] == half and u[3] == chunk]
                piece = block[half * self.unit : (half + 1) * self.unit]
                piece = lax.ppermute(piece, ("wide", "tp"), pairs)
                if result is None:
                    result = piece
                else:
                    result = jnp.where(self.part % self.chunks == half, piece, result)
            chunks.append(result)
        return chunks

    def to_work_whole(self, block):
        received = []
        own = (self.wide_index * self.chunks // self.tp) % self.chunks
        for turn_index in range(self.chunks):
            piece = block[: self.unit]
            for half in range(1, self.chunks):
                here = (own - turn_index) % self.chunks == half
                piece = jnp.where(here, block[half * self.unit : (half + 1) * self.unit], piece)
            pairs = [u[:2] for u in self.units() if (u[4] + turn_index) % self.chunks == u[3]]
            received.append(lax.ppermute(piece, ("wide", "tp"), pairs))
        chunks = []
        for chunk in range(self.chunks):
            piece = received[0]
            for turn_index in range(1, self.chunks):
                here = (self.part + turn_index) % self.chunks == chunk
                piece = jnp.where(here, received[turn_index], piece)
            chunks.append(piece)
        return chunks

    def to_owner(self, chunks, layer, micro, only=None, both=False):
        devices = self.wide * self.tp
        received = {}
        for turn_index in range(self.chunks):
            for chunk in range(self.chunks) if only is None else [only]:
                pairs = []
                for owner, worker, _, held, part in self.units():
                    moved = held if only is None else only
                    if held == moved and (part + turn_index) % self.chunks == held:
                        pairs.append((micro * devices + worker, layer * devices + owner))
                        if both:
                            pairs.append(
                                ((1 - micro) * devices + worker, (1 - layer) * devices + owner)
                            )
                if only is None:
                    piece = chunks[0]
                    for other in range(1, self.chunks):
                        here = (self.part + turn_index) % self.chunks == other
                        piece = jnp.where(here, chunks[other], piece)
                else:
                    piece = chunks[only]
                received[turn_index] = lax.ppermute(piece, ("section", "wide", "tp"), pairs)
                if only is None:
                    break
        if self.chunks == 1:
            return received[0]
        chunk = (self.wide_index * self.chunks // self.tp) % self.chunks
        ordered = []
        for half in range(self.chunks):
            piece = received[0]
            for turn_index in range(1, self.chunks):
                piece = jnp.where(
                    (chunk - half) % self.chunks == turn_index, received[turn_index], piece
                )
            ordered.append(piece)
        return jnp.concatenate(ordered, 0)

    def exchange(self, first, second):
        mine = [pick(self.section, a, b) for a, b in zip(first, second)]
        other = [pick(self.section, b, a) for a, b in zip(first, second)]
        same, cross = self.to_owner(mine, 0, 0, both=True), self.to_owner(other, 1, 0, both=True)
        return jnp.stack([pick(self.section, same, cross), pick(self.section, cross, same)])

    def owned(self, chunks, layer):
        return jnp.stack([self.to_owner(chunks, layer, micro) for micro in range(2)])

    def owned_late(self, chunks, layer):
        own = (self.wide_index * self.chunks // self.tp) % self.chunks
        result = None
        for chunk in reversed(range(self.chunks)):
            part = jnp.stack([self.to_owner(chunks, layer, micro, chunk) for micro in range(2)])
            result = part if result is None else jnp.where(own == chunk, part, result)
        return result

    def wide_steps(self, value_at):
        return [
            lax.ppermute(
                value_at(step), "wide", [(index, index ^ step) for index in range(self.wide)]
            )
            for step in range(1, self.wide)
        ]

    def wide_gather(self, block):
        if self.wide > 4:
            return lax.all_gather(block, "wide", axis=0, tiled=True)
        pieces = [block] + self.wide_steps(lambda step: block)
        step = 1
        while len(pieces) > 1:
            here = (self.wide_index // step) % 2
            pieces = [
                pick(here, jnp.concatenate([a, b], 0), jnp.concatenate([b, a], 0))
                for a, b in zip(pieces[::2], pieces[1::2])
            ]
            step *= 2
        return pieces[0]

    def wide_scatter(self, block):
        if self.wide > 4:
            return lax.psum_scatter(
                block, "wide", scatter_dimension=0, tiled=True
            ).astype(f32)
        return sum(item.astype(f32) for item in self.wide_steps_of(block))

    def wide_steps_of(self, block):
        if self.wide > 4:
            return [self.wide_scatter(block)]
        rows = block.shape[0] // self.wide

        def share(step):
            first = (self.wide_index ^ step) * rows
            return lax.dynamic_slice_in_dim(block, first, rows, 0)

        return [share(0)] + self.wide_steps(share)

    def send(self, value, source):
        return lax.ppermute(value, "section", [(source, 1 - source)])

    def gather(self, block):
        for bit in reversed(range(self.bits)):
            other = lax.ppermute(
                block, "tp", [(index, index ^ (1 << bit)) for index in range(self.tp)]
            )
            here = (self.tp_index >> bit) & 1
            block = jnp.concatenate([pick(here, block, other), pick(here, other, block)], 0)
        return block

    def scatter_first(self, pieces):
        here = self.tp_index & 1
        if len(pieces) == 1:
            half = pieces[0].shape[0] // 2
            pieces = [pieces[0][:half], pieces[0][half:]]
        other = lax.ppermute(
            pick(here, pieces[1], pieces[0]), "tp", [(i, i ^ 1) for i in range(self.tp)]
        )
        return pick(here, pieces[0], pieces[1]).astype(f32) + other.astype(f32)

    def scatter_rest(self, block):
        for bit in range(1, self.bits):
            half = block.shape[0] // 2
            here = (self.tp_index >> bit) & 1
            sent = pick(here, block[half:], block[:half]).astype(bf16)
            kept = pick(here, block[:half], block[half:])
            other = lax.ppermute(
                sent, "tp", [(index, index ^ (1 << bit)) for index in range(self.tp)]
            )
            block = kept + other.astype(f32)
        return block

    def groups(self):
        return [
            [sequence * self.group + sub for sub in range(self.group)]
            for sequence in range(self.batch)
        ]

    def all_places(self, block):
        if self.group == 1:
            return block
        return lax.all_gather(block, "wide", axis=0, tiled=True, axis_index_groups=self.groups())

    def own_places(self, block):
        if self.group == 1:
            return block
        return lax.psum_scatter(
            block.astype(bf16), "wide", scatter_dimension=0, tiled=True,
            axis_index_groups=self.groups(),
        ).astype(f32)


def angle_tables(length):
    half = ROTARY // 2
    freqs = np.float32(rotary_base) ** (-(2.0 * np.arange(half, dtype=np.float32)) / ROTARY)
    turned = np.arange(length, dtype=np.float32)[:, None] * freqs[None, :].astype(np.float32)
    cosine, sine = np.cos(turned), np.sin(turned)
    rest = np.zeros((length, HEAD_DIM - ROTARY), np.float32)
    return (
        np.concatenate([cosine, cosine, rest + 1.0] * 2, 1).astype(np.float32),
        np.concatenate([-sine, sine, rest] * 2, 1).astype(np.float32),
    )


def on_device(
    inputs, cotangent, segment_ids, norm_gain, norm_shift, qkv_weight, qkv_bias, out_weight,
    out_bias, up_weight, up_bias, down_weight, down_bias,
):
    batch, length = segment_ids.shape[1], segment_ids.shape[2]
    plan = Plan(batch, length)
    width = inputs.shape[-1]
    local = qkv_weight.shape[-1]
    hidden = up_weight.shape[-1]
    heads = local // HEAD_DIM
    section = plan.section
    space = LANES - local

    fill = ((0, 0), (0, 0), (0, space))
    qkv = qkv_weight[0].reshape(-1, 3 * local)
    up = up_weight[0]
    leaving = jnp.concatenate(
        [down_weight[0].T, jnp.pad(out_weight[0].T, ((0, 0), (0, space)))], 1
    )
    small = jnp.concatenate(
        [
            norm_gain[0].reshape(-1), norm_shift[0].reshape(-1), out_bias[0] + down_bias[0],
            jnp.pad(qkv_bias[0], ((0, 0), (0, space))).reshape(-1), up_bias[0],
        ]
    )
    qkv_there = plan.send(qkv, 0)
    source = plan.to_work(jnp.where(section == 0, inputs[0, 0], inputs[1, 0]))
    small_there = lax.ppermute(small, "section", [(0, 1), (1, 0)])
    rest = jnp.concatenate([up, leaving], 1)
    share = rest.shape[0] // 2
    first = section == 0
    halves_there = [plan.send(rest[share:], 0), plan.send(rest[:share], 1)]
    half_rests = [
        jnp.where(first, rest[:share], halves_there[0]),
        jnp.where(first, halves_there[1], rest[share:]),
    ]

    def gather_rest(half):
        return lax.all_gather(half, ("wide", "section"), axis=0, tiled=True)

    def gather_qkv(value):
        value = plan.wide_gather(value).reshape(width, 3, local)
        return jnp.pad(value, fill).reshape(width, 3 * LANES)

    wq = gather_qkv(jnp.where(first, qkv, qkv_there))
    rests = [gather_rest(half_rests[0])]
    mixed = 3 * LANES
    layers = [dict(wq=View(wq, 0, mixed)), {}]

    def views(array):
        return dict(
            wu=View(array, 0, hidden), wd=View(array, hidden, hidden),
            wo=View(array, 2 * hidden, LANES),
        )

    layers[0].update(views(rests[0]))
    for layer, w in enumerate(layers):
        values = jnp.where(section == layer, small, small_there)
        at = 5 * width
        w["gs"] = values[: 4 * width].reshape(4, width)
        w["after"] = values[4 * width : at]
        w["bq"] = values[at : at + mixed].reshape(1, mixed)
        w["bu"] = values[at + mixed :].reshape(1, hidden)

    segments = lax.dynamic_index_in_dim(segment_ids, section, 0, False)
    segments = lax.dynamic_index_in_dim(segments, plan.sequence, 0, False)
    sub_length = length // plan.group
    first_place = (plan.wide_index % plan.group) * sub_length
    tables = angle_tables(length)
    if plan.group > 1:
        segments = lax.dynamic_slice_in_dim(segments, first_place, sub_length, 0)
        tables = [lax.dynamic_slice_in_dim(t, first_place, sub_length, 0) for t in tables]
    size = plan.unit * plan.tp
    starts = [(first_place + index * size).reshape(1) for index in range(plan.chunks)]
    spans = [slice(index * size, (index + 1) * size) for index in range(plan.chunks)]
    chunk_tables = [[jnp.asarray(table[span]) for table in tables] for span in spans]
    chunk_segments = [segments[span].reshape(-1, 1) for span in spans]
    last = plan.chunks - 1

    outputs, kept = [], []
    blocks = source

    def finished(index, pending, blocks, w):
        done = plan.scatter_rest(pending)
        return (blocks[index].astype(f32) + done + w["after"]).astype(bf16)

    for layer in range(2):
        w = layers[layer]
        state, after, pending = [], [], []
        keys, values = [], []
        for index in range(plan.chunks):
            x = plan.gather(blocks[index])
            a0, a1, q, k, v = project(x, w, chunk_tables[index], chunk_segments[index], heads)
            keys, values = keys + [plan.all_places(k)], values + [plan.all_places(v)]
            tied = ()
            if layer > 0 and pending:
                tied = (pending[-1],)
            o, lse = attend(starts[index], q, keys, values, heads, tied)
            state.append(dict(x=x, a0=a0, a1=a1, q=q, o=o, lse=lse, k=keys, v=values))
            if layer == 0 and index == 0:
                there = plan.send(hold(qkv, q), 1)
                there = gather_qkv(jnp.where(first, there, qkv))
                layers[1]["wq"] = View(there, 0, mixed)
                layers[1].update(views(gather_rest(hold(half_rests[1], rests[0]))))
            if layer > 0:
                if pending:
                    after.append(finished(index - 1, pending[-1], blocks, w))
                s = state[index]
                s["h"], s["d"], part = feed(a1, o, w, tuple(after))
                pending.append(plan.scatter_first([part]))
        if layer == 0:
            for index, s in enumerate(state):
                s["h"], s["d"], part = feed(s["a1"], s["o"], w)
                pending.append(plan.scatter_first([part]))
        while len(after) < plan.chunks:
            after.append(finished(len(after), pending[len(after)], blocks, w))
        kept.append((blocks, state))
        outputs.append(after)
        blocks = after

    grads = jnp.where(section == 0, cotangent[0, 0], cotangent[1, 0])
    grads = plan.to_work_whole(hold(grads, kept[1][1][0]["q"]))
    gathered = {index: plan.gather(grads[index]) for index in reversed(range(plan.chunks))}
    held = [hold(item, gathered[0]) for item in outputs[0]]
    section_outputs = plan.exchange(held, outputs[1])
    input_grads, weight_grads, small_grads = {}, {}, {}

    def over_tokens(left, right):
        left, right = jnp.concatenate(left, 0), jnp.concatenate(right, 0)
        return lax.dot_general(left, right, (((0,), (0,)), ((), ())), preferred_element_type=f32)

    for layer in reversed(range(2)):
        w = layers[layer]
        blocks, state = kept[layer]
        carried = ((), ())
        after, pending = {}, {}
        if layer == 0:
            gathered = {
                index: plan.gather(grads[index]) for index in reversed(range(plan.chunks))
            }
        every_grad = [gathered[index] for index in range(plan.chunks)]
        grad_up, grad_mixed, sums = {}, {}, 0.0
        for index in reversed(range(plan.chunks)):
            s = state[index]
            dq, dk, dv = attend_back(
                starts[index], gathered[index], w, s["q"], s["o"], s["lse"],
                s["k"], s["v"], carried, heads,
            )
            carried = (dk[:-1], dv[:-1])
            dk, dv = plan.own_places(dk[-1]), plan.own_places(dv[-1])
            if index == last:
                for other in reversed(range(plan.chunks)):
                    grad_up[other] = feed_back(gathered[other], w, state[other]["d"])
                ups = [grad_up[other] for other in range(plan.chunks)]
                early = [
                    over_tokens(every_grad, [s["o"] for s in state])[:, :local].astype(bf16),
                    over_tokens(every_grad, [s["h"] for s in state]).astype(bf16),
                    over_tokens([s["a1"] for s in state], ups).astype(bf16),
                ]
                if layer == 0:
                    early = jnp.concatenate(early, 1)
            tied = ()
            if index < last:
                tied = (pending[index + 1],)
            gm, e, norm_part, mixed_part, up_part = leave(
                s["x"], dq, dk, dv, grad_up[index], w, chunk_tables[index], tied
            )
            mixed_part = mixed_part.reshape(3, LANES)[:, :local].reshape(-1)
            sums += jnp.concatenate([norm_part.reshape(-1), mixed_part, up_part.reshape(-1)])
            pending[index] = plan.scatter_first([e])
            if layer == 0 and index == last:
                early = plan.wide_steps_of(early)
            if layer == 0 and index == last:
                held = [hold(item, dq) for item in input_grads[1]]
                owned_second = plan.owned(held, 1)
            grad_mixed[index] = gm
        for index in reversed(range(plan.chunks)):
            scaled = plan.scatter_rest(pending[index])
            normed, inverse = standardize(blocks[index].astype(f32))
            after[index] = grads[index].astype(f32) + inverse * (
                scaled
                - jnp.mean(scaled, -1, keepdims=True)
                - normed * jnp.mean(scaled * normed, -1, keepdims=True)
            )
        qkv_term = over_tokens(
            [s["a0"] for s in state], [grad_mixed[index] for index in range(plan.chunks)]
        )
        qkv_term = qkv_term.reshape(width, 3, LANES)[:, :, :local].reshape(width, 3 * local)
        if layer == 0:
            early = sum(hold(item, gm).astype(f32) for item in early)
            weight_grads[0] = [early, plan.wide_scatter(qkv_term.astype(bf16))]
        else:
            weight_grads[1] = lax.psum_scatter(
                jnp.concatenate(early + [qkv_term.astype(bf16)], 1),
                ("wide", "section"), scatter_dimension=0, tiled=True,
            )
        bias = sum(jnp.sum(item.astype(f32), 0) for item in grads)
        small_grads[layer] = jnp.concatenate([sums, bias])
        input_grads[layer] = [after[index].astype(bf16) for index in range(plan.chunks)]
        grads = input_grads[layer]

    owned_grads = [plan.owned_late(input_grads[0], 0), owned_second]
    all_grads = pick(section, *owned_grads).astype(f32)
    early, qkv_grad = [
        item + plan.send(item.astype(bf16), 1).astype(f32) for item in weight_grads[0]
    ]
    half = weight_grads[1]
    whole = jnp.concatenate([plan.send(half, 0), half], 0).astype(f32)
    split = local + 2 * hidden
    early, qkv_grad = pick(section, early, whole[:, :split]), pick(section, qkv_grad, whole[:, split:])
    out_grad, down_grad = early[:, :local], early[:, local : local + hidden]
    up_grad = early[:, local + hidden :]
    total = jnp.stack([small_grads[0], small_grads[1]])
    total = lax.all_gather(total, ("section", "wide", "tp"), axis=0)
    total = pick(section, total[:, 0], total[:, 1]).reshape(2 * plan.wide, plan.tp, -1)
    total = jnp.sum(total, 0)
    at = 4 * width + 3 * local
    own = lax.dynamic_index_in_dim(total, plan.tp_index, 0, False)[4 * width : at + hidden]
    shared = jnp.sum(total, 0)
    shared = jnp.concatenate([shared[: 4 * width], shared[at + hidden :]])
    bias_grad = shared[4 * width :]
    return (
        section_outputs[None, :, None],
        all_grads[None, :, None],
        shared[: 2 * width].reshape(1, 2, width),
        shared[2 * width : 4 * width].reshape(1, 2, width),
        qkv_grad.reshape(1, -1, 3, local),
        own[: 3 * local].reshape(1, 3, local),
        out_grad.T[None],
        bias_grad[None],
        up_grad[None],
        own[3 * local :][None],
        down_grad.T[None],
        bias_grad[None],
    )


def solution(mesh):
    return jax.shard_map(
        on_device,
        mesh=mesh,
        in_specs=(
            P(None, "tp", "wide", None),
            P(None, "tp", "wide", None),
            P(),
            P("section", None, None),
            P("section", None, None),
            P("section", "wide", None, "tp"),
            P("section", None, "tp"),
            P("section", "tp", "wide"),
            P("section", None),
            P("section", "wide", "tp"),
            P("section", "tp"),
            P("section", "tp", "wide"),
            P("section", None),
        ),
        out_specs=(
            P("section", None, "tp", "wide", None),
            P("section", None, "tp", "wide", None),
            P("section", None, None),
            P("section", None, None),
            P("section", "wide", None, "tp"),
            P("section", None, "tp"),
            P("section", "tp", "wide"),
            P("section", None),
            P("section", "wide", "tp"),
            P("section", "tp"),
            P("section", "tp", "wide"),
            P("section", None),
        ),
        check_vma=False,
    )
```

```python
import functools

import jax
import jax.numpy as jnp
import numpy as np
from jax import lax
from jax.experimental import pallas as pl
from jax.experimental.pallas import tpu as pltpu
from jax.sharding import PartitionSpec as P

HEAD_DIM = 64
ROTARY = 16
LANES = 256
CHUNKS = 1
QUERY_BLOCK = 256
KEY_BLOCK = 512
ROW_BLOCK = 256

epsilon = 1e-05
rotary_base = 10000.0
masked_out = -1e30
f32 = jnp.float32
bf16 = jnp.bfloat16
NT = (((1,), (1,)), ((), ()))


def params(size=44):
    return pltpu.CompilerParams(
        dimension_semantics=("arbitrary",), vmem_limit_bytes=size * 1024 * 1024
    )


def dot(left, right):
    return jnp.dot(left, right, preferred_element_type=f32)


def dot_nt(left, right):
    return lax.dot_general(left, right, NT, preferred_element_type=f32)


def rows_spec(rows, columns):
    return pl.BlockSpec((rows, columns), lambda i: (i, 0))


def whole_spec(array):
    return pl.BlockSpec(array.shape, lambda i: (0,) * array.ndim)


def smem_spec():
    return pl.BlockSpec(memory_space=pltpu.SMEM)


def standardize(values):
    centred = values - jnp.mean(values, -1, keepdims=True)
    inverse = lax.rsqrt(jnp.mean(centred * centred, -1, keepdims=True) + epsilon)
    return centred * inverse, inverse


def wide_table(ref):
    return jnp.concatenate([ref[...]] * (LANES // ref.shape[1]), 1)


def halves(signed):
    place = lax.broadcasted_iota(jnp.int32, signed.shape, 1) % HEAD_DIM
    zero = jnp.zeros_like(signed)
    half = ROTARY // 2
    return jnp.where(place < half, signed, zero), jnp.where(place < half, zero, signed)


def turn(values, cosine, signed):
    half = ROTARY // 2
    low, high = halves(signed)
    ahead = pltpu.roll(values, LANES - half, 1)
    behind = pltpu.roll(values, half, 1)
    return values * cosine + ahead * low + behind * high


def turn_back(grads, cosine, signed):
    half = ROTARY // 2
    low, high = halves(signed)
    ahead = pltpu.roll(grads * high, LANES - half, 1)
    behind = pltpu.roll(grads * low, half, 1)
    return grads * cosine + ahead + behind


def any_specs(arrays):
    return [pl.BlockSpec(memory_space=pl.ANY)] * len(arrays)


def cost(micros, transfers):
    return pl.CostEstimate(
        flops=int(micros * 1.15e9), bytes_accessed=int(transfers), transcendentals=0
    )


class View:
    def __init__(self, array, first, width, part=0, parts=1):
        if first % width:
            array, first = array[:, first : first + width], 0
        self.array, self.block = array, (part, first // width)
        self.shape = (array.shape[0] // parts, width)

    def spec(self):
        block = self.block
        return pl.BlockSpec(self.shape, lambda i: block)


def project_kernel(heads, x_ref, gs_ref, w_ref, b_ref, c_ref, s_ref, seg_ref, *rest):
    a0_ref, a1_ref, q_ref, k_ref, v_ref = rest[-5:]
    normed, _ = standardize(x_ref[...].astype(f32))
    first = (normed * gs_ref[0:1] + gs_ref[2:3]).astype(bf16)
    a0_ref[...] = first
    a1_ref[...] = (normed * gs_ref[1:2] + gs_ref[3:4]).astype(bf16)
    mixed = dot(first, w_ref[...]) + b_ref[...]
    cosine, signed = wide_table(c_ref), wide_table(s_ref)
    query = turn(mixed[:, :LANES], cosine, signed)
    keys = turn(mixed[:, LANES : 2 * LANES], cosine, signed)
    lane = lax.broadcasted_iota(jnp.int32, query.shape, 1)
    used = heads * HEAD_DIM
    mine = (lane - used) == seg_ref[...]
    spare = lane >= used
    q_ref[...] = jnp.where(
        spare, jnp.where(mine, 1.0, 0.0), query * HEAD_DIM ** (-0.5)
    ).astype(bf16)
    k_ref[...] = jnp.where(spare, jnp.where(mine, 0.0, masked_out), keys).astype(bf16)
    v_ref[...] = mixed[:, 2 * LANES :].astype(bf16)


def project(x, w, tables, seg, heads, after=()):
    tokens, width = x.shape
    rows = min(ROW_BLOCK, tokens)
    columns = (width, width, LANES, LANES, LANES)
    return pl.pallas_call(
        functools.partial(project_kernel, heads),
        grid=(tokens // rows,),
        in_specs=[rows_spec(rows, width), whole_spec(w["gs"]), w["wq"].spec()]
        + [whole_spec(w["bq"])]
        + [rows_spec(rows, item.shape[1]) for item in tables]
        + [rows_spec(rows, 1)]
        + any_specs(after),
        out_specs=[rows_spec(rows, item) for item in columns],
        out_shape=[jax.ShapeDtypeStruct((tokens, item), bf16) for item in columns],
        compiler_params=params(),
        cost_estimate=cost(4.0 * tokens / 1024, 6 * tokens * width),
        name="project",
    )(x, w["gs"], w["wq"].array, w["bq"], *tables, seg, *after)


def feed_kernel(a_ref, o_ref, wu_ref, bu_ref, wd_ref, wo_ref, *rest):
    h_ref, d_ref, part_ref = rest[-3:]
    before = dot(a_ref[...], wu_ref[...]) + bu_ref[...]
    phi = 0.5 + 0.5 * lax.erf(before * (0.5**0.5))
    density = jnp.exp(before * before * (-0.5)) * 0.3989422804014327
    hidden = (before * phi).astype(bf16)
    h_ref[...] = hidden
    d_ref[...] = (phi + before * density).astype(bf16)
    part_ref[...] = (dot_nt(hidden, wd_ref[...]) + dot_nt(o_ref[...], wo_ref[...])).astype(bf16)


def feed(a1, o, w, after=()):
    tokens, width = a1.shape
    rows = min(ROW_BLOCK, tokens)
    hidden = w["bu"].shape[1]
    columns = (hidden, hidden, width)
    return pl.pallas_call(
        feed_kernel,
        grid=(tokens // rows,),
        in_specs=[rows_spec(rows, width), rows_spec(rows, LANES), w["wu"].spec()]
        + [whole_spec(w["bu"]), w["wd"].spec(), w["wo"].spec()]
        + any_specs(after),
        out_specs=[rows_spec(rows, item) for item in columns],
        out_shape=[jax.ShapeDtypeStruct((tokens, item), bf16) for item in columns],
        compiler_params=params(),
        cost_estimate=cost(5.0 * tokens / 1024, 6 * tokens * width),
        name="feed",
    )(a1, o, w["wu"].array, w["bu"], w["wd"].array, w["wo"].array, *after)


def feed_back_kernel(gb_ref, wd_ref, d_ref, *rest):
    rest[-1][...] = (dot(gb_ref[...], wd_ref[...]) * d_ref[...].astype(f32)).astype(bf16)


def feed_back(gb, w, d, after=()):
    tokens, width = gb.shape
    rows = min(ROW_BLOCK, tokens)
    hidden = d.shape[1]
    return pl.pallas_call(
        feed_back_kernel,
        grid=(tokens // rows,),
        in_specs=[rows_spec(rows, width), w["wd"].spec(), rows_spec(rows, hidden)]
        + any_specs(after),
        out_specs=rows_spec(rows, hidden),
        out_shape=jax.ShapeDtypeStruct((tokens, hidden), bf16),
        compiler_params=params(),
        cost_estimate=cost(2.0 * tokens / 1024, 6 * tokens * width),
        name="feed_back",
    )(gb, w["wd"].array, d, *after)


def head_lanes(array, heads, spare):
    lane = lax.broadcasted_iota(jnp.int32, array.shape, 1)
    zero = jnp.zeros_like(array)
    result = []
    for head in range(heads):
        keep = (lane >= head * HEAD_DIM) & (lane < (head + 1) * HEAD_DIM)
        if spare:
            keep = keep | (lane >= heads * HEAD_DIM)
        result.append(jnp.where(keep, array, zero))
    return result


def join_once(parts, target):
    @pl.when(pl.program_id(0) == 0)
    def _():
        first = 0
        for part in parts:
            target[first : first + part.shape[0], :] = part[...]
            first += part.shape[0]


def attend_kernel(heads, key_block, pieces, start_ref, q_ref, *rest):
    k_refs, v_refs = rest[:pieces], rest[pieces : 2 * pieces]
    o_ref, lse_ref, top_ref, sum_ref, acc_ref, k_ref, vt_ref = rest[-7:]
    join_once(k_refs, k_ref)

    @pl.when(pl.program_id(0) == 0)
    def _():
        acc_ref[...] = jnp.zeros(acc_ref.shape, f32)
        first = 0
        for ref in v_refs:
            block = min(key_block, ref.shape[0])
            for at in range(0, ref.shape[0], block):
                vt_ref[:, first + at : first + at + block] = ref[at : at + block, :].T
            first += ref.shape[0]

    rows = q_ref.shape[0]
    queries = head_lanes(q_ref[...], heads, True)
    first_row = start_ref[0] + pl.program_id(0) * rows
    full = first_row // key_block

    def step(block, diagonal, fresh):
        place = pl.ds(pl.multiple_of(block * key_block, key_block), key_block)
        keys = k_ref[place, :]
        for head in range(heads):
            here = slice(head * HEAD_DIM, (head + 1) * HEAD_DIM)
            line = slice(head, head + 1)
            scores = dot_nt(keys, queries[head])
            if diagonal:
                column = lax.broadcasted_iota(jnp.int32, scores.shape, 0) + block * key_block
                row = lax.broadcasted_iota(jnp.int32, scores.shape, 1) + first_row
                scores = jnp.where(column <= row, scores, masked_out)
            top = jnp.max(scores, 0, keepdims=True)
            if not fresh:
                before = top_ref[line, :]
                top = jnp.maximum(before, top)
                fade = jnp.exp(before - top)
            probs = jnp.exp(scores - top)
            total = jnp.sum(probs, 0, keepdims=True)
            value = dot(vt_ref[here, place], probs.astype(bf16))
            if not fresh:
                total += sum_ref[line, :] * fade
                value += acc_ref[here, :] * fade
            top_ref[line, :] = top
            sum_ref[line, :] = total
            acc_ref[here, :] = value

    step(full, True, True)

    @pl.loop(0, full)
    def _(block):
        step(block, False, False)

    for head in range(heads):
        here = slice(head * HEAD_DIM, (head + 1) * HEAD_DIM)
        acc_ref[here, :] = acc_ref[here, :] / sum_ref[head : head + 1, :]
    o_ref[...] = acc_ref[...].T.astype(bf16)
    lse_ref[...] = jnp.zeros(lse_ref.shape, f32)
    lse_ref[:heads, :] = top_ref[:heads, :] + jnp.log(sum_ref[:heads, :])


def attend(start, q, keys, values, heads, after=()):
    tokens = q.shape[0]
    rows = min(QUERY_BLOCK, tokens)
    span = sum(item.shape[0] for item in keys)
    key_block = min(KEY_BLOCK, span)
    return pl.pallas_call(
        functools.partial(attend_kernel, heads, key_block, len(keys)),
        grid=(tokens // rows,),
        in_specs=[smem_spec(), rows_spec(rows, LANES)]
        + [whole_spec(item) for item in (*keys, *values)]
        + any_specs(after),
        out_specs=[rows_spec(rows, LANES), pl.BlockSpec((8, rows), lambda i: (0, i))],
        out_shape=[
            jax.ShapeDtypeStruct((tokens, LANES), bf16),
            jax.ShapeDtypeStruct((8, tokens), f32),
        ],
        scratch_shapes=[pltpu.VMEM((8, rows), f32)] * 2
        + [pltpu.VMEM((LANES, rows), f32)]
        + [pltpu.VMEM((span, LANES), bf16), pltpu.VMEM((LANES, span), bf16)],
        compiler_params=params(),
        cost_estimate=cost(7.0 * tokens * span / 1024 / 1024, 6 * tokens * LANES),
        name="attend",
    )(start, q, *keys, *values, *after)


def attend_back_kernel(
    heads, key_block, pieces, carried, start_ref, gb_ref, w_ref, q_ref, o_ref, *rest,
):
    lse_ref, rest = rest[0], rest[1:]
    k_refs, v_refs, rest = rest[:pieces], rest[pieces : 2 * pieces], rest[2 * pieces :]
    carry_refs = rest[: 2 * carried]
    dq_ref, rest = rest[-(2 * pieces + 7)], rest[-(2 * pieces + 6) :]
    dk_refs, dv_refs, rest = rest[:pieces], rest[pieces : 2 * pieces], rest[2 * pieces :]
    k_ref, v_ref, kt_ref, dk_ref, dv_ref, dqt_ref = rest
    rows = q_ref.shape[0]
    first_row = start_ref[0] + pl.program_id(0) * rows
    full = first_row // key_block
    join_once(k_refs, k_ref)
    join_once(v_refs, v_ref)

    @pl.when(pl.program_id(0) == 0)
    def _():
        dk_ref[...] = jnp.zeros(dk_ref.shape, f32)
        dv_ref[...] = jnp.zeros(dv_ref.shape, f32)
        for refs, target in ((carry_refs[:carried], dk_ref), (carry_refs[carried:], dv_ref)):
            first = 0
            for ref in refs:
                target[first : first + ref.shape[0], :] = ref[...]
                first += ref.shape[0]
        for first in range(0, k_ref.shape[0], key_block):
            kt_ref[:, first : first + key_block] = k_ref[first : first + key_block, :].T

    grad = gb_ref[...]
    grad_out = dot(grad, w_ref[...]).astype(bf16)
    product = (grad_out.astype(f32) * o_ref[...].astype(f32)).T
    centres = [
        jnp.sum(product[head * HEAD_DIM : (head + 1) * HEAD_DIM], 0, keepdims=True)
        for head in range(heads)
    ]
    queries = head_lanes(q_ref[...], heads, True)
    grads = head_lanes(grad_out, heads, False)
    dqt_ref[...] = jnp.zeros(dqt_ref.shape, f32)

    def step(block, diagonal):
        place = pl.ds(pl.multiple_of(block * key_block, key_block), key_block)
        keys = k_ref[place, :]
        values = v_ref[place, :]
        grad_keys = dk_ref[place, :]
        grad_values = dv_ref[place, :]
        for head in range(heads):
            here = slice(head * HEAD_DIM, (head + 1) * HEAD_DIM)
            scores = dot_nt(keys, queries[head])
            probs = jnp.exp(scores - lse_ref[head : head + 1, :])
            if diagonal:
                column = lax.broadcasted_iota(jnp.int32, scores.shape, 0) + block * key_block
                row = lax.broadcasted_iota(jnp.int32, scores.shape, 1) + first_row
                probs = jnp.where(column <= row, probs, 0.0)
            grad_probs = dot_nt(values, grads[head])
            grad_scores = (probs * (grad_probs - centres[head])).astype(bf16)
            grad_values += dot(probs.astype(bf16), grads[head])
            grad_keys += dot(grad_scores, queries[head])
            dqt_ref[here, :] += dot(kt_ref[here, place], grad_scores)
        dk_ref[place, :] = grad_keys
        dv_ref[place, :] = grad_values

    @pl.loop(0, full)
    def _(block):
        step(block, False)

    step(full, True)
    dq_ref[...] = dqt_ref[...].T * HEAD_DIM ** (-0.5)

    @pl.when(pl.program_id(0) == pl.num_programs(0) - 1)
    def _():
        for refs, source in ((dk_refs, dk_ref), (dv_refs, dv_ref)):
            first = 0
            for ref in refs:
                ref[...] = source[first : first + ref.shape[0], :]
                first += ref.shape[0]


def attend_back(start, gb, w, q, o, lse, keys, values, carried, heads, after=()):
    tokens, width = gb.shape
    rows = min(QUERY_BLOCK, tokens)
    sizes = [item.shape[0] for item in keys]
    span = sum(sizes)
    key_block = min(KEY_BLOCK, span)
    carry_keys, carry_values = carried
    whole = [pl.BlockSpec((size, LANES), lambda i: (0, 0)) for size in sizes]
    result = pl.pallas_call(
        functools.partial(attend_back_kernel, heads, key_block, len(keys), len(carry_keys)),
        grid=(tokens // rows,),
        in_specs=[smem_spec(), rows_spec(rows, width), w["wo"].spec()]
        + [rows_spec(rows, LANES), rows_spec(rows, LANES)]
        + [pl.BlockSpec((8, rows), lambda i: (0, i))]
        + [whole_spec(item) for item in (*keys, *values, *carry_keys, *carry_values)]
        + any_specs(after),
        out_specs=[rows_spec(rows, LANES)] + whole + whole,
        out_shape=[jax.ShapeDtypeStruct((tokens, LANES), f32)]
        + [jax.ShapeDtypeStruct((size, LANES), f32) for size in sizes] * 2,
        scratch_shapes=[pltpu.VMEM((span, LANES), bf16)] * 2
        + [pltpu.VMEM((LANES, span), bf16)]
        + [pltpu.VMEM((span, LANES), f32)] * 2
        + [pltpu.VMEM((LANES, rows), f32)],
        compiler_params=params(),
        cost_estimate=cost(12.5 * tokens * span / 1024 / 1024, 4 * tokens * width),
        name="attend_back",
    )(start, gb, w["wo"].array, q, o, lse, *keys, *values, *carry_keys, *carry_values, *after)
    pieces = len(keys)
    return result[0], result[1 : 1 + pieces], result[1 + pieces :]


def leave_kernel(
    x_ref, gs_ref, dq_ref, dk_ref, dv_ref, gu_ref, wq_ref, wu_ref, c_ref, s_ref, *rest,
):
    gm_ref, e_ref, norm_ref, mixed_ref, up_ref = rest[-5:]

    @pl.when(pl.program_id(0) == 0)
    def _():
        norm_ref[...] = jnp.zeros(norm_ref.shape, f32)
        mixed_ref[...] = jnp.zeros(mixed_ref.shape, f32)
        up_ref[...] = jnp.zeros(up_ref.shape, f32)

    cosine, signed = wide_table(c_ref), wide_table(s_ref)
    grads = jnp.concatenate(
        [
            turn_back(dq_ref[...], cosine, signed),
            turn_back(dk_ref[...], cosine, signed),
            dv_ref[...],
        ],
        1,
    ).astype(bf16)
    gm_ref[...] = grads
    grad_up = gu_ref[...]
    mixed_ref[...] += jnp.sum(grads.astype(f32), 0, keepdims=True)
    up_ref[...] += jnp.sum(grad_up.astype(f32), 0, keepdims=True)
    grad_first = dot_nt(grads, wq_ref[...])
    grad_second = dot_nt(grad_up, wu_ref[...])
    normed, _ = standardize(x_ref[...].astype(f32))
    norm_ref[0:1] += jnp.sum(grad_first * normed, 0, keepdims=True)
    norm_ref[1:2] += jnp.sum(grad_second * normed, 0, keepdims=True)
    norm_ref[2:3] += jnp.sum(grad_first, 0, keepdims=True)
    norm_ref[3:4] += jnp.sum(grad_second, 0, keepdims=True)
    e_ref[...] = (grad_first * gs_ref[0:1] + grad_second * gs_ref[1:2]).astype(bf16)


def leave(x, dq, dk, dv, gu, w, tables, after=()):
    tokens, width = x.shape
    rows = min(ROW_BLOCK, tokens)
    mixed = 3 * LANES
    hidden = gu.shape[1]
    sums = [(4, width), (1, mixed), (1, hidden)]
    return pl.pallas_call(
        leave_kernel,
        grid=(tokens // rows,),
        in_specs=[rows_spec(rows, width), whole_spec(w["gs"])]
        + [rows_spec(rows, LANES)] * 3
        + [rows_spec(rows, hidden), w["wq"].spec(), w["wu"].spec()]
        + [rows_spec(rows, item.shape[1]) for item in tables]
        + any_specs(after),
        out_specs=[rows_spec(rows, mixed), rows_spec(rows, width)]
        + [pl.BlockSpec(item, lambda i: (0, 0)) for item in sums],
        out_shape=[
            jax.ShapeDtypeStruct((tokens, mixed), bf16),
            jax.ShapeDtypeStruct((tokens, width), bf16),
        ]
        + [jax.ShapeDtypeStruct(item, f32) for item in sums],
        compiler_params=params(),
        cost_estimate=cost(6.7 * tokens / 1024, 6 * tokens * width),
        name="leave",
    )(x, w["gs"], dq, dk, dv, gu, w["wq"].array, w["wu"].array, *tables, *after)


def hold(value, *tokens):
    for token in tokens:
        first = token[(slice(0, 1),) * token.ndim].reshape((1,) * value.ndim)
        value = jnp.where(first == jnp.inf, jnp.zeros_like(value), value)
    return value


def pick(bit, zero, one):
    return jnp.where(bit == 0, zero, one)


def mirrored(index, bits):
    return sum(((index >> bit) & 1) << (bits - 1 - bit) for bit in range(bits))


class Plan:
    def __init__(self, batch, length):
        self.wide, self.tp = lax.axis_size("wide"), lax.axis_size("tp")
        self.batch, self.length = batch, length
        self.bits = self.tp.bit_length() - 1
        self.group = self.wide // batch
        self.sequence_bits = batch.bit_length() - 1
        self.chunks = CHUNKS if self.group == 1 else 1
        self.unit = length // (self.wide * self.chunks)
        self.section = lax.axis_index("section")
        self.wide_index = lax.axis_index("wide")
        self.tp_index = lax.axis_index("tp")
        self.sequence = mirrored(self.wide_index // self.group, self.sequence_bits)
        self.part = mirrored(self.tp_index, self.bits)

    def units(self):
        for unit in range(self.wide * self.chunks):
            owner, half = divmod(unit, self.chunks)
            rest, part = divmod(unit, self.tp)
            sub, chunk = divmod(rest, self.chunks)
            for sequence in range(self.batch):
                place = mirrored(sequence, self.sequence_bits) * self.group + sub
                worker = place * self.tp + mirrored(part, self.bits)
                yield owner * self.tp + sequence, worker, half, chunk, part

    def to_work(self, block):
        chunks = []
        for chunk in range(self.chunks):
            result = None
            for half in range(self.chunks):
                pairs = [u[:2] for u in self.units() if u[2] == half and u[3] == chunk]
                piece = block[half * self.unit : (half + 1) * self.unit]
                if chunks:
                    piece = hold(piece, chunks[0])
                piece = lax.ppermute(piece, ("wide", "tp"), pairs)
                if result is None:
                    result = piece
                else:
                    result = jnp.where(self.part % self.chunks == half, piece, result)
            chunks.append(result)
        return chunks

    def to_work_whole(self, block):
        received = []
        own = (self.wide_index * self.chunks // self.tp) % self.chunks
        for turn_index in range(self.chunks):
            piece = block[: self.unit]
            for half in range(1, self.chunks):
                here = (own - turn_index) % self.chunks == half
                piece = jnp.where(here, block[half * self.unit : (half + 1) * self.unit], piece)
            pairs = [u[:2] for u in self.units() if (u[4] + turn_index) % self.chunks == u[3]]
            received.append(lax.ppermute(piece, ("wide", "tp"), pairs))
        chunks = []
        for chunk in range(self.chunks):
            piece = received[0]
            for turn_index in range(1, self.chunks):
                here = (self.part + turn_index) % self.chunks == chunk
                piece = jnp.where(here, received[turn_index], piece)
            chunks.append(piece)
        return chunks

    def to_owner(self, chunks, cross, tokens):
        devices = self.wide * self.tp
        received = []
        for turn_index in range(self.chunks):
            piece = chunks[0]
            for chunk in range(1, self.chunks):
                here = (self.part + turn_index) % self.chunks == chunk
                piece = jnp.where(here, chunks[chunk], piece)
            pairs = []
            for owner, worker, _, chunk, part in self.units():
                if (part + turn_index) % self.chunks == chunk:
                    for plane in range(2):
                        target = plane ^ cross
                        pairs.append((plane * devices + worker, target * devices + owner))
            piece = lax.ppermute(piece, ("section", "wide", "tp"), pairs)
            received.append(hold(piece, *tokens))
        if self.chunks == 1:
            return received[0]
        chunk = (self.wide_index * self.chunks // self.tp) % self.chunks
        ordered = []
        for half in range(self.chunks):
            piece = received[0]
            for turn_index in range(1, self.chunks):
                piece = jnp.where(
                    (chunk - half) % self.chunks == turn_index, received[turn_index], piece
                )
            ordered.append(piece)
        return jnp.concatenate(ordered, 0)

    def exchange(self, first, second, *tokens):
        mine = [pick(self.section, a, b) for a, b in zip(first, second)]
        other = [pick(self.section, b, a) for a, b in zip(first, second)]
        same, cross = self.to_owner(mine, 0, tokens), self.to_owner(other, 1, tokens)
        return jnp.stack([pick(self.section, same, cross), pick(self.section, cross, same)])

    def wide_steps(self, value_at):
        return [
            lax.ppermute(
                value_at(step), "wide", [(index, index ^ step) for index in range(self.wide)]
            )
            for step in range(1, self.wide)
        ]

    def wide_gather(self, block):
        if self.wide > 4:
            return lax.all_gather(block, "wide", axis=0, tiled=True)
        return self.wide_join(self.wide_pieces(block))

    def wide_pieces(self, block):
        if self.wide > 4:
            return [lax.all_gather(block, "wide", axis=0, tiled=True)]
        return [block] + self.wide_steps(lambda step: block)

    def wide_join(self, pieces):
        step = 1
        while len(pieces) > 1:
            here = (self.wide_index // step) % 2
            pieces = [
                pick(here, jnp.concatenate([a, b], 0), jnp.concatenate([b, a], 0))
                for a, b in zip(pieces[::2], pieces[1::2])
            ]
            step *= 2
        return pieces[0]

    def wide_scatter(self, block):
        if self.wide > 4:
            return lax.psum_scatter(
                block, "wide", scatter_dimension=0, tiled=True
            ).astype(f32)
        return sum(item.astype(f32) for item in self.wide_steps_of(block))

    def wide_steps_of(self, block):
        if self.wide > 4:
            return [self.wide_scatter(block)]
        rows = block.shape[0] // self.wide

        def share(step):
            first = (self.wide_index ^ step) * rows
            return lax.dynamic_slice_in_dim(block, first, rows, 0)

        return [share(0)] + self.wide_steps(share)

    def sum_all(self, value, axes):
        for axis in axes:
            count = lax.axis_size(axis)
            step = 1
            while step < count:
                pairs = [(index, index ^ step) for index in range(count)]
                value = value + lax.ppermute(value, axis, pairs)
                step *= 2
        return value

    def swap(self, value):
        return lax.ppermute(value, "section", [(0, 1), (1, 0)])

    def send(self, value, source):
        return lax.ppermute(value, "section", [(source, 1 - source)])

    def gather(self, block):
        return self.gather_rest(self.gather_first(block))

    def gather_first(self, block):
        return self.gather_bits(block, range(self.bits - 1, 0, -1))

    def gather_rest(self, block):
        return self.gather_bits(block, [0])

    def gather_bits(self, block, bits):
        for bit in bits:
            other = lax.ppermute(
                block, "tp", [(index, index ^ (1 << bit)) for index in range(self.tp)]
            )
            here = (self.tp_index >> bit) & 1
            block = jnp.concatenate([pick(here, block, other), pick(here, other, block)], 0)
        return block

    def scatter_first(self, pieces):
        here = self.tp_index & 1
        if len(pieces) == 1:
            half = pieces[0].shape[0] // 2
            pieces = [pieces[0][:half], pieces[0][half:]]
        other = lax.ppermute(
            pick(here, pieces[1], pieces[0]), "tp", [(i, i ^ 1) for i in range(self.tp)]
        )
        return pick(here, pieces[0], pieces[1]).astype(f32) + other.astype(f32)

    def scatter_rest(self, block, *tokens):
        for bit in range(1, self.bits):
            half = block.shape[0] // 2
            here = (self.tp_index >> bit) & 1
            sent = pick(here, block[half:], block[:half]).astype(bf16)
            kept = pick(here, block[:half], block[half:])
            other = lax.ppermute(
                sent, "tp", [(index, index ^ (1 << bit)) for index in range(self.tp)]
            )
            block = kept + hold(other, *tokens).astype(f32)
        return block

    def groups(self):
        return [
            [sequence * self.group + sub for sub in range(self.group)]
            for sequence in range(self.batch)
        ]

    def all_places(self, block):
        if self.group == 1:
            return block
        return lax.all_gather(block, "wide", axis=0, tiled=True, axis_index_groups=self.groups())

    def own_places(self, block):
        if self.group == 1:
            return block
        return lax.psum_scatter(
            block.astype(bf16), "wide", scatter_dimension=0, tiled=True,
            axis_index_groups=self.groups(),
        ).astype(f32)


def angle_tables(length):
    half = ROTARY // 2
    freqs = np.float32(rotary_base) ** (-(2.0 * np.arange(half, dtype=np.float32)) / ROTARY)
    turned = np.arange(length, dtype=np.float32)[:, None] * freqs[None, :].astype(np.float32)
    cosine, sine = np.cos(turned), np.sin(turned)
    rest = np.zeros((length, HEAD_DIM - ROTARY), np.float32)
    return (
        np.concatenate([cosine, cosine, rest + 1.0] * 2, 1).astype(np.float32),
        np.concatenate([-sine, sine, rest] * 2, 1).astype(np.float32),
    )


def on_device(
    inputs, cotangent, segment_ids, norm_gain, norm_shift, qkv_weight, qkv_bias, out_weight,
    out_bias, up_weight, up_bias, down_weight, down_bias,
):
    batch, length = segment_ids.shape[1], segment_ids.shape[2]
    plan = Plan(batch, length)
    width = inputs.shape[-1]
    local = qkv_weight.shape[-1]
    hidden = up_weight.shape[-1]
    heads = local // HEAD_DIM
    section = plan.section
    space = LANES - local

    fill = ((0, 0), (0, 0), (0, space))
    qkv = qkv_weight[0].reshape(-1, 3 * local)
    up = up_weight[0]
    leaving = jnp.concatenate(
        [down_weight[0].T, jnp.pad(out_weight[0].T, ((0, 0), (0, space)))], 1
    )
    small = jnp.concatenate(
        [
            norm_gain[0].reshape(-1), norm_shift[0].reshape(-1), out_bias[0] + down_bias[0],
            jnp.pad(qkv_bias[0], ((0, 0), (0, space))).reshape(-1), up_bias[0],
        ]
    )
    first = section == 0
    mixed = 3 * LANES
    small_there = plan.swap(small)
    padded = jnp.pad(qkv_weight[0], fill).reshape(-1, mixed)
    weights = jnp.concatenate([padded, up, leaving], 1)
    share = weights.shape[0] // 2
    half_there = plan.swap(jnp.where(first, weights[share:], weights[:share]))

    def gather_halves(plane_zero, plane_one):
        half = jnp.where(first, plane_zero, plane_one)
        array = lax.all_gather(half, ("wide", "section"), axis=0, tiled=True)
        at = mixed + hidden
        return array, dict(
            wq=View(array, 0, mixed), wu=View(array, mixed, hidden),
            wd=View(array, at, hidden), wo=View(array, at + hidden, LANES),
        )

    source = plan.to_work(jnp.where(first, inputs[0, 0], inputs[1, 0]))
    weights_first, views_first = gather_halves(weights[:share], half_there)
    weights_second, views_second = gather_halves(
        half_there, hold(weights[share:], weights_first)
    )
    layers = [views_first, views_second]
    for layer, w in enumerate(layers):
        values = jnp.where(section == layer, small, small_there)
        at = 5 * width
        w["gs"] = values[: 4 * width].reshape(4, width)
        w["after"] = values[4 * width : at]
        w["bq"] = values[at : at + mixed].reshape(1, mixed)
        w["bu"] = values[at + mixed :].reshape(1, hidden)

    segments = lax.dynamic_index_in_dim(segment_ids, section, 0, False)
    segments = lax.dynamic_index_in_dim(segments, plan.sequence, 0, False)
    sub_length = length // plan.group
    first_place = (plan.wide_index % plan.group) * sub_length
    tables = angle_tables(length)
    if plan.group > 1:
        segments = lax.dynamic_slice_in_dim(segments, first_place, sub_length, 0)
        tables = [lax.dynamic_slice_in_dim(t, first_place, sub_length, 0) for t in tables]
    size = plan.unit * plan.tp
    starts = [(first_place + index * size).reshape(1) for index in range(plan.chunks)]
    spans = [slice(index * size, (index + 1) * size) for index in range(plan.chunks)]
    chunk_tables = [[jnp.asarray(table[span]) for table in tables] for span in spans]
    chunk_segments = [segments[span].reshape(-1, 1) for span in spans]
    last = plan.chunks - 1

    outputs, kept = [], []
    blocks = source

    def finished(index, pending, blocks, w, *tokens):
        done = plan.scatter_rest(pending, *tokens)
        return (blocks[index].astype(f32) + done + w["after"]).astype(bf16)

    def step_in(layer, index, x, keys, values, tied):
        w = layers[layer]
        a0, a1, q, k, v = project(x, w, chunk_tables[index], chunk_segments[index], heads, tied)
        keys.append(plan.all_places(k))
        values.append(plan.all_places(v))
        return dict(x=x, a0=a0, a1=a1, q=q, k=list(keys), v=list(values))

    def step_attend(index, s, tied):
        s["o"], s["lse"] = attend(starts[index], s["q"], s["k"], s["v"], heads, tied)

    def step_out(layer, s, tied):
        s["h"], s["d"], part = feed(s["a1"], s["o"], layers[layer], tied)
        return part

    keys, values, state, parts, pending = [], [], [], [], []
    for index in range(plan.chunks):
        x = blocks[index]
        if index == 0:
            x = hold(x, small_there, half_there)
        state.append(step_in(0, index, plan.gather(x), keys, values, ()))
        if index == 0:
            grads = jnp.where(section == 0, cotangent[0, 0], cotangent[1, 0])
            grads = plan.to_work_whole(hold(grads, state[0]["q"]))
        step_attend(index, state[index], ())
    for index in range(plan.chunks):
        parts.append(step_out(0, state[index], tuple(grads) if index == last else ()))
        pending.append(plan.scatter_first([parts[index]]))
    after = []
    for index in range(plan.chunks):
        if after:
            pending[index] = hold(pending[index], after[-1])
        after.append(finished(index, pending[index], blocks, layers[0]))
    kept.append((blocks, state))
    outputs.append(after)

    blocks = after
    keys, values, state, pending, after = [], [], [], [], []
    for index in range(plan.chunks):
        s = step_in(1, index, plan.gather(blocks[index]), keys, values, ())
        state.append(s)
        if index == last:
            coming = plan.gather_first(hold(grads[last], s["q"]))
            step_attend(index, s, (parts[0], coming) if last else ())
        else:
            step_attend(index, s, ())
        parts[index] = step_out(1, s, (coming,) if index == last else ())
        pending.append(plan.scatter_first([parts[index]]))
    kept.append((blocks, state))
    pending_out = pending
    gathered = {last: plan.gather_rest(coming)}
    for index in range(last):
        gathered[index] = plan.gather(hold(grads[index], parts[index]))

    def over_tokens(left, right):
        left, right = jnp.concatenate(left, 0), jnp.concatenate(right, 0)
        return lax.dot_general(left, right, (((0,), (0,)), ((), ())), preferred_element_type=f32)

    def step_back(layer, index, gb, carried, tied):
        s = kept[layer][1][index]
        dq, dk, dv = attend_back(
            starts[index], gb, layers[layer], s["q"], s["o"], s["lse"], s["k"], s["v"], carried,
            heads, tied,
        )
        carried = (dk[:-1], dv[:-1])
        return dq, plan.own_places(dk[-1]), plan.own_places(dv[-1]), carried

    def step_leave(layer, index, s, gu, tied):
        dq, dk, dv, _ = s
        x = kept[layer][1][index]["x"]
        gm, e, norm_part, mixed_part, up_part = leave(
            x, dq, dk, dv, gu, layers[layer], chunk_tables[index], tied
        )
        mixed_part = mixed_part.reshape(3, LANES)[:, :local].reshape(-1)
        return gm, e, jnp.concatenate([norm_part.reshape(-1), mixed_part, up_part.reshape(-1)])

    def step_grad(layer, index, pending):
        scaled = plan.scatter_rest(pending)
        normed, inverse = standardize(kept[layer][0][index].astype(f32))
        grad = grads[index].astype(f32) + inverse * (
            scaled
            - jnp.mean(scaled, -1, keepdims=True)
            - normed * jnp.mean(scaled * normed, -1, keepdims=True)
        )
        return grad.astype(bf16)

    def early_terms(layer, gathered, grad_up):
        state = kept[layer][1]
        every = [gathered[index] for index in range(plan.chunks)]
        ups = [grad_up[index] for index in range(plan.chunks)]
        return [
            over_tokens(every, [s["h"] for s in state]).astype(bf16),
            over_tokens([s["a1"] for s in state], ups).astype(bf16),
            over_tokens(every, [s["o"] for s in state]).astype(bf16),
        ]

    def qkv_terms(layer, grad_mixed):
        term = over_tokens(
            [s["a0"] for s in kept[layer][1]], [grad_mixed[index] for index in range(plan.chunks)]
        )
        return term.astype(bf16)

    def without_fill(array):
        return array.reshape(-1, 3, LANES)[:, :, :local].reshape(-1, 3 * local)

    def bias_sum(grads):
        return sum(jnp.sum(item.astype(f32), 0) for item in grads)

    order = list(reversed(range(plan.chunks)))
    second_grads = grads
    results, grad_mixed, pending, sums, carried = {}, {}, {}, 0.0, ((), ())
    grad_up, waiting = {}, tuple(parts)
    for index in order:
        results[index] = step_back(1, index, gathered[index], carried, waiting)
        carried = results[index][-1]
        grad_up[index] = feed_back(gathered[index], layers[1], kept[1][1][index]["d"])
        if index == last:
            token = results[last][0]
            second_outputs = [
                finished(other, pending_out[other], blocks, layers[1], token)
                for other in range(plan.chunks)
            ]
            tied = tuple(second_outputs)
        else:
            tied = (pending[index + 1],)
        grad_mixed[index], e, part = step_leave(1, index, results[index], grad_up[index], tied)
        sums += part
        pending[index] = plan.scatter_first([e])
        waiting = (e,)
    early = jnp.concatenate(early_terms(1, gathered, grad_up), 1)
    early_second = lax.psum_scatter(
        early, ("wide", "section"), scatter_dimension=0, tiled=True
    )
    after = {}
    for index in order:
        if after:
            pending[index] = hold(pending[index], after[index + 1])
        after[index] = hold(step_grad(1, index, pending[index]), early)
    small_second = jnp.concatenate([sums, bias_sum(grads)])
    second_qkv = qkv_terms(1, grad_mixed)
    input_second = [after[index] for index in range(plan.chunks)]
    grads = input_second
    gathered = {index: plan.gather(grads[index]) for index in order}
    results, grad_mixed, pending, sums, carried = {}, {}, {}, 0.0, ((), ())
    grad_up, waiting = {}, ()
    for index in order:
        results[index] = step_back(0, index, gathered[index], carried, waiting)
        carried = results[index][-1]
        if index == last:
            for other in order:
                grad_up[other] = feed_back(
                    gathered[other], layers[0], kept[0][1][other]["d"]
                )
            early = jnp.concatenate(early_terms(0, gathered, grad_up) + [second_qkv], 1)
            early_sum = lax.psum_scatter(
                early, ("wide", "section"), scatter_dimension=0, tiled=True
            )
            token = results[last][0]
            tied = (early,)
        else:
            tied = (pending[index + 1],)
        grad_mixed[index], e, part = step_leave(0, index, results[index], grad_up[index], tied)
        sums += part
        pending[index] = plan.scatter_first([e])
        waiting = (e,)
    after = {index: step_grad(0, index, pending[index]) for index in order}
    input_first = [after[index] for index in range(plan.chunks)]
    all_grads = plan.exchange(input_first, input_second)
    held = [hold(item, gathered[last]) for item in second_outputs]
    section_outputs = plan.exchange(outputs[0], held, all_grads)
    qkv_shares = plan.wide_steps_of(
        hold(without_fill(qkv_terms(0, grad_mixed)), after[0])
    )
    total = jnp.stack([jnp.concatenate([sums, bias_sum(grads)]), small_second])
    at = 4 * width + 3 * local
    shared = jnp.concatenate([total[:, : 4 * width], total[:, at + hidden :]], 1)
    shared = plan.sum_all(shared, ("tp",))
    total = hold(jnp.concatenate([shared, total[:, 4 * width : at + hidden]], 1), after[0])
    if plan.wide > 4:
        total = lax.psum(total, "wide")
    else:
        terms = [total] + plan.wide_steps(lambda step: total)
        while len(terms) > 1:
            terms = [one + two for one, two in zip(terms[::2], terms[1::2])]
        total = terms[0]
    first_qkv_sum = sum(item.astype(f32) for item in qkv_shares)
    split = 2 * hidden + LANES
    here = plan.send(early_second, 0)
    there, here_qkv = plan.send(early_sum[:, :split], 1), plan.send(early_sum[:, split:], 0)
    early = pick(
        section,
        jnp.concatenate([early_sum[:, :split], there], 0),
        jnp.concatenate([here, early_second], 0),
    ).astype(f32)
    qkv_grad = first_qkv_sum + plan.send(first_qkv_sum.astype(bf16), 1).astype(f32)
    second_qkv = without_fill(jnp.concatenate([here_qkv, early_sum[:, split:]], 0)).astype(f32)
    qkv_grad = pick(section, qkv_grad, second_qkv)
    down_grad, up_grad = early[:, :hidden], early[:, hidden : 2 * hidden]
    out_grad = early[:, 2 * hidden : 2 * hidden + local]
    total = total + plan.swap(total)
    total = pick(section, total[0], total[1])
    shared, own = total[: 5 * width], total[5 * width :]
    bias_grad = shared[4 * width :]
    return (
        section_outputs[None, :, None],
        all_grads.astype(f32)[None, :, None],
        shared[: 2 * width].reshape(1, 2, width),
        shared[2 * width : 4 * width].reshape(1, 2, width),
        qkv_grad.reshape(1, -1, 3, local),
        own[: 3 * local].reshape(1, 3, local),
        out_grad.T[None],
        bias_grad[None],
        up_grad[None],
        own[3 * local :][None],
        down_grad.T[None],
        bias_grad[None],
    )


def solution(mesh):
    return jax.shard_map(
        on_device,
        mesh=mesh,
        in_specs=(
            P(None, "tp", "wide", None),
            P(None, "tp", "wide", None),
            P(),
            P("section", None, None),
            P("section", None, None),
            P("section", "wide", None, "tp"),
            P("section", None, "tp"),
            P("section", "tp", "wide"),
            P("section", None),
            P("section", "wide", "tp"),
            P("section", "tp"),
            P("section", "tp", "wide"),
            P("section", None),
        ),
        out_specs=(
            P("section", None, "tp", "wide", None),
            P("section", None, "tp", "wide", None),
            P("section", None, None),
            P("section", None, None),
            P("section", "wide", None, "tp"),
            P("section", None, "tp"),
            P("section", "tp", "wide"),
            P("section", None),
            P("section", "wide", "tp"),
            P("section", "tp"),
            P("section", "tp", "wide"),
            P("section", None),
        ),
        check_vma=False,
    )
```

```python
import functools

import jax
import jax.numpy as jnp
import numpy as np
from jax import lax
from jax.experimental import pallas as pl
from jax.experimental.pallas import tpu as pltpu
from jax.sharding import PartitionSpec as P

HEAD_DIM = 64
ROTARY = 16
LANES = 256
CHUNKS = 1
QUERY_BLOCK = 256
KEY_BLOCK = 512
ROW_BLOCK = 256

epsilon = 1e-05
rotary_base = 10000.0
masked_out = -1e30
f32 = jnp.float32
bf16 = jnp.bfloat16
NT = (((1,), (1,)), ((), ()))


def params(size=44):
    return pltpu.CompilerParams(
        dimension_semantics=("arbitrary",), vmem_limit_bytes=size * 1024 * 1024
    )


def dot(left, right):
    return jnp.dot(left, right, preferred_element_type=f32)


def dot_nt(left, right):
    return lax.dot_general(left, right, NT, preferred_element_type=f32)


def rows_spec(rows, columns):
    return pl.BlockSpec((rows, columns), lambda i: (i, 0))


def whole_spec(array):
    return pl.BlockSpec(array.shape, lambda i: (0,) * array.ndim)


def smem_spec():
    return pl.BlockSpec(memory_space=pltpu.SMEM)


def standardize(values):
    centred = values - jnp.mean(values, -1, keepdims=True)
    inverse = lax.rsqrt(jnp.mean(centred * centred, -1, keepdims=True) + epsilon)
    return centred * inverse, inverse


def wide_table(ref):
    return jnp.concatenate([ref[...]] * (LANES // ref.shape[1]), 1)


def halves(signed):
    place = lax.broadcasted_iota(jnp.int32, signed.shape, 1) % HEAD_DIM
    zero = jnp.zeros_like(signed)
    half = ROTARY // 2
    return jnp.where(place < half, signed, zero), jnp.where(place < half, zero, signed)


def turn(values, cosine, signed):
    half = ROTARY // 2
    low, high = halves(signed)
    ahead = pltpu.roll(values, LANES - half, 1)
    behind = pltpu.roll(values, half, 1)
    return values * cosine + ahead * low + behind * high


def turn_back(grads, cosine, signed):
    half = ROTARY // 2
    low, high = halves(signed)
    ahead = pltpu.roll(grads * high, LANES - half, 1)
    behind = pltpu.roll(grads * low, half, 1)
    return grads * cosine + ahead + behind


def any_specs(arrays):
    return [pl.BlockSpec(memory_space=pl.ANY)] * len(arrays)


def cost(micros, transfers):
    return pl.CostEstimate(
        flops=int(micros * 1.15e9), bytes_accessed=int(transfers), transcendentals=0
    )


class View:
    def __init__(self, array, first, width, part=0, parts=1):
        if first % width:
            array, first = array[:, first : first + width], 0
        self.array, self.block = array, (part, first // width)
        self.shape = (array.shape[0] // parts, width)

    def spec(self):
        block = self.block
        return pl.BlockSpec(self.shape, lambda i: block)


def project_kernel(heads, x_ref, gs_ref, w_ref, b_ref, c_ref, s_ref, seg_ref, *rest):
    a0_ref, a1_ref, q_ref, k_ref, v_ref = rest[-5:]
    normed, _ = standardize(x_ref[...].astype(f32))
    first = (normed * gs_ref[0:1] + gs_ref[2:3]).astype(bf16)
    a0_ref[...] = first
    a1_ref[...] = (normed * gs_ref[1:2] + gs_ref[3:4]).astype(bf16)
    mixed = dot(first, w_ref[...]) + b_ref[...]
    cosine, signed = wide_table(c_ref), wide_table(s_ref)
    query = turn(mixed[:, :LANES], cosine, signed)
    keys = turn(mixed[:, LANES : 2 * LANES], cosine, signed)
    lane = lax.broadcasted_iota(jnp.int32, query.shape, 1)
    used = heads * HEAD_DIM
    mine = (lane - used) == seg_ref[...]
    spare = lane >= used
    q_ref[...] = jnp.where(
        spare, jnp.where(mine, 1.0, 0.0), query * HEAD_DIM ** (-0.5)
    ).astype(bf16)
    k_ref[...] = jnp.where(spare, jnp.where(mine, 0.0, masked_out), keys).astype(bf16)
    v_ref[...] = mixed[:, 2 * LANES :].astype(bf16)


def project(x, w, tables, seg, heads, after=()):
    tokens, width = x.shape
    rows = min(ROW_BLOCK, tokens)
    columns = (width, width, LANES, LANES, LANES)
    return pl.pallas_call(
        functools.partial(project_kernel, heads),
        grid=(tokens // rows,),
        in_specs=[rows_spec(rows, width), whole_spec(w["gs"]), w["wq"].spec()]
        + [whole_spec(w["bq"])]
        + [rows_spec(rows, item.shape[1]) for item in tables]
        + [rows_spec(rows, 1)]
        + any_specs(after),
        out_specs=[rows_spec(rows, item) for item in columns],
        out_shape=[jax.ShapeDtypeStruct((tokens, item), bf16) for item in columns],
        compiler_params=params(),
        cost_estimate=cost(4.0 * tokens / 1024, 6 * tokens * width),
        name="project",
    )(x, w["gs"], w["wq"].array, w["bq"], *tables, seg, *after)


def feed_kernel(a_ref, o_ref, wu_ref, bu_ref, wd_ref, wo_ref, *rest):
    h_ref, d_ref, part_ref = rest[-3:]
    before = dot(a_ref[...], wu_ref[...]) + bu_ref[...]
    phi = 0.5 + 0.5 * lax.erf(before * (0.5**0.5))
    density = jnp.exp(before * before * (-0.5)) * 0.3989422804014327
    hidden = (before * phi).astype(bf16)
    h_ref[...] = hidden
    d_ref[...] = (phi + before * density).astype(bf16)
    part_ref[...] = (dot_nt(hidden, wd_ref[...]) + dot_nt(o_ref[...], wo_ref[...])).astype(bf16)


def feed(a1, o, w, after=()):
    tokens, width = a1.shape
    rows = min(ROW_BLOCK, tokens)
    hidden = w["bu"].shape[1]
    columns = (hidden, hidden, width)
    return pl.pallas_call(
        feed_kernel,
        grid=(tokens // rows,),
        in_specs=[rows_spec(rows, width), rows_spec(rows, LANES), w["wu"].spec()]
        + [whole_spec(w["bu"]), w["wd"].spec(), w["wo"].spec()]
        + any_specs(after),
        out_specs=[rows_spec(rows, item) for item in columns],
        out_shape=[jax.ShapeDtypeStruct((tokens, item), bf16) for item in columns],
        compiler_params=params(),
        cost_estimate=cost(5.0 * tokens / 1024, 6 * tokens * width),
        name="feed",
    )(a1, o, w["wu"].array, w["bu"], w["wd"].array, w["wo"].array, *after)


def feed_back_kernel(gb_ref, wd_ref, d_ref, *rest):
    rest[-1][...] = (dot(gb_ref[...], wd_ref[...]) * d_ref[...].astype(f32)).astype(bf16)


def feed_back(gb, w, d, after=()):
    tokens, width = gb.shape
    rows = min(ROW_BLOCK, tokens)
    hidden = d.shape[1]
    return pl.pallas_call(
        feed_back_kernel,
        grid=(tokens // rows,),
        in_specs=[rows_spec(rows, width), w["wd"].spec(), rows_spec(rows, hidden)]
        + any_specs(after),
        out_specs=rows_spec(rows, hidden),
        out_shape=jax.ShapeDtypeStruct((tokens, hidden), bf16),
        compiler_params=params(),
        cost_estimate=cost(2.0 * tokens / 1024, 6 * tokens * width),
        name="feed_back",
    )(gb, w["wd"].array, d, *after)


def head_lanes(array, heads, spare):
    lane = lax.broadcasted_iota(jnp.int32, array.shape, 1)
    zero = jnp.zeros_like(array)
    result = []
    for head in range(heads):
        keep = (lane >= head * HEAD_DIM) & (lane < (head + 1) * HEAD_DIM)
        if spare:
            keep = keep | (lane >= heads * HEAD_DIM)
        result.append(jnp.where(keep, array, zero))
    return result


def join_once(parts, target):
    @pl.when(pl.program_id(0) == 0)
    def _():
        first = 0
        for part in parts:
            target[first : first + part.shape[0], :] = part[...]
            first += part.shape[0]


def attend_kernel(heads, key_block, pieces, start_ref, q_ref, *rest):
    k_refs, v_refs = rest[:pieces], rest[pieces : 2 * pieces]
    o_ref, lse_ref, top_ref, sum_ref, acc_ref, k_ref, vt_ref = rest[-7:]
    join_once(k_refs, k_ref)

    @pl.when(pl.program_id(0) == 0)
    def _():
        acc_ref[...] = jnp.zeros(acc_ref.shape, f32)
        first = 0
        for ref in v_refs:
            block = min(key_block, ref.shape[0])
            for at in range(0, ref.shape[0], block):
                vt_ref[:, first + at : first + at + block] = ref[at : at + block, :].T
            first += ref.shape[0]

    rows = q_ref.shape[0]
    queries = head_lanes(q_ref[...], heads, True)
    first_row = start_ref[0] + pl.program_id(0) * rows
    full = first_row // key_block

    def step(block, diagonal, fresh):
        place = pl.ds(pl.multiple_of(block * key_block, key_block), key_block)
        keys = k_ref[place, :]
        for head in range(heads):
            here = slice(head * HEAD_DIM, (head + 1) * HEAD_DIM)
            line = slice(head, head + 1)
            scores = dot_nt(keys, queries[head])
            if diagonal:
                column = lax.broadcasted_iota(jnp.int32, scores.shape, 0) + block * key_block
                row = lax.broadcasted_iota(jnp.int32, scores.shape, 1) + first_row
                scores = jnp.where(column <= row, scores, masked_out)
            top = jnp.max(scores, 0, keepdims=True)
            if not fresh:
                before = top_ref[line, :]
                top = jnp.maximum(before, top)
                fade = jnp.exp(before - top)
            probs = jnp.exp(scores - top)
            total = jnp.sum(probs, 0, keepdims=True)
            value = dot(vt_ref[here, place], probs.astype(bf16))
            if not fresh:
                total += sum_ref[line, :] * fade
                value += acc_ref[here, :] * fade
            top_ref[line, :] = top
            sum_ref[line, :] = total
            acc_ref[here, :] = value

    step(full, True, True)

    @pl.loop(0, full)
    def _(block):
        step(block, False, False)

    for head in range(heads):
        here = slice(head * HEAD_DIM, (head + 1) * HEAD_DIM)
        acc_ref[here, :] = acc_ref[here, :] / sum_ref[head : head + 1, :]
    o_ref[...] = acc_ref[...].T.astype(bf16)
    lse_ref[...] = jnp.zeros(lse_ref.shape, f32)
    lse_ref[:heads, :] = top_ref[:heads, :] + jnp.log(sum_ref[:heads, :])


def attend(start, q, keys, values, heads, after=()):
    tokens = q.shape[0]
    rows = min(QUERY_BLOCK, tokens)
    span = sum(item.shape[0] for item in keys)
    key_block = min(KEY_BLOCK, span)
    return pl.pallas_call(
        functools.partial(attend_kernel, heads, key_block, len(keys)),
        grid=(tokens // rows,),
        in_specs=[smem_spec(), rows_spec(rows, LANES)]
        + [whole_spec(item) for item in (*keys, *values)]
        + any_specs(after),
        out_specs=[rows_spec(rows, LANES), pl.BlockSpec((8, rows), lambda i: (0, i))],
        out_shape=[
            jax.ShapeDtypeStruct((tokens, LANES), bf16),
            jax.ShapeDtypeStruct((8, tokens), f32),
        ],
        scratch_shapes=[pltpu.VMEM((8, rows), f32)] * 2
        + [pltpu.VMEM((LANES, rows), f32)]
        + [pltpu.VMEM((span, LANES), bf16), pltpu.VMEM((LANES, span), bf16)],
        compiler_params=params(),
        cost_estimate=cost(7.0 * tokens * span / 1024 / 1024, 6 * tokens * LANES),
        name="attend",
    )(start, q, *keys, *values, *after)


def attend_back_kernel(
    heads, key_block, pieces, carried, start_ref, gb_ref, w_ref, q_ref, o_ref, *rest,
):
    lse_ref, rest = rest[0], rest[1:]
    k_refs, v_refs, rest = rest[:pieces], rest[pieces : 2 * pieces], rest[2 * pieces :]
    carry_refs = rest[: 2 * carried]
    dq_ref, rest = rest[-(2 * pieces + 7)], rest[-(2 * pieces + 6) :]
    dk_refs, dv_refs, rest = rest[:pieces], rest[pieces : 2 * pieces], rest[2 * pieces :]
    k_ref, v_ref, kt_ref, dk_ref, dv_ref, dqt_ref = rest
    rows = q_ref.shape[0]
    first_row = start_ref[0] + pl.program_id(0) * rows
    full = first_row // key_block
    join_once(k_refs, k_ref)
    join_once(v_refs, v_ref)

    @pl.when(pl.program_id(0) == 0)
    def _():
        dk_ref[...] = jnp.zeros(dk_ref.shape, f32)
        dv_ref[...] = jnp.zeros(dv_ref.shape, f32)
        for refs, target in ((carry_refs[:carried], dk_ref), (carry_refs[carried:], dv_ref)):
            first = 0
            for ref in refs:
                target[first : first + ref.shape[0], :] = ref[...]
                first += ref.shape[0]
        for first in range(0, k_ref.shape[0], key_block):
            kt_ref[:, first : first + key_block] = k_ref[first : first + key_block, :].T

    grad = gb_ref[...]
    grad_out = dot(grad, w_ref[...]).astype(bf16)
    product = (grad_out.astype(f32) * o_ref[...].astype(f32)).T
    centres = [
        jnp.sum(product[head * HEAD_DIM : (head + 1) * HEAD_DIM], 0, keepdims=True)
        for head in range(heads)
    ]
    queries = head_lanes(q_ref[...], heads, True)
    grads = head_lanes(grad_out, heads, False)
    dqt_ref[...] = jnp.zeros(dqt_ref.shape, f32)

    def step(block, diagonal):
        place = pl.ds(pl.multiple_of(block * key_block, key_block), key_block)
        keys = k_ref[place, :]
        values = v_ref[place, :]
        grad_keys = dk_ref[place, :]
        grad_values = dv_ref[place, :]
        for head in range(heads):
            here = slice(head * HEAD_DIM, (head + 1) * HEAD_DIM)
            scores = dot_nt(keys, queries[head])
            probs = jnp.exp(scores - lse_ref[head : head + 1, :])
            if diagonal:
                column = lax.broadcasted_iota(jnp.int32, scores.shape, 0) + block * key_block
                row = lax.broadcasted_iota(jnp.int32, scores.shape, 1) + first_row
                probs = jnp.where(column <= row, probs, 0.0)
            grad_probs = dot_nt(values, grads[head])
            grad_scores = (probs * (grad_probs - centres[head])).astype(bf16)
            grad_values += dot(probs.astype(bf16), grads[head])
            grad_keys += dot(grad_scores, queries[head])
            dqt_ref[here, :] += dot(kt_ref[here, place], grad_scores)
        dk_ref[place, :] = grad_keys
        dv_ref[place, :] = grad_values

    @pl.loop(0, full)
    def _(block):
        step(block, False)

    step(full, True)
    dq_ref[...] = dqt_ref[...].T * HEAD_DIM ** (-0.5)

    @pl.when(pl.program_id(0) == pl.num_programs(0) - 1)
    def _():
        for refs, source in ((dk_refs, dk_ref), (dv_refs, dv_ref)):
            first = 0
            for ref in refs:
                ref[...] = source[first : first + ref.shape[0], :]
                first += ref.shape[0]


def attend_back(start, gb, w, q, o, lse, keys, values, carried, heads, after=()):
    tokens, width = gb.shape
    rows = min(QUERY_BLOCK, tokens)
    sizes = [item.shape[0] for item in keys]
    span = sum(sizes)
    key_block = min(KEY_BLOCK, span)
    carry_keys, carry_values = carried
    whole = [pl.BlockSpec((size, LANES), lambda i: (0, 0)) for size in sizes]
    result = pl.pallas_call(
        functools.partial(attend_back_kernel, heads, key_block, len(keys), len(carry_keys)),
        grid=(tokens // rows,),
        in_specs=[smem_spec(), rows_spec(rows, width), w["wo"].spec()]
        + [rows_spec(rows, LANES), rows_spec(rows, LANES)]
        + [pl.BlockSpec((8, rows), lambda i: (0, i))]
        + [whole_spec(item) for item in (*keys, *values, *carry_keys, *carry_values)]
        + any_specs(after),
        out_specs=[rows_spec(rows, LANES)] + whole + whole,
        out_shape=[jax.ShapeDtypeStruct((tokens, LANES), f32)]
        + [jax.ShapeDtypeStruct((size, LANES), f32) for size in sizes] * 2,
        scratch_shapes=[pltpu.VMEM((span, LANES), bf16)] * 2
        + [pltpu.VMEM((LANES, span), bf16)]
        + [pltpu.VMEM((span, LANES), f32)] * 2
        + [pltpu.VMEM((LANES, rows), f32)],
        compiler_params=params(),
        cost_estimate=cost(12.5 * tokens * span / 1024 / 1024, 4 * tokens * width),
        name="attend_back",
    )(start, gb, w["wo"].array, q, o, lse, *keys, *values, *carry_keys, *carry_values, *after)
    pieces = len(keys)
    return result[0], result[1 : 1 + pieces], result[1 + pieces :]


def leave_kernel(
    x_ref, gs_ref, dq_ref, dk_ref, dv_ref, gu_ref, wq_ref, wu_ref, c_ref, s_ref, *rest,
):
    gm_ref, e_ref, norm_ref, mixed_ref, up_ref = rest[-5:]

    @pl.when(pl.program_id(0) == 0)
    def _():
        norm_ref[...] = jnp.zeros(norm_ref.shape, f32)
        mixed_ref[...] = jnp.zeros(mixed_ref.shape, f32)
        up_ref[...] = jnp.zeros(up_ref.shape, f32)

    cosine, signed = wide_table(c_ref), wide_table(s_ref)
    grads = jnp.concatenate(
        [
            turn_back(dq_ref[...], cosine, signed),
            turn_back(dk_ref[...], cosine, signed),
            dv_ref[...],
        ],
        1,
    ).astype(bf16)
    gm_ref[...] = grads
    grad_up = gu_ref[...]
    mixed_ref[...] += jnp.sum(grads.astype(f32), 0, keepdims=True)
    up_ref[...] += jnp.sum(grad_up.astype(f32), 0, keepdims=True)
    grad_first = dot_nt(grads, wq_ref[...])
    grad_second = dot_nt(grad_up, wu_ref[...])
    normed, _ = standardize(x_ref[...].astype(f32))
    norm_ref[0:1] += jnp.sum(grad_first * normed, 0, keepdims=True)
    norm_ref[1:2] += jnp.sum(grad_second * normed, 0, keepdims=True)
    norm_ref[2:3] += jnp.sum(grad_first, 0, keepdims=True)
    norm_ref[3:4] += jnp.sum(grad_second, 0, keepdims=True)
    e_ref[...] = (grad_first * gs_ref[0:1] + grad_second * gs_ref[1:2]).astype(bf16)


def leave(x, dq, dk, dv, gu, w, tables, after=()):
    tokens, width = x.shape
    rows = min(ROW_BLOCK, tokens)
    mixed = 3 * LANES
    hidden = gu.shape[1]
    sums = [(4, width), (1, mixed), (1, hidden)]
    return pl.pallas_call(
        leave_kernel,
        grid=(tokens // rows,),
        in_specs=[rows_spec(rows, width), whole_spec(w["gs"])]
        + [rows_spec(rows, LANES)] * 3
        + [rows_spec(rows, hidden), w["wq"].spec(), w["wu"].spec()]
        + [rows_spec(rows, item.shape[1]) for item in tables]
        + any_specs(after),
        out_specs=[rows_spec(rows, mixed), rows_spec(rows, width)]
        + [pl.BlockSpec(item, lambda i: (0, 0)) for item in sums],
        out_shape=[
            jax.ShapeDtypeStruct((tokens, mixed), bf16),
            jax.ShapeDtypeStruct((tokens, width), bf16),
        ]
        + [jax.ShapeDtypeStruct(item, f32) for item in sums],
        compiler_params=params(),
        cost_estimate=cost(6.7 * tokens / 1024, 6 * tokens * width),
        name="leave",
    )(x, w["gs"], dq, dk, dv, gu, w["wq"].array, w["wu"].array, *tables, *after)


def hold(value, *tokens):
    for token in tokens:
        first = token[(slice(0, 1),) * token.ndim].reshape((1,) * value.ndim)
        value = jnp.where(first == jnp.inf, jnp.zeros_like(value), value)
    return value


def pick(bit, zero, one):
    return jnp.where(bit == 0, zero, one)


def mirrored(index, bits):
    return sum(((index >> bit) & 1) << (bits - 1 - bit) for bit in range(bits))


class Plan:
    def __init__(self, batch, length):
        self.wide, self.tp = lax.axis_size("wide"), lax.axis_size("tp")
        self.batch, self.length = batch, length
        self.bits = self.tp.bit_length() - 1
        self.group = self.wide // batch
        self.sequence_bits = batch.bit_length() - 1
        self.chunks = CHUNKS if self.group == 1 else 1
        self.unit = length // (self.wide * self.chunks)
        self.section = lax.axis_index("section")
        self.wide_index = lax.axis_index("wide")
        self.tp_index = lax.axis_index("tp")
        self.sequence = mirrored(self.wide_index // self.group, self.sequence_bits)
        self.part = mirrored(self.tp_index, self.bits)

    def units(self):
        for unit in range(self.wide * self.chunks):
            owner, half = divmod(unit, self.chunks)
            rest, part = divmod(unit, self.tp)
            sub, chunk = divmod(rest, self.chunks)
            for sequence in range(self.batch):
                place = mirrored(sequence, self.sequence_bits) * self.group + sub
                worker = place * self.tp + mirrored(part, self.bits)
                yield owner * self.tp + sequence, worker, half, chunk, part

    def to_work(self, block):
        chunks = []
        for chunk in range(self.chunks):
            result = None
            for half in range(self.chunks):
                pairs = [u[:2] for u in self.units() if u[2] == half and u[3] == chunk]
                piece = block[half * self.unit : (half + 1) * self.unit]
                if chunks:
                    piece = hold(piece, chunks[0])
                piece = lax.ppermute(piece, ("wide", "tp"), pairs)
                if result is None:
                    result = piece
                else:
                    result = jnp.where(self.part % self.chunks == half, piece, result)
            chunks.append(result)
        return chunks

    def to_work_whole(self, block):
        received = []
        own = (self.wide_index * self.chunks // self.tp) % self.chunks
        for turn_index in range(self.chunks):
            piece = block[: self.unit]
            for half in range(1, self.chunks):
                here = (own - turn_index) % self.chunks == half
                piece = jnp.where(here, block[half * self.unit : (half + 1) * self.unit], piece)
            pairs = [u[:2] for u in self.units() if (u[4] + turn_index) % self.chunks == u[3]]
            received.append(lax.ppermute(piece, ("wide", "tp"), pairs))
        chunks = []
        for chunk in range(self.chunks):
            piece = received[0]
            for turn_index in range(1, self.chunks):
                here = (self.part + turn_index) % self.chunks == chunk
                piece = jnp.where(here, received[turn_index], piece)
            chunks.append(piece)
        return chunks

    def to_owner(self, chunks, planes, tokens):
        devices = self.wide * self.tp
        received = []
        for turn_index in range(self.chunks):
            piece = chunks[0]
            for chunk in range(1, self.chunks):
                here = (self.part + turn_index) % self.chunks == chunk
                piece = jnp.where(here, chunks[chunk], piece)
            pairs = []
            for owner, worker, _, chunk, part in self.units():
                if (part + turn_index) % self.chunks == chunk:
                    for plane, target in planes:
                        pairs.append((plane * devices + worker, target * devices + owner))
            piece = lax.ppermute(piece, ("section", "wide", "tp"), pairs)
            received.append(hold(piece, *tokens))
        if self.chunks == 1:
            return received[0]
        chunk = (self.wide_index * self.chunks // self.tp) % self.chunks
        ordered = []
        for half in range(self.chunks):
            piece = received[0]
            for turn_index in range(1, self.chunks):
                piece = jnp.where(
                    (chunk - half) % self.chunks == turn_index, received[turn_index], piece
                )
            ordered.append(piece)
        return jnp.concatenate(ordered, 0)

    def owned(self, chunks, layer, *tokens):
        return jnp.stack([self.to_owner(chunks, [(micro, layer)], tokens) for micro in range(2)])

    def exchange(self, first, second, *tokens):
        mine = [pick(self.section, a, b) for a, b in zip(first, second)]
        other = [pick(self.section, b, a) for a, b in zip(first, second)]
        same = self.to_owner(mine, [(0, 0), (1, 1)], tokens)
        cross = self.to_owner(other, [(0, 1), (1, 0)], tokens)
        return jnp.stack([pick(self.section, same, cross), pick(self.section, cross, same)])

    def wide_steps(self, value_at):
        return [
            lax.ppermute(
                value_at(step), "wide", [(index, index ^ step) for index in range(self.wide)]
            )
            for step in range(1, self.wide)
        ]

    def wide_scatter(self, block):
        if self.wide > 4:
            return lax.psum_scatter(
                block, "wide", scatter_dimension=0, tiled=True
            ).astype(f32)
        return sum(item.astype(f32) for item in self.wide_steps_of(block))

    def wide_steps_of(self, block):
        if self.wide > 4:
            return [self.wide_scatter(block)]
        rows = block.shape[0] // self.wide

        def share(step):
            first = (self.wide_index ^ step) * rows
            return lax.dynamic_slice_in_dim(block, first, rows, 0)

        return [share(0)] + self.wide_steps(share)

    def sum_all(self, value, axes):
        for axis in axes:
            count = lax.axis_size(axis)
            step = 1
            while step < count:
                pairs = [(index, index ^ step) for index in range(count)]
                value = value + lax.ppermute(value, axis, pairs)
                step *= 2
        return value

    def swap(self, value):
        return lax.ppermute(value, "section", [(0, 1), (1, 0)])

    def send(self, value, source):
        return lax.ppermute(value, "section", [(source, 1 - source)])

    def gather(self, block):
        return self.gather_rest(self.gather_first(block))

    def gather_first(self, block):
        return self.gather_bits(block, range(self.bits - 1, 0, -1))

    def gather_rest(self, block):
        return self.gather_bits(block, [0])

    def gather_bits(self, block, bits):
        for bit in bits:
            other = lax.ppermute(
                block, "tp", [(index, index ^ (1 << bit)) for index in range(self.tp)]
            )
            here = (self.tp_index >> bit) & 1
            block = jnp.concatenate([pick(here, block, other), pick(here, other, block)], 0)
        return block

    def scatter_first(self, pieces):
        here = self.tp_index & 1
        if len(pieces) == 1:
            half = pieces[0].shape[0] // 2
            pieces = [pieces[0][:half], pieces[0][half:]]
        other = lax.ppermute(
            pick(here, pieces[1], pieces[0]), "tp", [(i, i ^ 1) for i in range(self.tp)]
        )
        return pick(here, pieces[0], pieces[1]).astype(f32) + other.astype(f32)

    def scatter_rest(self, block, *tokens):
        for bit in range(1, self.bits):
            half = block.shape[0] // 2
            here = (self.tp_index >> bit) & 1
            sent = pick(here, block[half:], block[:half]).astype(bf16)
            kept = pick(here, block[:half], block[half:])
            other = lax.ppermute(
                sent, "tp", [(index, index ^ (1 << bit)) for index in range(self.tp)]
            )
            block = kept + hold(other, *tokens).astype(f32)
        return block

    def groups(self):
        return [
            [sequence * self.group + sub for sub in range(self.group)]
            for sequence in range(self.batch)
        ]

    def all_places(self, block):
        if self.group == 1:
            return block
        return lax.all_gather(block, "wide", axis=0, tiled=True, axis_index_groups=self.groups())

    def own_places(self, block):
        if self.group == 1:
            return block
        return lax.psum_scatter(
            block.astype(bf16), "wide", scatter_dimension=0, tiled=True,
            axis_index_groups=self.groups(),
        ).astype(f32)


def angle_tables(length):
    half = ROTARY // 2
    freqs = np.float32(rotary_base) ** (-(2.0 * np.arange(half, dtype=np.float32)) / ROTARY)
    turned = np.arange(length, dtype=np.float32)[:, None] * freqs[None, :].astype(np.float32)
    cosine, sine = np.cos(turned), np.sin(turned)
    rest = np.zeros((length, HEAD_DIM - ROTARY), np.float32)
    return (
        np.concatenate([cosine, cosine, rest + 1.0] * 2, 1).astype(np.float32),
        np.concatenate([-sine, sine, rest] * 2, 1).astype(np.float32),
    )


def on_device(
    inputs, cotangent, segment_ids, norm_gain, norm_shift, qkv_weight, qkv_bias, out_weight,
    out_bias, up_weight, up_bias, down_weight, down_bias,
):
    batch, length = segment_ids.shape[1], segment_ids.shape[2]
    plan = Plan(batch, length)
    width = inputs.shape[-1]
    local = qkv_weight.shape[-1]
    hidden = up_weight.shape[-1]
    heads = local // HEAD_DIM
    section = plan.section
    space = LANES - local

    fill = ((0, 0), (0, 0), (0, space))
    qkv = qkv_weight[0].reshape(-1, 3 * local)
    up = up_weight[0]
    leaving = jnp.concatenate(
        [down_weight[0].T, jnp.pad(out_weight[0].T, ((0, 0), (0, space)))], 1
    )
    small = jnp.concatenate(
        [
            norm_gain[0].reshape(-1), norm_shift[0].reshape(-1), out_bias[0] + down_bias[0],
            jnp.pad(qkv_bias[0], ((0, 0), (0, space))).reshape(-1), up_bias[0],
        ]
    )
    first = section == 0
    mixed = 3 * LANES
    small_there = plan.swap(small)
    padded = jnp.pad(qkv_weight[0], fill).reshape(-1, mixed)
    weights = jnp.concatenate([padded, up, leaving], 1)
    share = weights.shape[0] // 2
    half_there = plan.swap(jnp.where(first, weights[share:], weights[:share]))

    def gather_halves(plane_zero, plane_one):
        half = jnp.where(first, plane_zero, plane_one)
        array = lax.all_gather(half, ("wide", "section"), axis=0, tiled=True)
        at = mixed + hidden
        return array, dict(
            wq=View(array, 0, mixed), wu=View(array, mixed, hidden),
            wd=View(array, at, hidden), wo=View(array, at + hidden, LANES),
        )

    source = plan.to_work(jnp.where(first, inputs[0, 0], inputs[1, 0]))
    weights_first, views_first = gather_halves(weights[:share], half_there)
    weights_second, views_second = gather_halves(
        half_there, hold(weights[share:], weights_first)
    )
    layers = [views_first, views_second]
    for layer, w in enumerate(layers):
        values = jnp.where(section == layer, small, small_there)
        at = 5 * width
        w["gs"] = values[: 4 * width].reshape(4, width)
        w["after"] = values[4 * width : at]
        w["bq"] = values[at : at + mixed].reshape(1, mixed)
        w["bu"] = values[at + mixed :].reshape(1, hidden)

    segments = lax.dynamic_index_in_dim(segment_ids, section, 0, False)
    segments = lax.dynamic_index_in_dim(segments, plan.sequence, 0, False)
    sub_length = length // plan.group
    first_place = (plan.wide_index % plan.group) * sub_length
    tables = angle_tables(length)
    if plan.group > 1:
        segments = lax.dynamic_slice_in_dim(segments, first_place, sub_length, 0)
        tables = [lax.dynamic_slice_in_dim(t, first_place, sub_length, 0) for t in tables]
    size = plan.unit * plan.tp
    starts = [(first_place + index * size).reshape(1) for index in range(plan.chunks)]
    spans = [slice(index * size, (index + 1) * size) for index in range(plan.chunks)]
    chunk_tables = [[jnp.asarray(table[span]) for table in tables] for span in spans]
    chunk_segments = [segments[span].reshape(-1, 1) for span in spans]
    last = plan.chunks - 1

    outputs, kept = [], []
    blocks = source

    def finished(index, pending, blocks, w, *tokens):
        done = plan.scatter_rest(pending, *tokens)
        return (blocks[index].astype(f32) + done + w["after"]).astype(bf16)

    def step_in(layer, index, x, keys, values, tied):
        w = layers[layer]
        a0, a1, q, k, v = project(x, w, chunk_tables[index], chunk_segments[index], heads, tied)
        keys.append(plan.all_places(k))
        values.append(plan.all_places(v))
        return dict(x=x, a0=a0, a1=a1, q=q, k=list(keys), v=list(values))

    def step_attend(index, s, tied):
        s["o"], s["lse"] = attend(starts[index], s["q"], s["k"], s["v"], heads, tied)

    def step_out(layer, s, tied):
        s["h"], s["d"], part = feed(s["a1"], s["o"], layers[layer], tied)
        return part

    keys, values, state, parts, pending = [], [], [], [], []
    for index in range(plan.chunks):
        x = blocks[index]
        if index == 0:
            x = hold(x, small_there, half_there)
        state.append(step_in(0, index, plan.gather(x), keys, values, ()))
        if index == 0:
            grads = jnp.where(section == 0, cotangent[0, 0], cotangent[1, 0])
            grads = plan.to_work_whole(hold(grads, weights_first))
        step_attend(index, state[index], ())
    for index in range(plan.chunks):
        parts.append(step_out(0, state[index], tuple(grads) if index == last else ()))
        pending.append(plan.scatter_first([parts[index]]))
    after = []
    for index in range(plan.chunks):
        if after:
            pending[index] = hold(pending[index], after[-1])
        after.append(finished(index, pending[index], blocks, layers[0]))
    kept.append((blocks, state))
    outputs.append(after)

    blocks = after
    keys, values, state, pending, after = [], [], [], [], []
    for index in range(plan.chunks):
        s = step_in(1, index, plan.gather(blocks[index]), keys, values, ())
        state.append(s)
        if index == last:
            coming = plan.gather_first(hold(grads[last], s["q"]))
            step_attend(index, s, (parts[0], coming) if last else ())
        else:
            step_attend(index, s, ())
        parts[index] = step_out(1, s, (coming,) if index == last else ())
        pending.append(plan.scatter_first([parts[index]]))
    kept.append((blocks, state))
    pending_out = pending
    gathered = {last: plan.gather_rest(coming)}
    for index in range(last):
        gathered[index] = plan.gather(hold(grads[index], parts[index]))

    def over_tokens(left, right):
        left, right = jnp.concatenate(left, 0), jnp.concatenate(right, 0)
        return lax.dot_general(left, right, (((0,), (0,)), ((), ())), preferred_element_type=f32)

    def step_back(layer, index, gb, carried, tied):
        s = kept[layer][1][index]
        dq, dk, dv = attend_back(
            starts[index], gb, layers[layer], s["q"], s["o"], s["lse"], s["k"], s["v"], carried,
            heads, tied,
        )
        carried = (dk[:-1], dv[:-1])
        return dq, plan.own_places(dk[-1]), plan.own_places(dv[-1]), carried

    def step_leave(layer, index, s, gu, tied):
        dq, dk, dv, _ = s
        x = kept[layer][1][index]["x"]
        gm, e, norm_part, mixed_part, up_part = leave(
            x, dq, dk, dv, gu, layers[layer], chunk_tables[index], tied
        )
        mixed_part = mixed_part.reshape(3, LANES)[:, :local].reshape(-1)
        return gm, e, jnp.concatenate([norm_part.reshape(-1), mixed_part, up_part.reshape(-1)])

    def step_grad(layer, index, pending):
        scaled = plan.scatter_rest(pending)
        normed, inverse = standardize(kept[layer][0][index].astype(f32))
        grad = grads[index].astype(f32) + inverse * (
            scaled
            - jnp.mean(scaled, -1, keepdims=True)
            - normed * jnp.mean(scaled * normed, -1, keepdims=True)
        )
        return grad.astype(bf16)

    def early_terms(layer, gathered, grad_up):
        state = kept[layer][1]
        every = [gathered[index] for index in range(plan.chunks)]
        ups = [grad_up[index] for index in range(plan.chunks)]
        return [
            over_tokens(every, [s["h"] for s in state]).astype(bf16),
            over_tokens([s["a1"] for s in state], ups).astype(bf16),
            over_tokens(every, [s["o"] for s in state]).astype(bf16),
        ]

    def qkv_terms(layer, grad_mixed):
        term = over_tokens(
            [s["a0"] for s in kept[layer][1]], [grad_mixed[index] for index in range(plan.chunks)]
        )
        return term.astype(bf16)

    def without_fill(array):
        return array.reshape(-1, 3, LANES)[:, :, :local].reshape(-1, 3 * local)

    def bias_sum(grads):
        return sum(jnp.sum(item.astype(f32), 0) for item in grads)

    order = list(reversed(range(plan.chunks)))
    second_grads = grads
    results, grad_mixed, pending, sums, carried = {}, {}, {}, 0.0, ((), ())
    grad_up = {
        index: feed_back(gathered[index], layers[1], kept[1][1][index]["d"]) for index in order
    }
    early = jnp.concatenate(early_terms(1, gathered, grad_up), 1)
    held = [hold(item, kept[1][1][last]["q"]) for item in outputs[0]]
    owned_first = plan.owned(held, 0, kept[1][1][last]["o"])
    early_second = lax.psum_scatter(
        early, ("wide", "section"), scatter_dimension=0, tiled=True
    )
    waiting = tuple(parts) + (early,)
    for index in order:
        results[index] = step_back(1, index, gathered[index], carried, waiting)
        carried = results[index][-1]
        if index == last:
            token = results[last][0]
            second_outputs = [
                finished(other, pending_out[other], blocks, layers[1], token)
                for other in range(plan.chunks)
            ]
            tied = (owned_first, *second_outputs)
        else:
            tied = (pending[index + 1],)
        grad_mixed[index], e, part = step_leave(1, index, results[index], grad_up[index], tied)
        sums += part
        pending[index] = plan.scatter_first([e])
        waiting = (e,)
    after = {}
    for index in order:
        if after:
            pending[index] = hold(pending[index], after[index + 1])
        after[index] = step_grad(1, index, pending[index])
    small_second = jnp.concatenate([sums, bias_sum(grads)])
    second_qkv = qkv_terms(1, grad_mixed)
    input_second = [after[index] for index in range(plan.chunks)]
    grads = input_second
    gathered = {index: plan.gather(grads[index]) for index in order}
    results, grad_mixed, pending, sums, carried = {}, {}, {}, 0.0, ((), ())
    grad_up = {
        index: feed_back(gathered[index], layers[0], kept[0][1][index]["d"]) for index in order
    }
    early = jnp.concatenate(early_terms(0, gathered, grad_up) + [second_qkv], 1)
    early_sum = lax.psum_scatter(early, ("wide", "section"), scatter_dimension=0, tiled=True)
    held = [hold(item, gathered[last]) for item in second_outputs]
    waiting = (early,)
    for index in order:
        results[index] = step_back(0, index, gathered[index], carried, waiting)
        carried = results[index][-1]
        tied = (early_second,) if index == last else (pending[index + 1],)
        grad_mixed[index], e, part = step_leave(0, index, results[index], grad_up[index], tied)
        sums += part
        pending[index] = plan.scatter_first([e])
        waiting = (e,)
    after = {index: step_grad(0, index, pending[index]) for index in order}
    input_first = [hold(after[index], early_sum) for index in range(plan.chunks)]
    all_grads = plan.exchange(input_first, input_second)
    qkv_shares = plan.wide_steps_of(
        hold(without_fill(qkv_terms(0, grad_mixed)), after[0])
    )
    owned_second = plan.owned(held, 1, grad_mixed[0])
    total = jnp.stack([jnp.concatenate([sums, bias_sum(grads)]), small_second])
    at = 4 * width + 3 * local
    shared = jnp.concatenate([total[:, : 4 * width], total[:, at + hidden :]], 1)
    shared = plan.sum_all(shared, ("tp",))
    total = hold(jnp.concatenate([shared, total[:, 4 * width : at + hidden]], 1), after[0])
    if plan.wide > 4:
        total = lax.psum(total, "wide")
    else:
        terms = [total] + plan.wide_steps(lambda step: total)
        while len(terms) > 1:
            terms = [one + two for one, two in zip(terms[::2], terms[1::2])]
        total = terms[0]
    first_qkv_sum = sum(item.astype(f32) for item in qkv_shares)
    split = 2 * hidden + LANES
    here = plan.send(early_second, 0)
    there, here_qkv = plan.send(early_sum[:, :split], 1), plan.send(early_sum[:, split:], 0)
    early = pick(
        section,
        jnp.concatenate([early_sum[:, :split], there], 0),
        jnp.concatenate([here, early_second], 0),
    ).astype(f32)
    qkv_grad = first_qkv_sum + plan.send(first_qkv_sum.astype(bf16), 1).astype(f32)
    second_qkv = without_fill(jnp.concatenate([here_qkv, early_sum[:, split:]], 0)).astype(f32)
    qkv_grad = pick(section, qkv_grad, second_qkv)
    down_grad, up_grad = early[:, :hidden], early[:, hidden : 2 * hidden]
    out_grad = early[:, 2 * hidden : 2 * hidden + local]
    total = total + plan.swap(total)
    total = pick(section, total[0], total[1])
    shared, own = total[: 5 * width], total[5 * width :]
    bias_grad = shared[4 * width :]
    return (
        pick(section, owned_first, owned_second)[None, :, None],
        all_grads.astype(f32)[None, :, None],
        shared[: 2 * width].reshape(1, 2, width),
        shared[2 * width : 4 * width].reshape(1, 2, width),
        qkv_grad.reshape(1, -1, 3, local),
        own[: 3 * local].reshape(1, 3, local),
        out_grad.T[None],
        bias_grad[None],
        up_grad[None],
        own[3 * local :][None],
        down_grad.T[None],
        bias_grad[None],
    )


def solution(mesh):
    return jax.shard_map(
        on_device,
        mesh=mesh,
        in_specs=(
            P(None, "tp", "wide", None),
            P(None, "tp", "wide", None),
            P(),
            P("section", None, None),
            P("section", None, None),
            P("section", "wide", None, "tp"),
            P("section", None, "tp"),
            P("section", "tp", "wide"),
            P("section", None),
            P("section", "wide", "tp"),
            P("section", "tp"),
            P("section", "tp", "wide"),
            P("section", None),
        ),
        out_specs=(
            P("section", None, "tp", "wide", None),
            P("section", None, "tp", "wide", None),
            P("section", None, None),
            P("section", None, None),
            P("section", "wide", None, "tp"),
            P("section", None, "tp"),
            P("section", "tp", "wide"),
            P("section", None),
            P("section", "wide", "tp"),
            P("section", "tp"),
            P("section", "tp", "wide"),
            P("section", None),
        ),
        check_vma=False,
    )
```

```python
import functools

import jax
import jax.numpy as jnp
import numpy as np
from jax import lax
from jax.experimental import pallas as pl
from jax.experimental.pallas import tpu as pltpu
from jax.sharding import PartitionSpec as P

HEAD_DIM = 64
ROTARY = 16
LANES = 256
CHUNKS = 1
QUERY_BLOCK = 256
KEY_BLOCK = 512
ROW_BLOCK = 256

epsilon = 1e-05
rotary_base = 10000.0
masked_out = -1e30
f32 = jnp.float32
bf16 = jnp.bfloat16
NT = (((1,), (1,)), ((), ()))


def params(size=44):
    return pltpu.CompilerParams(
        dimension_semantics=("arbitrary",), vmem_limit_bytes=size * 1024 * 1024
    )


def dot(left, right):
    return jnp.dot(left, right, preferred_element_type=f32)


def dot_nt(left, right):
    return lax.dot_general(left, right, NT, preferred_element_type=f32)


def rows_spec(rows, columns):
    return pl.BlockSpec((rows, columns), lambda i: (i, 0))


def whole_spec(array):
    return pl.BlockSpec(array.shape, lambda i: (0,) * array.ndim)


def smem_spec():
    return pl.BlockSpec(memory_space=pltpu.SMEM)


def standardize(values):
    centred = values - jnp.mean(values, -1, keepdims=True)
    inverse = lax.rsqrt(jnp.mean(centred * centred, -1, keepdims=True) + epsilon)
    return centred * inverse, inverse


def wide_table(ref):
    return jnp.concatenate([ref[...]] * (LANES // ref.shape[1]), 1)


def halves(signed):
    place = lax.broadcasted_iota(jnp.int32, signed.shape, 1) % HEAD_DIM
    zero = jnp.zeros_like(signed)
    half = ROTARY // 2
    return jnp.where(place < half, signed, zero), jnp.where(place < half, zero, signed)


def turn(values, cosine, signed):
    half = ROTARY // 2
    low, high = halves(signed)
    ahead = pltpu.roll(values, LANES - half, 1)
    behind = pltpu.roll(values, half, 1)
    return values * cosine + ahead * low + behind * high


def turn_back(grads, cosine, signed):
    half = ROTARY // 2
    low, high = halves(signed)
    ahead = pltpu.roll(grads * high, LANES - half, 1)
    behind = pltpu.roll(grads * low, half, 1)
    return grads * cosine + ahead + behind


def any_specs(arrays):
    return [pl.BlockSpec(memory_space=pl.ANY)] * len(arrays)


def cost(micros, transfers):
    return pl.CostEstimate(
        flops=int(micros * 1.15e9), bytes_accessed=int(transfers), transcendentals=0
    )


class View:
    def __init__(self, array, first, width, part=0, parts=1):
        if first % width:
            array, first = array[:, first : first + width], 0
        self.array, self.block = array, (part, first // width)
        self.shape = (array.shape[0] // parts, width)

    def spec(self):
        block = self.block
        return pl.BlockSpec(self.shape, lambda i: block)


def project_kernel(heads, x_ref, gs_ref, w_ref, b_ref, c_ref, s_ref, seg_ref, *rest):
    a0_ref, a1_ref, q_ref, k_ref, v_ref = rest[-5:]
    normed, _ = standardize(x_ref[...].astype(f32))
    first = (normed * gs_ref[0:1] + gs_ref[2:3]).astype(bf16)
    a0_ref[...] = first
    a1_ref[...] = (normed * gs_ref[1:2] + gs_ref[3:4]).astype(bf16)
    mixed = dot(first, w_ref[...]) + b_ref[...]
    cosine, signed = wide_table(c_ref), wide_table(s_ref)
    query = turn(mixed[:, :LANES], cosine, signed)
    keys = turn(mixed[:, LANES : 2 * LANES], cosine, signed)
    lane = lax.broadcasted_iota(jnp.int32, query.shape, 1)
    used = heads * HEAD_DIM
    mine = (lane - used) == seg_ref[...]
    spare = lane >= used
    q_ref[...] = jnp.where(
        spare, jnp.where(mine, 1.0, 0.0), query * HEAD_DIM ** (-0.5)
    ).astype(bf16)
    k_ref[...] = jnp.where(spare, jnp.where(mine, 0.0, masked_out), keys).astype(bf16)
    v_ref[...] = mixed[:, 2 * LANES :].astype(bf16)


def project(x, w, tables, seg, heads, after=()):
    tokens, width = x.shape
    rows = min(ROW_BLOCK, tokens)
    columns = (width, width, LANES, LANES, LANES)
    return pl.pallas_call(
        functools.partial(project_kernel, heads),
        grid=(tokens // rows,),
        in_specs=[rows_spec(rows, width), whole_spec(w["gs"]), w["wq"].spec()]
        + [whole_spec(w["bq"])]
        + [rows_spec(rows, item.shape[1]) for item in tables]
        + [rows_spec(rows, 1)]
        + any_specs(after),
        out_specs=[rows_spec(rows, item) for item in columns],
        out_shape=[jax.ShapeDtypeStruct((tokens, item), bf16) for item in columns],
        compiler_params=params(),
        cost_estimate=cost(4.0 * tokens / 1024, 6 * tokens * width),
        name="project",
    )(x, w["gs"], w["wq"].array, w["bq"], *tables, seg, *after)


def feed_kernel(a_ref, o_ref, wu_ref, bu_ref, wd_ref, wo_ref, *rest):
    h_ref, d_ref, part_ref = rest[-3:]
    before = dot(a_ref[...], wu_ref[...]) + bu_ref[...]
    phi = 0.5 + 0.5 * lax.erf(before * (0.5**0.5))
    density = jnp.exp(before * before * (-0.5)) * 0.3989422804014327
    hidden = (before * phi).astype(bf16)
    h_ref[...] = hidden
    d_ref[...] = (phi + before * density).astype(bf16)
    part_ref[...] = (dot_nt(hidden, wd_ref[...]) + dot_nt(o_ref[...], wo_ref[...])).astype(bf16)


def feed(a1, o, w, after=()):
    tokens, width = a1.shape
    rows = min(ROW_BLOCK, tokens)
    hidden = w["bu"].shape[1]
    columns = (hidden, hidden, width)
    return pl.pallas_call(
        feed_kernel,
        grid=(tokens // rows,),
        in_specs=[rows_spec(rows, width), rows_spec(rows, LANES), w["wu"].spec()]
        + [whole_spec(w["bu"]), w["wd"].spec(), w["wo"].spec()]
        + any_specs(after),
        out_specs=[rows_spec(rows, item) for item in columns],
        out_shape=[jax.ShapeDtypeStruct((tokens, item), bf16) for item in columns],
        compiler_params=params(),
        cost_estimate=cost(5.0 * tokens / 1024, 6 * tokens * width),
        name="feed",
    )(a1, o, w["wu"].array, w["bu"], w["wd"].array, w["wo"].array, *after)


def feed_back_kernel(gb_ref, wd_ref, d_ref, *rest):
    rest[-1][...] = (dot(gb_ref[...], wd_ref[...]) * d_ref[...].astype(f32)).astype(bf16)


def feed_back(gb, w, d, after=()):
    tokens, width = gb.shape
    rows = min(ROW_BLOCK, tokens)
    hidden = d.shape[1]
    return pl.pallas_call(
        feed_back_kernel,
        grid=(tokens // rows,),
        in_specs=[rows_spec(rows, width), w["wd"].spec(), rows_spec(rows, hidden)]
        + any_specs(after),
        out_specs=rows_spec(rows, hidden),
        out_shape=jax.ShapeDtypeStruct((tokens, hidden), bf16),
        compiler_params=params(),
        cost_estimate=cost(2.0 * tokens / 1024, 6 * tokens * width),
        name="feed_back",
    )(gb, w["wd"].array, d, *after)


def head_lanes(array, heads, spare):
    lane = lax.broadcasted_iota(jnp.int32, array.shape, 1)
    zero = jnp.zeros_like(array)
    result = []
    for head in range(heads):
        keep = (lane >= head * HEAD_DIM) & (lane < (head + 1) * HEAD_DIM)
        if spare:
            keep = keep | (lane >= heads * HEAD_DIM)
        result.append(jnp.where(keep, array, zero))
    return result


def join_once(parts, target):
    @pl.when(pl.program_id(0) == 0)
    def _():
        first = 0
        for part in parts:
            target[first : first + part.shape[0], :] = part[...]
            first += part.shape[0]


def attend_kernel(heads, key_block, pieces, start_ref, q_ref, *rest):
    k_refs, v_refs = rest[:pieces], rest[pieces : 2 * pieces]
    o_ref, lse_ref, top_ref, sum_ref, acc_ref, k_ref, vt_ref = rest[-7:]
    join_once(k_refs, k_ref)

    @pl.when(pl.program_id(0) == 0)
    def _():
        acc_ref[...] = jnp.zeros(acc_ref.shape, f32)
        first = 0
        for ref in v_refs:
            block = min(key_block, ref.shape[0])
            for at in range(0, ref.shape[0], block):
                vt_ref[:, first + at : first + at + block] = ref[at : at + block, :].T
            first += ref.shape[0]

    rows = q_ref.shape[0]
    queries = head_lanes(q_ref[...], heads, True)
    first_row = start_ref[0] + pl.program_id(0) * rows
    full = first_row // key_block

    def step(block, diagonal, fresh):
        place = pl.ds(pl.multiple_of(block * key_block, key_block), key_block)
        keys = k_ref[place, :]
        for head in range(heads):
            here = slice(head * HEAD_DIM, (head + 1) * HEAD_DIM)
            line = slice(head, head + 1)
            scores = dot_nt(keys, queries[head])
            if diagonal:
                column = lax.broadcasted_iota(jnp.int32, scores.shape, 0) + block * key_block
                row = lax.broadcasted_iota(jnp.int32, scores.shape, 1) + first_row
                scores = jnp.where(column <= row, scores, masked_out)
            top = jnp.max(scores, 0, keepdims=True)
            if not fresh:
                before = top_ref[line, :]
                top = jnp.maximum(before, top)
                fade = jnp.exp(before - top)
            probs = jnp.exp(scores - top)
            total = jnp.sum(probs, 0, keepdims=True)
            value = dot(vt_ref[here, place], probs.astype(bf16))
            if not fresh:
                total += sum_ref[line, :] * fade
                value += acc_ref[here, :] * fade
            top_ref[line, :] = top
            sum_ref[line, :] = total
            acc_ref[here, :] = value

    step(full, True, True)

    @pl.loop(0, full)
    def _(block):
        step(block, False, False)

    for head in range(heads):
        here = slice(head * HEAD_DIM, (head + 1) * HEAD_DIM)
        acc_ref[here, :] = acc_ref[here, :] / sum_ref[head : head + 1, :]
    o_ref[...] = acc_ref[...].T.astype(bf16)
    lse_ref[...] = jnp.zeros(lse_ref.shape, f32)
    lse_ref[:heads, :] = top_ref[:heads, :] + jnp.log(sum_ref[:heads, :])


def attend(start, q, keys, values, heads, after=()):
    tokens = q.shape[0]
    rows = min(QUERY_BLOCK, tokens)
    span = sum(item.shape[0] for item in keys)
    key_block = min(KEY_BLOCK, span)
    return pl.pallas_call(
        functools.partial(attend_kernel, heads, key_block, len(keys)),
        grid=(tokens // rows,),
        in_specs=[smem_spec(), rows_spec(rows, LANES)]
        + [whole_spec(item) for item in (*keys, *values)]
        + any_specs(after),
        out_specs=[rows_spec(rows, LANES), pl.BlockSpec((8, rows), lambda i: (0, i))],
        out_shape=[
            jax.ShapeDtypeStruct((tokens, LANES), bf16),
            jax.ShapeDtypeStruct((8, tokens), f32),
        ],
        scratch_shapes=[pltpu.VMEM((8, rows), f32)] * 2
        + [pltpu.VMEM((LANES, rows), f32)]
        + [pltpu.VMEM((span, LANES), bf16), pltpu.VMEM((LANES, span), bf16)],
        compiler_params=params(),
        cost_estimate=cost(7.0 * tokens * span / 1024 / 1024, 6 * tokens * LANES),
        name="attend",
    )(start, q, *keys, *values, *after)


def attend_back_kernel(
    heads, key_block, pieces, carried, start_ref, gb_ref, w_ref, q_ref, o_ref, *rest,
):
    lse_ref, rest = rest[0], rest[1:]
    k_refs, v_refs, rest = rest[:pieces], rest[pieces : 2 * pieces], rest[2 * pieces :]
    carry_refs = rest[: 2 * carried]
    dq_ref, rest = rest[-(2 * pieces + 7)], rest[-(2 * pieces + 6) :]
    dk_refs, dv_refs, rest = rest[:pieces], rest[pieces : 2 * pieces], rest[2 * pieces :]
    k_ref, v_ref, kt_ref, dk_ref, dv_ref, dqt_ref = rest
    rows = q_ref.shape[0]
    first_row = start_ref[0] + pl.program_id(0) * rows
    full = first_row // key_block
    join_once(k_refs, k_ref)
    join_once(v_refs, v_ref)

    @pl.when(pl.program_id(0) == 0)
    def _():
        dk_ref[...] = jnp.zeros(dk_ref.shape, f32)
        dv_ref[...] = jnp.zeros(dv_ref.shape, f32)
        for refs, target in ((carry_refs[:carried], dk_ref), (carry_refs[carried:], dv_ref)):
            first = 0
            for ref in refs:
                target[first : first + ref.shape[0], :] = ref[...]
                first += ref.shape[0]
        for first in range(0, k_ref.shape[0], key_block):
            kt_ref[:, first : first + key_block] = k_ref[first : first + key_block, :].T

    grad = gb_ref[...]
    grad_out = dot(grad, w_ref[...]).astype(bf16)
    product = (grad_out.astype(f32) * o_ref[...].astype(f32)).T
    centres = [
        jnp.sum(product[head * HEAD_DIM : (head + 1) * HEAD_DIM], 0, keepdims=True)
        for head in range(heads)
    ]
    queries = head_lanes(q_ref[...], heads, True)
    grads = head_lanes(grad_out, heads, False)
    dqt_ref[...] = jnp.zeros(dqt_ref.shape, f32)

    def step(block, diagonal):
        place = pl.ds(pl.multiple_of(block * key_block, key_block), key_block)
        keys = k_ref[place, :]
        values = v_ref[place, :]
        grad_keys = dk_ref[place, :]
        grad_values = dv_ref[place, :]
        for head in range(heads):
            here = slice(head * HEAD_DIM, (head + 1) * HEAD_DIM)
            scores = dot_nt(keys, queries[head])
            probs = jnp.exp(scores - lse_ref[head : head + 1, :])
            if diagonal:
                column = lax.broadcasted_iota(jnp.int32, scores.shape, 0) + block * key_block
                row = lax.broadcasted_iota(jnp.int32, scores.shape, 1) + first_row
                probs = jnp.where(column <= row, probs, 0.0)
            grad_probs = dot_nt(values, grads[head])
            grad_scores = (probs * (grad_probs - centres[head])).astype(bf16)
            grad_values += dot(probs.astype(bf16), grads[head])
            grad_keys += dot(grad_scores, queries[head])
            dqt_ref[here, :] += dot(kt_ref[here, place], grad_scores)
        dk_ref[place, :] = grad_keys
        dv_ref[place, :] = grad_values

    @pl.loop(0, full)
    def _(block):
        step(block, False)

    step(full, True)
    dq_ref[...] = dqt_ref[...].T * HEAD_DIM ** (-0.5)

    @pl.when(pl.program_id(0) == pl.num_programs(0) - 1)
    def _():
        for refs, source in ((dk_refs, dk_ref), (dv_refs, dv_ref)):
            first = 0
            for ref in refs:
                ref[...] = source[first : first + ref.shape[0], :]
                first += ref.shape[0]


def attend_back(start, gb, w, q, o, lse, keys, values, carried, heads, after=()):
    tokens, width = gb.shape
    rows = min(QUERY_BLOCK, tokens)
    sizes = [item.shape[0] for item in keys]
    span = sum(sizes)
    key_block = min(KEY_BLOCK, span)
    carry_keys, carry_values = carried
    whole = [pl.BlockSpec((size, LANES), lambda i: (0, 0)) for size in sizes]
    result = pl.pallas_call(
        functools.partial(attend_back_kernel, heads, key_block, len(keys), len(carry_keys)),
        grid=(tokens // rows,),
        in_specs=[smem_spec(), rows_spec(rows, width), w["wo"].spec()]
        + [rows_spec(rows, LANES), rows_spec(rows, LANES)]
        + [pl.BlockSpec((8, rows), lambda i: (0, i))]
        + [whole_spec(item) for item in (*keys, *values, *carry_keys, *carry_values)]
        + any_specs(after),
        out_specs=[rows_spec(rows, LANES)] + whole + whole,
        out_shape=[jax.ShapeDtypeStruct((tokens, LANES), f32)]
        + [jax.ShapeDtypeStruct((size, LANES), f32) for size in sizes] * 2,
        scratch_shapes=[pltpu.VMEM((span, LANES), bf16)] * 2
        + [pltpu.VMEM((LANES, span), bf16)]
        + [pltpu.VMEM((span, LANES), f32)] * 2
        + [pltpu.VMEM((LANES, rows), f32)],
        compiler_params=params(),
        cost_estimate=cost(12.5 * tokens * span / 1024 / 1024, 4 * tokens * width),
        name="attend_back",
    )(start, gb, w["wo"].array, q, o, lse, *keys, *values, *carry_keys, *carry_values, *after)
    pieces = len(keys)
    return result[0], result[1 : 1 + pieces], result[1 + pieces :]


def leave_kernel(
    x_ref, gs_ref, dq_ref, dk_ref, dv_ref, gu_ref, wq_ref, wu_ref, c_ref, s_ref, *rest,
):
    gm_ref, e_ref, norm_ref, mixed_ref, up_ref = rest[-5:]

    @pl.when(pl.program_id(0) == 0)
    def _():
        norm_ref[...] = jnp.zeros(norm_ref.shape, f32)
        mixed_ref[...] = jnp.zeros(mixed_ref.shape, f32)
        up_ref[...] = jnp.zeros(up_ref.shape, f32)

    cosine, signed = wide_table(c_ref), wide_table(s_ref)
    grads = jnp.concatenate(
        [
            turn_back(dq_ref[...], cosine, signed),
            turn_back(dk_ref[...], cosine, signed),
            dv_ref[...],
        ],
        1,
    ).astype(bf16)
    gm_ref[...] = grads
    grad_up = gu_ref[...]
    mixed_ref[...] += jnp.sum(grads.astype(f32), 0, keepdims=True)
    up_ref[...] += jnp.sum(grad_up.astype(f32), 0, keepdims=True)
    grad_first = dot_nt(grads, wq_ref[...])
    grad_second = dot_nt(grad_up, wu_ref[...])
    normed, _ = standardize(x_ref[...].astype(f32))
    norm_ref[0:1] += jnp.sum(grad_first * normed, 0, keepdims=True)
    norm_ref[1:2] += jnp.sum(grad_second * normed, 0, keepdims=True)
    norm_ref[2:3] += jnp.sum(grad_first, 0, keepdims=True)
    norm_ref[3:4] += jnp.sum(grad_second, 0, keepdims=True)
    e_ref[...] = (grad_first * gs_ref[0:1] + grad_second * gs_ref[1:2]).astype(bf16)


def leave(x, dq, dk, dv, gu, w, tables, after=()):
    tokens, width = x.shape
    rows = min(ROW_BLOCK, tokens)
    mixed = 3 * LANES
    hidden = gu.shape[1]
    sums = [(4, width), (1, mixed), (1, hidden)]
    return pl.pallas_call(
        leave_kernel,
        grid=(tokens // rows,),
        in_specs=[rows_spec(rows, width), whole_spec(w["gs"])]
        + [rows_spec(rows, LANES)] * 3
        + [rows_spec(rows, hidden), w["wq"].spec(), w["wu"].spec()]
        + [rows_spec(rows, item.shape[1]) for item in tables]
        + any_specs(after),
        out_specs=[rows_spec(rows, mixed), rows_spec(rows, width)]
        + [pl.BlockSpec(item, lambda i: (0, 0)) for item in sums],
        out_shape=[
            jax.ShapeDtypeStruct((tokens, mixed), bf16),
            jax.ShapeDtypeStruct((tokens, width), bf16),
        ]
        + [jax.ShapeDtypeStruct(item, f32) for item in sums],
        compiler_params=params(),
        cost_estimate=cost(6.7 * tokens / 1024, 6 * tokens * width),
        name="leave",
    )(x, w["gs"], dq, dk, dv, gu, w["wq"].array, w["wu"].array, *tables, *after)


def hold(value, *tokens):
    for token in tokens:
        first = token[(slice(0, 1),) * token.ndim].reshape((1,) * value.ndim)
        value = jnp.where(first == jnp.inf, jnp.zeros_like(value), value)
    return value


def pick(bit, zero, one):
    return jnp.where(bit == 0, zero, one)


def mirrored(index, bits):
    return sum(((index >> bit) & 1) << (bits - 1 - bit) for bit in range(bits))


class Plan:
    def __init__(self, batch, length):
        self.wide, self.tp = lax.axis_size("wide"), lax.axis_size("tp")
        self.batch, self.length = batch, length
        self.bits = self.tp.bit_length() - 1
        self.group = self.wide // batch
        self.sequence_bits = batch.bit_length() - 1
        self.chunks = CHUNKS if self.group == 1 else 1
        self.unit = length // (self.wide * self.chunks)
        self.section = lax.axis_index("section")
        self.wide_index = lax.axis_index("wide")
        self.tp_index = lax.axis_index("tp")
        self.sequence = mirrored(self.wide_index // self.group, self.sequence_bits)
        self.part = mirrored(self.tp_index, self.bits)

    def units(self):
        for unit in range(self.wide * self.chunks):
            owner, half = divmod(unit, self.chunks)
            rest, part = divmod(unit, self.tp)
            sub, chunk = divmod(rest, self.chunks)
            for sequence in range(self.batch):
                place = mirrored(sequence, self.sequence_bits) * self.group + sub
                worker = place * self.tp + mirrored(part, self.bits)
                yield owner * self.tp + sequence, worker, half, chunk, part

    def to_work(self, block):
        chunks = []
        for chunk in range(self.chunks):
            result = None
            for half in range(self.chunks):
                pairs = [u[:2] for u in self.units() if u[2] == half and u[3] == chunk]
                piece = block[half * self.unit : (half + 1) * self.unit]
                if chunks:
                    piece = hold(piece, chunks[0])
                piece = lax.ppermute(piece, ("wide", "tp"), pairs)
                if result is None:
                    result = piece
                else:
                    result = jnp.where(self.part % self.chunks == half, piece, result)
            chunks.append(result)
        return chunks

    def to_work_whole(self, block):
        received = []
        own = (self.wide_index * self.chunks // self.tp) % self.chunks
        for turn_index in range(self.chunks):
            piece = block[: self.unit]
            for half in range(1, self.chunks):
                here = (own - turn_index) % self.chunks == half
                piece = jnp.where(here, block[half * self.unit : (half + 1) * self.unit], piece)
            pairs = [u[:2] for u in self.units() if (u[4] + turn_index) % self.chunks == u[3]]
            received.append(lax.ppermute(piece, ("wide", "tp"), pairs))
        chunks = []
        for chunk in range(self.chunks):
            piece = received[0]
            for turn_index in range(1, self.chunks):
                here = (self.part + turn_index) % self.chunks == chunk
                piece = jnp.where(here, received[turn_index], piece)
            chunks.append(piece)
        return chunks

    def to_owner(self, chunks, planes, tokens):
        devices = self.wide * self.tp
        received = []
        for turn_index in range(self.chunks):
            piece = chunks[0]
            for chunk in range(1, self.chunks):
                here = (self.part + turn_index) % self.chunks == chunk
                piece = jnp.where(here, chunks[chunk], piece)
            pairs = []
            for owner, worker, _, chunk, part in self.units():
                if (part + turn_index) % self.chunks == chunk:
                    for plane, target in planes:
                        pairs.append((plane * devices + worker, target * devices + owner))
            piece = lax.ppermute(piece, ("section", "wide", "tp"), pairs)
            received.append(hold(piece, *tokens))
        if self.chunks == 1:
            return received[0]
        chunk = (self.wide_index * self.chunks // self.tp) % self.chunks
        ordered = []
        for half in range(self.chunks):
            piece = received[0]
            for turn_index in range(1, self.chunks):
                piece = jnp.where(
                    (chunk - half) % self.chunks == turn_index, received[turn_index], piece
                )
            ordered.append(piece)
        return jnp.concatenate(ordered, 0)

    def owned(self, chunks, layer, *tokens):
        return jnp.stack([self.to_owner(chunks, [(micro, layer)], tokens) for micro in range(2)])

    def exchange(self, first, second, *tokens):
        mine = [pick(self.section, a, b) for a, b in zip(first, second)]
        other = [pick(self.section, b, a) for a, b in zip(first, second)]
        same = self.to_owner(mine, [(0, 0), (1, 1)], tokens)
        cross = self.to_owner(other, [(0, 1), (1, 0)], tokens)
        return jnp.stack([pick(self.section, same, cross), pick(self.section, cross, same)])

    def wide_steps(self, value_at):
        return [
            lax.ppermute(
                value_at(step), "wide", [(index, index ^ step) for index in range(self.wide)]
            )
            for step in range(1, self.wide)
        ]

    def wide_scatter(self, block):
        if self.wide > 4:
            return lax.psum_scatter(
                block, "wide", scatter_dimension=0, tiled=True
            ).astype(f32)
        return sum(item.astype(f32) for item in self.wide_steps_of(block))

    def wide_steps_of(self, block):
        if self.wide > 4:
            return [self.wide_scatter(block)]
        rows = block.shape[0] // self.wide

        def share(step):
            first = (self.wide_index ^ step) * rows
            return lax.dynamic_slice_in_dim(block, first, rows, 0)

        return [share(0)] + self.wide_steps(share)

    def sum_all(self, value, axes):
        for axis in axes:
            count = lax.axis_size(axis)
            step = 1
            while step < count:
                pairs = [(index, index ^ step) for index in range(count)]
                value = value + lax.ppermute(value, axis, pairs)
                step *= 2
        return value

    def swap(self, value):
        return lax.ppermute(value, "section", [(0, 1), (1, 0)])

    def send(self, value, source):
        return lax.ppermute(value, "section", [(source, 1 - source)])

    def gather(self, block):
        return self.gather_rest(self.gather_first(block))

    def gather_first(self, block):
        return self.gather_bits(block, range(self.bits - 1, 0, -1))

    def gather_rest(self, block):
        return self.gather_bits(block, [0])

    def gather_bits(self, block, bits):
        for bit in bits:
            other = lax.ppermute(
                block, "tp", [(index, index ^ (1 << bit)) for index in range(self.tp)]
            )
            here = (self.tp_index >> bit) & 1
            block = jnp.concatenate([pick(here, block, other), pick(here, other, block)], 0)
        return block

    def scatter_first(self, pieces):
        here = self.tp_index & 1
        if len(pieces) == 1:
            half = pieces[0].shape[0] // 2
            pieces = [pieces[0][:half], pieces[0][half:]]
        other = lax.ppermute(
            pick(here, pieces[1], pieces[0]), "tp", [(i, i ^ 1) for i in range(self.tp)]
        )
        return pick(here, pieces[0], pieces[1]).astype(f32) + other.astype(f32)

    def scatter_rest(self, block, *tokens):
        for bit in range(1, self.bits):
            half = block.shape[0] // 2
            here = (self.tp_index >> bit) & 1
            sent = pick(here, block[half:], block[:half]).astype(bf16)
            kept = pick(here, block[:half], block[half:])
            other = lax.ppermute(
                sent, "tp", [(index, index ^ (1 << bit)) for index in range(self.tp)]
            )
            block = kept + hold(other, *tokens).astype(f32)
        return block

    def groups(self):
        return [
            [sequence * self.group + sub for sub in range(self.group)]
            for sequence in range(self.batch)
        ]

    def all_places(self, block):
        if self.group == 1:
            return block
        return lax.all_gather(block, "wide", axis=0, tiled=True, axis_index_groups=self.groups())

    def own_places(self, block):
        if self.group == 1:
            return block
        return lax.psum_scatter(
            block.astype(bf16), "wide", scatter_dimension=0, tiled=True,
            axis_index_groups=self.groups(),
        ).astype(f32)


def angle_tables(length):
    half = ROTARY // 2
    freqs = np.float32(rotary_base) ** (-(2.0 * np.arange(half, dtype=np.float32)) / ROTARY)
    turned = np.arange(length, dtype=np.float32)[:, None] * freqs[None, :].astype(np.float32)
    cosine, sine = np.cos(turned), np.sin(turned)
    rest = np.zeros((length, HEAD_DIM - ROTARY), np.float32)
    return (
        np.concatenate([cosine, cosine, rest + 1.0] * 2, 1).astype(np.float32),
        np.concatenate([-sine, sine, rest] * 2, 1).astype(np.float32),
    )


def on_device(
    inputs, cotangent, segment_ids, norm_gain, norm_shift, qkv_weight, qkv_bias, out_weight,
    out_bias, up_weight, up_bias, down_weight, down_bias,
):
    batch, length = segment_ids.shape[1], segment_ids.shape[2]
    plan = Plan(batch, length)
    width = inputs.shape[-1]
    local = qkv_weight.shape[-1]
    hidden = up_weight.shape[-1]
    heads = local // HEAD_DIM
    section = plan.section
    space = LANES - local

    fill = ((0, 0), (0, 0), (0, space))
    qkv = qkv_weight[0].reshape(-1, 3 * local)
    up = up_weight[0]
    leaving = jnp.concatenate(
        [down_weight[0].T, jnp.pad(out_weight[0].T, ((0, 0), (0, space)))], 1
    )
    small = jnp.concatenate(
        [
            norm_gain[0].reshape(-1), norm_shift[0].reshape(-1), out_bias[0] + down_bias[0],
            jnp.pad(qkv_bias[0], ((0, 0), (0, space))).reshape(-1), up_bias[0],
        ]
    )
    first = section == 0
    mixed = 3 * LANES
    small_there = plan.swap(small)
    padded = jnp.pad(qkv_weight[0], fill).reshape(-1, mixed)
    weights = jnp.concatenate([padded, up, leaving], 1)
    share = weights.shape[0] // 2
    half_there = plan.swap(jnp.where(first, weights[share:], weights[:share]))

    def gather_halves(plane_zero, plane_one):
        half = jnp.where(first, plane_zero, plane_one)
        array = lax.all_gather(half, ("wide", "section"), axis=0, tiled=True)
        at = mixed + hidden
        return array, dict(
            wq=View(array, 0, mixed), wu=View(array, mixed, hidden),
            wd=View(array, at, hidden), wo=View(array, at + hidden, LANES),
        )

    source = plan.to_work(jnp.where(first, inputs[0, 0], inputs[1, 0]))
    weights_first, views_first = gather_halves(weights[:share], half_there)
    weights_second, views_second = gather_halves(
        half_there, hold(weights[share:], weights_first)
    )
    layers = [views_first, views_second]
    for layer, w in enumerate(layers):
        values = jnp.where(section == layer, small, small_there)
        at = 5 * width
        w["gs"] = values[: 4 * width].reshape(4, width)
        w["after"] = values[4 * width : at]
        w["bq"] = values[at : at + mixed].reshape(1, mixed)
        w["bu"] = values[at + mixed :].reshape(1, hidden)

    segments = lax.dynamic_index_in_dim(segment_ids, section, 0, False)
    segments = lax.dynamic_index_in_dim(segments, plan.sequence, 0, False)
    sub_length = length // plan.group
    first_place = (plan.wide_index % plan.group) * sub_length
    tables = angle_tables(length)
    if plan.group > 1:
        segments = lax.dynamic_slice_in_dim(segments, first_place, sub_length, 0)
        tables = [lax.dynamic_slice_in_dim(t, first_place, sub_length, 0) for t in tables]
    size = plan.unit * plan.tp
    starts = [(first_place + index * size).reshape(1) for index in range(plan.chunks)]
    spans = [slice(index * size, (index + 1) * size) for index in range(plan.chunks)]
    chunk_tables = [[jnp.asarray(table[span]) for table in tables] for span in spans]
    chunk_segments = [segments[span].reshape(-1, 1) for span in spans]
    last = plan.chunks - 1

    outputs, kept = [], []
    blocks = source

    def finished(index, pending, blocks, w, *tokens):
        done = plan.scatter_rest(pending, *tokens)
        return (blocks[index].astype(f32) + done + w["after"]).astype(bf16)

    def step_in(layer, index, x, keys, values, tied):
        w = layers[layer]
        a0, a1, q, k, v = project(x, w, chunk_tables[index], chunk_segments[index], heads, tied)
        keys.append(plan.all_places(k))
        values.append(plan.all_places(v))
        return dict(x=x, a0=a0, a1=a1, q=q, k=list(keys), v=list(values))

    def step_attend(index, s, tied):
        s["o"], s["lse"] = attend(starts[index], s["q"], s["k"], s["v"], heads, tied)

    def step_out(layer, s, tied):
        s["h"], s["d"], part = feed(s["a1"], s["o"], layers[layer], tied)
        return part

    keys, values, state, parts, pending = [], [], [], [], []
    for index in range(plan.chunks):
        x = blocks[index]
        if index == 0:
            x = hold(x, small_there, half_there)
        state.append(step_in(0, index, plan.gather(x), keys, values, ()))
        if index == 0:
            grads = jnp.where(section == 0, cotangent[0, 0], cotangent[1, 0])
            grads = plan.to_work_whole(hold(grads, weights_first))
        step_attend(index, state[index], ())
    for index in range(plan.chunks):
        parts.append(step_out(0, state[index], tuple(grads) if index == last else ()))
        pending.append(plan.scatter_first([parts[index]]))
    after = []
    for index in range(plan.chunks):
        if after:
            pending[index] = hold(pending[index], after[-1])
        after.append(finished(index, pending[index], blocks, layers[0]))
    kept.append((blocks, state))
    outputs.append(after)

    blocks = after
    keys, values, state, pending, after = [], [], [], [], []
    for index in range(plan.chunks):
        s = step_in(1, index, plan.gather(blocks[index]), keys, values, ())
        state.append(s)
        if index == last:
            coming = plan.gather_first(hold(grads[last], s["q"]))
            step_attend(index, s, (parts[0], coming) if last else ())
        else:
            step_attend(index, s, ())
        parts[index] = step_out(1, s, (coming,) if index == last else ())
        pending.append(plan.scatter_first([parts[index]]))
    kept.append((blocks, state))
    pending_out = pending
    gathered = {last: plan.gather_rest(coming)}
    for index in range(last):
        gathered[index] = plan.gather(hold(grads[index], parts[index]))

    def over_tokens(left, right):
        left, right = jnp.concatenate(left, 0), jnp.concatenate(right, 0)
        return lax.dot_general(left, right, (((0,), (0,)), ((), ())), preferred_element_type=f32)

    def step_back(layer, index, gb, carried, tied):
        s = kept[layer][1][index]
        dq, dk, dv = attend_back(
            starts[index], gb, layers[layer], s["q"], s["o"], s["lse"], s["k"], s["v"], carried,
            heads, tied,
        )
        carried = (dk[:-1], dv[:-1])
        return dq, plan.own_places(dk[-1]), plan.own_places(dv[-1]), carried

    def step_leave(layer, index, s, gu, tied):
        dq, dk, dv, _ = s
        x = kept[layer][1][index]["x"]
        gm, e, norm_part, mixed_part, up_part = leave(
            x, dq, dk, dv, gu, layers[layer], chunk_tables[index], tied
        )
        mixed_part = mixed_part.reshape(3, LANES)[:, :local].reshape(-1)
        return gm, e, jnp.concatenate([norm_part.reshape(-1), mixed_part, up_part.reshape(-1)])

    def step_grad(layer, index, pending):
        scaled = plan.scatter_rest(pending)
        normed, inverse = standardize(kept[layer][0][index].astype(f32))
        grad = grads[index].astype(f32) + inverse * (
            scaled
            - jnp.mean(scaled, -1, keepdims=True)
            - normed * jnp.mean(scaled * normed, -1, keepdims=True)
        )
        return grad.astype(bf16)

    def early_terms(layer, gathered, grad_up):
        state = kept[layer][1]
        every = [gathered[index] for index in range(plan.chunks)]
        ups = [grad_up[index] for index in range(plan.chunks)]
        return [
            over_tokens(every, [s["h"] for s in state]).astype(bf16),
            over_tokens([s["a1"] for s in state], ups).astype(bf16),
            over_tokens(every, [s["o"] for s in state]).astype(bf16),
        ]

    def qkv_terms(layer, grad_mixed):
        term = over_tokens(
            [s["a0"] for s in kept[layer][1]], [grad_mixed[index] for index in range(plan.chunks)]
        )
        return term.astype(bf16)

    def without_fill(array):
        return array.reshape(-1, 3, LANES)[:, :, :local].reshape(-1, 3 * local)

    def bias_sum(grads):
        return sum(jnp.sum(item.astype(f32), 0) for item in grads)

    order = list(reversed(range(plan.chunks)))
    second_grads = grads
    results, grad_mixed, pending, sums, carried = {}, {}, {}, 0.0, ((), ())
    grad_up = {
        index: feed_back(gathered[index], layers[1], kept[1][1][index]["d"]) for index in order
    }
    early = jnp.concatenate(early_terms(1, gathered, grad_up), 1)
    held = [hold(item, kept[1][1][last]["q"]) for item in outputs[0]]
    early_second = lax.psum_scatter(
        early, ("wide", "section"), scatter_dimension=0, tiled=True
    )
    waiting = tuple(parts) + (early,)
    for index in order:
        results[index] = step_back(1, index, gathered[index], carried, waiting)
        carried = results[index][-1]
        if index == last:
            token = results[last][0]
            second_outputs = [
                finished(other, pending_out[other], blocks, layers[1], token)
                for other in range(plan.chunks)
            ]
            owned_first = plan.owned(held, 0, token)
            tied = (owned_first, *second_outputs)
        else:
            tied = (pending[index + 1],)
        grad_mixed[index], e, part = step_leave(1, index, results[index], grad_up[index], tied)
        sums += part
        pending[index] = plan.scatter_first([e])
        waiting = (e,)
    after = {}
    for index in order:
        if after:
            pending[index] = hold(pending[index], after[index + 1])
        after[index] = step_grad(1, index, pending[index])
    small_second = jnp.concatenate([sums, bias_sum(grads)])
    second_qkv = qkv_terms(1, grad_mixed)
    input_second = [after[index] for index in range(plan.chunks)]
    grads = input_second
    gathered = {index: plan.gather(grads[index]) for index in order}
    results, grad_mixed, pending, sums, carried = {}, {}, {}, 0.0, ((), ())
    grad_up = {
        index: feed_back(gathered[index], layers[0], kept[0][1][index]["d"]) for index in order
    }
    early = jnp.concatenate(early_terms(0, gathered, grad_up) + [second_qkv], 1)
    early_sum = lax.psum_scatter(early, ("wide", "section"), scatter_dimension=0, tiled=True)
    held = [hold(item, gathered[last]) for item in second_outputs]
    waiting = (early,)
    for index in order:
        results[index] = step_back(0, index, gathered[index], carried, waiting)
        carried = results[index][-1]
        tied = (early_second,) if index == last else (pending[index + 1],)
        grad_mixed[index], e, part = step_leave(0, index, results[index], grad_up[index], tied)
        sums += part
        pending[index] = plan.scatter_first([e])
        waiting = (e,)
    after = {index: step_grad(0, index, pending[index]) for index in order}
    input_first = [hold(after[index], early_sum) for index in range(plan.chunks)]
    all_grads = plan.exchange(input_first, input_second)
    qkv_shares = plan.wide_steps_of(
        hold(without_fill(qkv_terms(0, grad_mixed)), after[0])
    )
    owned_second = plan.owned(held, 1, grad_mixed[0])
    total = jnp.stack([jnp.concatenate([sums, bias_sum(grads)]), small_second])
    at = 4 * width + 3 * local
    shared = jnp.concatenate([total[:, : 4 * width], total[:, at + hidden :]], 1)
    shared = plan.sum_all(shared, ("tp",))
    total = hold(jnp.concatenate([shared, total[:, 4 * width : at + hidden]], 1), after[0])
    if plan.wide > 4:
        total = lax.psum(total, "wide")
    else:
        terms = [total] + plan.wide_steps(lambda step: total)
        while len(terms) > 1:
            terms = [one + two for one, two in zip(terms[::2], terms[1::2])]
        total = terms[0]
    first_qkv_sum = sum(item.astype(f32) for item in qkv_shares)
    split = 2 * hidden + LANES
    here = plan.send(hold(early_second, grad_mixed[0]), 0)
    there, here_qkv = plan.send(early_sum[:, :split], 1), plan.send(early_sum[:, split:], 0)
    early = pick(
        section,
        jnp.concatenate([early_sum[:, :split], there], 0),
        jnp.concatenate([here, early_second], 0),
    ).astype(f32)
    qkv_grad = first_qkv_sum + plan.send(first_qkv_sum.astype(bf16), 1).astype(f32)
    second_qkv = without_fill(jnp.concatenate([here_qkv, early_sum[:, split:]], 0)).astype(f32)
    qkv_grad = pick(section, qkv_grad, second_qkv)
    down_grad, up_grad = early[:, :hidden], early[:, hidden : 2 * hidden]
    out_grad = early[:, 2 * hidden : 2 * hidden + local]
    total = total + plan.swap(total)
    total = pick(section, total[0], total[1])
    shared, own = total[: 5 * width], total[5 * width :]
    bias_grad = shared[4 * width :]
    return (
        pick(section, owned_first, owned_second)[None, :, None],
        all_grads.astype(f32)[None, :, None],
        shared[: 2 * width].reshape(1, 2, width),
        shared[2 * width : 4 * width].reshape(1, 2, width),
        qkv_grad.reshape(1, -1, 3, local),
        own[: 3 * local].reshape(1, 3, local),
        out_grad.T[None],
        bias_grad[None],
        up_grad[None],
        own[3 * local :][None],
        down_grad.T[None],
        bias_grad[None],
    )


def solution(mesh):
    return jax.shard_map(
        on_device,
        mesh=mesh,
        in_specs=(
            P(None, "tp", "wide", None),
            P(None, "tp", "wide", None),
            P(),
            P("section", None, None),
            P("section", None, None),
            P("section", "wide", None, "tp"),
            P("section", None, "tp"),
            P("section", "tp", "wide"),
            P("section", None),
            P("section", "wide", "tp"),
            P("section", "tp"),
            P("section", "tp", "wide"),
            P("section", None),
        ),
        out_specs=(
            P("section", None, "tp", "wide", None),
            P("section", None, "tp", "wide", None),
            P("section", None, None),
            P("section", None, None),
            P("section", "wide", None, "tp"),
            P("section", None, "tp"),
            P("section", "tp", "wide"),
            P("section", None),
            P("section", "wide", "tp"),
            P("section", "tp"),
            P("section", "tp", "wide"),
            P("section", None),
        ),
        check_vma=False,
    )
```
